32 devices in a mesh: gx: 8 (over y, x, core), gy: 4 (over z).
Axes of the slice: x: 2, y: 2, z: 4, core: 2. Of those that a mesh axis runs over, the one named last changes fastest.
Arguments:
- basis: bfloat16 [16, 4, 128, 1024], P(None, None, 'gy', 'gx'), may hold values from -56 to 56
- mobility: bfloat16 [4, 128, 1024], P(None, 'gy', 'gx'), may hold values from 0.12 to 8.2
- accumulation: float32 [4, 128, 1024], P(None, 'gy', 'gx'), may hold values from 0.03 to 0.32
- residual: float32 [4, 128, 1024], P(None, 'gy', 'gx'), may hold values from -140 to 140
Outputs:
- correction: float32 [4, 128, 1024], P(None, 'gy', 'gx')
- coarse_solution: float32 [8, 4, 16], P('gx', 'gy')
The draws below stay inside these ranges and needn't reach their ends.
All inputs are finite; a program needn't handle non-finite values.
Results may differ from the reference program's by a relative error of at most 0.0003.
Values may be sent and summed in bfloat16 or wider, within the bound.
No kernel may reach another device: no remote copies, remote signals or barrier semaphores. Data moves between devices by JAX's collectives and lax.ppermute only.
A program may use at most 64 MiB of HBM per device.

```python
import jax
import jax.numpy as jnp
from jax import lax

K = 16
CX = 128
CY = 32
CZ = 4
ITERS = 2
SUBX = 8
SUBY = 4
NX = 1024
NY = 128
N_GX = 8
N_GY = 4


def cosine_table(mode_count, length):
    wavenumber = jnp.arange(mode_count, dtype=jnp.float32)
    position = (jnp.arange(length, dtype=jnp.float32) + 0.5) / length
    return jnp.cos(jnp.pi * wavenumber[:, None] * position[None, :])


def mode_weights(count_z, count_y, count_x):
    along_z = jnp.arange(count_z, dtype=jnp.float32)
    along_y = jnp.arange(count_y, dtype=jnp.float32)
    along_x = jnp.arange(count_x, dtype=jnp.float32)
    return 1.0 / (1.0 + along_z[:, None, None] + along_y[None, :, None] + along_x[None, None, :])


def global_smooth(key):
    coefficient = jax.random.truncated_normal(key, -3.0, 3.0, (2, 8, 8)) * mode_weights(2, 8, 8)
    return jnp.einsum('cde,cz,dy,ex->zyx', coefficient, cosine_table(2, CZ), cosine_table(8, NY), cosine_table(8, NX))


def draw_basis(key, part):
    coefficient_key, jitter_key = jax.random.split(jax.random.fold_in(key, 404), 2)
    weight = mode_weights(4, 4, 4)
    coefficient = jax.random.truncated_normal(coefficient_key, -3.0, 3.0, (K, SUBX, SUBY, 4, 4, 4)) * weight
    jitter = 0.1 * jax.random.truncated_normal(jitter_key, -4.0, 4.0, (K, CZ, NY, NX))
    smooth = jnp.einsum('kabcde,cz,dq,ep->kzbqap', coefficient, cosine_table(4, CZ), cosine_table(4, CY), cosine_table(4, CX))
    return (smooth.reshape(K, CZ, NY, NX) + jitter).astype(jnp.bfloat16)


def draw_mobility(key, part):
    smooth_key, jitter_key = jax.random.split(jax.random.fold_in(key, 101))
    smooth = global_smooth(smooth_key)
    jitter = jax.random.uniform(jitter_key, (CZ, NY, NX), minval=-0.6, maxval=0.6)
    return jnp.exp(1.5 * jnp.tanh(0.5 * smooth) + jitter).astype(jnp.bfloat16)


def draw_accumulation(key, part):
    smooth_key, jitter_key = jax.random.split(jax.random.fold_in(key, 202))
    smooth = global_smooth(smooth_key)
    jitter = jax.random.uniform(jitter_key, (CZ, NY, NX), minval=-0.35, maxval=0.35)
    return 0.1 * jnp.exp(0.8 * jnp.tanh(0.5 * smooth) + jitter)


def draw_residual(key, part):
    smooth_key, jitter_key = jax.random.split(jax.random.fold_in(key, 303))
    smooth = global_smooth(smooth_key)
    column = jnp.arange(NX, dtype=jnp.float32) / max(NX - 1, 1)
    slope_factor = jnp.broadcast_to(1.0 + 2.0 * column[None, None, :], (CZ, NY, NX))
    jitter = jax.random.truncated_normal(jitter_key, -4.0, 4.0, (CZ, NY, NX))
    return slope_factor * (0.25 * smooth + 0.15 * jitter)


def setup_inputs(seed: int = 0) -> dict:
    arg_keys = jax.random.split(jax.random.key(seed), 5)
    return {
        "basis": draw_basis(jax.random.fold_in(arg_keys[4], 71), 0),
        "mobility": draw_mobility(jax.random.fold_in(arg_keys[4], 71), 0),
        "accumulation": draw_accumulation(jax.random.fold_in(arg_keys[4], 71), 0),
        "residual": draw_residual(jax.random.fold_in(arg_keys[4], 71), 0),
    }


epsilon = 1e-6
vertical_ratio = 0.1


def harmonic(first, second):
    return 2.0 * first * second / (first + second)


def gram_sum(weighted, other):
    return jnp.einsum('kzyx,lzyx->kl', weighted, other, precision=lax.Precision.HIGHEST)


def face_blocks(padded_basis, padded_mobility, accumulation):
    interior = padded_basis[:, :, 1:-1, 1:-1]
    cell_mobility = padded_mobility[:, 1:-1, 1:-1]
    self_block = gram_sum(interior * accumulation, interior)
    conduct_x = harmonic(cell_mobility[:, :, :-1], cell_mobility[:, :, 1:])
    change_x = interior[:, :, :, 1:] - interior[:, :, :, :-1]
    self_block = self_block + gram_sum(change_x * conduct_x, change_x)
    conduct_y = harmonic(cell_mobility[:, :-1, :], cell_mobility[:, 1:, :])
    change_y = interior[:, :, 1:, :] - interior[:, :, :-1, :]
    self_block = self_block + gram_sum(change_y * conduct_y, change_y)
    conduct_z = vertical_ratio * harmonic(cell_mobility[:-1], cell_mobility[1:])
    change_z = interior[:, 1:] - interior[:, :-1]
    self_block = self_block + gram_sum(change_z * conduct_z, change_z)
    edges = (
        (interior[:, :, :, :1], padded_basis[:, :, 1:-1, :1], cell_mobility[:, :, :1], padded_mobility[:, 1:-1, :1]),
        (interior[:, :, :, -1:], padded_basis[:, :, 1:-1, -1:], cell_mobility[:, :, -1:], padded_mobility[:, 1:-1, -1:]),
        (interior[:, :, :1, :], padded_basis[:, :, :1, 1:-1], cell_mobility[:, :1, :], padded_mobility[:, :1, 1:-1]),
        (interior[:, :, -1:, :], padded_basis[:, :, -1:, 1:-1], cell_mobility[:, -1:, :], padded_mobility[:, -1:, 1:-1]),
    )
    side_blocks = []
    for edge_cells, ghost_cells, edge_mobility, ghost_mobility in edges:
        weighted = edge_cells * harmonic(edge_mobility, ghost_mobility)
        self_block = self_block + gram_sum(weighted, edge_cells)
        side_blocks.append(-gram_sum(weighted, ghost_cells))
    return jnp.stack([self_block] + side_blocks)


def coarse_apply(blocks, vector):
    padded = jnp.pad(vector, ((1, 1), (1, 1), (0, 0)))
    beside = jnp.stack([vector, padded[:-2, 1:-1], padded[2:, 1:-1], padded[1:-1, :-2], padded[1:-1, 2:]], axis=2)
    return jnp.einsum('abnkl,abnl->abk', blocks, beside, precision=lax.Precision.HIGHEST)


def coarse_solve(blocks, coarse_source):
    solution = jnp.zeros_like(coarse_source)
    remainder = coarse_source
    direction = coarse_source
    energy = jnp.sum(remainder * remainder)
    for iteration in range(ITERS):
        operator_image = coarse_apply(blocks, direction)
        step_length = energy / (jnp.sum(direction * operator_image) + epsilon)
        solution = solution + step_length * direction
        if iteration + 1 < ITERS:
            remainder = remainder - step_length * operator_image
            renewed = jnp.sum(remainder * remainder)
            direction = remainder + (renewed / (energy + epsilon)) * direction
            energy = renewed
    return solution


def reference(basis, mobility, accumulation, residual):
    padded_basis = jnp.pad(basis, ((0, 0), (0, 0), (1, 1), (1, 1)))
    padded_mobility = jnp.pad(mobility, ((0, 0), (1, 1), (1, 1)))

    def subdomain(number):
        along_x = number // N_GY
        along_y = number % N_GY
        start_y = (along_y * CY).astype(jnp.int32)
        start_x = (along_x * CX).astype(jnp.int32)
        anchor = jnp.zeros((), jnp.int32)
        window = lax.dynamic_slice(padded_basis, (anchor, anchor, start_y, start_x), (K, CZ, CY + 2, CX + 2)).astype(jnp.float32)
        beside_all = lax.dynamic_slice(padded_mobility, (anchor, start_y, start_x), (CZ, CY + 2, CX + 2)).astype(jnp.float32)
        storage = lax.dynamic_slice(accumulation, (anchor, start_y, start_x), (CZ, CY, CX))
        source = lax.dynamic_slice(residual, (anchor, start_y, start_x), (CZ, CY, CX))
        blocks = face_blocks(window, beside_all, storage)
        projected = jnp.einsum('kzyx,zyx->k', window[:, :, 1:-1, 1:-1], source, precision=lax.Precision.HIGHEST)
        return blocks, projected

    blocks, projected = lax.map(subdomain, jnp.arange(N_GX * N_GY, dtype=jnp.int32))
    blocks = blocks.reshape(N_GX, N_GY, 5, K, K)
    projected = projected.reshape(N_GX, N_GY, K)
    solution = coarse_solve(blocks, projected)
    expanded = basis.astype(jnp.float32).reshape(K, CZ, N_GY, CY, N_GX, CX)
    correction = jnp.einsum('kzbqap,abk->zbqap', expanded, solution, precision=lax.Precision.HIGHEST)
    return correction.reshape(CZ, NY, NX), solution
```

```python
import functools

import jax
import jax.numpy as jnp
from jax import lax
from jax.experimental import pallas as pl
from jax.experimental.pallas import tpu as pltpu
from jax.sharding import PartitionSpec as P

ITERS = 2
EPSILON = 1e-6
VERTICAL_RATIO = 0.1
TINY = 1e-30
TILE = 16
LANES = 128

F32 = jnp.float32
BF16 = jnp.bfloat16
VMEM = pl.BlockSpec(memory_space=pltpu.VMEM)


def iota(shape, dim):
    return lax.broadcasted_iota(jnp.int32, shape, dim)


def round_up(n, m):
    return (n + m - 1) // m * m


def harmonic(first, second):
    return 2.0 * first * second / jnp.maximum(first + second, TINY)


def dot_nt(a, b):
    return lax.dot_general(a, b, (((1,), (1,)), ((), ())), preferred_element_type=F32)


def three_terms(x):
    high = x.astype(BF16).astype(F32)
    rest = x - high
    middle = rest.astype(BF16).astype(F32)
    return high, middle, rest - middle


def position(axis, count):
    index = lax.axis_index(axis)
    odd = lax.rem(index, 2) == 1
    inner = jnp.logical_and(index > 0, index < count - 1)
    return odd, inner


def edges_kernel(counts, basis_ref, mobility_ref, residual_ref, x1_ref, x2_ref, y1_ref, y2_ref, b_ref):
    k_count, cz, cy, cx = basis_ref.shape
    cells = cz * cy
    odd_x, inner_x = position("gx", counts[0])
    odd_y, inner_y = position("gy", counts[1])

    residual = residual_ref[...]
    row = iota((k_count, cx), 0)
    partial = jnp.zeros((k_count, cx), F32)
    for k in range(k_count):
        product = basis_ref[k].astype(F32) * residual
        total = jnp.sum(jnp.sum(product, axis=0), axis=0, keepdims=True)
        partial = jnp.where(row == k, total, partial)
    b = jnp.broadcast_to(jnp.sum(partial, axis=1, keepdims=True), (k_count, LANES))
    b_ref[...] = b

    first = jnp.where(odd_x, 0, cx - 1)
    second = jnp.where(odd_x, cx - 1, 0)
    pick_row = iota((2 * k_count, cx), 0)
    pick_lane = iota((2 * k_count, cx), 1)
    wanted = pick_lane == jnp.where(pick_row < k_count, first, second)
    pick_k = jnp.where(pick_row < k_count, pick_row, pick_row - k_count)
    columns = jnp.zeros((2 * k_count, cells), F32)
    for k in range(k_count):
        pick = jnp.where(jnp.logical_and(wanted, pick_k == k), 1.0, 0.0).astype(BF16)
        columns = columns + dot_nt(pick, basis_ref[k].reshape(cells, cx))
    pick_row = iota((TILE, cx), 0)
    pick_lane = iota((TILE, cx), 1)
    pick = jnp.where(pick_lane == jnp.where(pick_row == 0, first, second), 1.0, 0.0).astype(BF16)
    edge_mobility = dot_nt(pick, mobility_ref[...].reshape(cells, cx))

    for number, ref in ((0, x1_ref), (1, x2_ref)):
        edge = columns[number * k_count : (number + 1) * k_count]
        ref[0:k_count, :] = edge.astype(BF16)
        field = jnp.sum(edge * b[:, :1], axis=0, keepdims=True)
        mobility = edge_mobility[number : number + 1]
        if number == 1:
            mobility = jnp.where(inner_x, mobility, 0.0)
        row = iota((TILE, cells), 0)
        extra = jnp.zeros((TILE, cells), F32)
        for place, value in enumerate((mobility, *three_terms(field))):
            extra = jnp.where(row == place, value, extra)
        ref[k_count : k_count + TILE, :] = extra.astype(BF16)

    row = iota((k_count, cx), 0)
    extra_rows = round_up(4 * cz, TILE)
    extra_row = iota((extra_rows, cx), 0)
    extras = [jnp.zeros((extra_rows, cx), F32) for _ in range(2)]
    for z in range(cz):
        low = jnp.zeros((k_count, cx), F32)
        high = jnp.zeros((k_count, cx), F32)
        for k in range(k_count):
            low = jnp.where(row == k, basis_ref[k, z, 0:TILE, :].astype(F32)[0:1], low)
            high = jnp.where(row == k, basis_ref[k, z, cy - TILE : cy, :].astype(F32)[TILE - 1 : TILE], high)
        low_mobility = mobility_ref[z, 0:TILE, :].astype(F32)[0:1]
        high_mobility = mobility_ref[z, cy - TILE : cy, :].astype(F32)[TILE - 1 : TILE]
        for number, ref in ((0, y1_ref), (1, y2_ref)):
            use_low = odd_y if number == 0 else jnp.logical_not(odd_y)
            edge = jnp.where(use_low, low, high)
            mobility = jnp.where(use_low, low_mobility, high_mobility)
            if number == 1:
                mobility = jnp.where(inner_y, mobility, 0.0)
            ref[z * k_count : (z + 1) * k_count, :] = edge.astype(BF16)
            field = jnp.sum(edge * b[:, :1], axis=0, keepdims=True)
            for place, value in enumerate((mobility, *three_terms(field))):
                extras[number] = jnp.where(extra_row == place * cz + z, value, extras[number])
    for number, ref in ((0, y1_ref), (1, y2_ref)):
        ref[cz * k_count : cz * k_count + extra_rows, :] = extras[number].astype(BF16)


def gram_kernel(basis_ref, mobility_ref, accumulation_ref, gram_ref, left_ref):
    k_count, cz, cy, cx = basis_ref.shape
    mobility = mobility_ref[...].astype(F32)
    accumulation = accumulation_ref[...]
    shape = mobility.shape
    along_x = jnp.where(iota(shape, 2) < cx - 1, harmonic(mobility, pltpu.roll(mobility, cx - 1, 2)), 0.0)
    along_y = jnp.where(iota(shape, 1) < cy - 1, harmonic(mobility, pltpu.roll(mobility, cy - 1, 1)), 0.0)
    along_z = VERTICAL_RATIO * harmonic(mobility[:-1], mobility[1:])
    rows = k_count * TILE
    strips = [(z, y) for z in range(cz) for y in range(0, cy, TILE)]
    for k in range(k_count):
        field = basis_ref[k].astype(F32)
        flow_x = along_x * (field - pltpu.roll(field, cx - 1, 2))
        image = accumulation * field + flow_x - pltpu.roll(flow_x, 1, 2)
        flow_y = along_y * (field - pltpu.roll(field, cy - 1, 1))
        image = image + flow_y - pltpu.roll(flow_y, 1, 1)
        flow_z = along_z * (field[:-1] - field[1:])
        nothing = jnp.zeros_like(field[:1])
        image = image + jnp.concatenate([flow_z, nothing], axis=0) - jnp.concatenate([nothing, flow_z], axis=0)
        high = image.astype(BF16)
        low = (image - high.astype(F32)).astype(BF16)
        for place, (z, y) in enumerate(strips):
            lanes = slice(place * cx, (place + 1) * cx)
            left_ref[k * TILE : (k + 1) * TILE, lanes] = high[z, y : y + TILE]
            left_ref[rows + k * TILE : rows + (k + 1) * TILE, lanes] = low[z, y : y + TILE]
    total = jnp.zeros((2 * rows, rows), F32)
    for place, (z, y) in enumerate(strips):
        right = basis_ref[:, z, y : y + TILE, :].reshape(rows, cx)
        total = total + dot_nt(left_ref[:, place * cx : (place + 1) * cx], right)
    total = total[:rows] + total[rows:]
    same = lax.rem(iota((rows, rows), 0), TILE) == lax.rem(iota((rows, rows), 1), TILE)
    total = jnp.where(same, total, 0.0)
    gram_ref[...] = jnp.sum(total.reshape(k_count, TILE, rows), axis=1)


def couple_kernel(
    cz, counts, x1_ref, x2_ref, y1_ref, y2_ref, rx1_ref, rx2_ref, ry1_ref, ry2_ref, b_ref, gram_ref, out_ref
):
    k_count = b_ref.shape[0]
    odd_x, _ = position("gx", counts[0])
    odd_y, _ = position("gy", counts[1])
    b = b_ref[...]
    gram = gram_ref[...]
    wide = gram.shape[1]
    spread = iota((k_count, wide), 1) // TILE == iota((k_count, wide), 0)

    def as_row(column):
        return jnp.sum(jnp.where(spread, column[:, :1], 0.0), axis=0, keepdims=True)

    def unpack(ref, layers):
        blocks = [ref[z * k_count : (z + 1) * k_count, :].astype(F32) for z in range(layers)]
        start = layers * k_count
        extra = ref[start : start + round_up(4 * layers, TILE), :].astype(F32)
        mobility, high, middle, low = (extra[n * layers : (n + 1) * layers] for n in range(4))
        return blocks, mobility, high + middle + low

    faces = []
    for own_ref, other_ref, layers in (
        (x1_ref, rx1_ref, 1),
        (x2_ref, rx2_ref, 1),
        (y1_ref, ry1_ref, cz),
        (y2_ref, ry2_ref, cz),
    ):
        own, own_mobility, own_field = unpack(own_ref, layers)
        other, other_mobility, other_field = unpack(other_ref, layers)
        faces.append((own, other, harmonic(own_mobility, other_mobility), own_field, other_field))

    b_row = as_row(b)
    along = jnp.zeros((k_count, LANES), F32)
    for own, _, conductance, own_field, other_field in faces:
        flow = conductance * (own_field - other_field)
        for z, block in enumerate(own):
            along = along + block * flow[z : z + 1]
    image = jnp.sum(along, axis=1, keepdims=True) + jnp.sum(gram * b_row, axis=1, keepdims=True)
    b_col = b[:, :1]
    source_square = jnp.sum(b_col * b_col, axis=0, keepdims=True)
    source_image = jnp.sum(b_col * image, axis=0, keepdims=True)
    quotient = source_image / jnp.maximum(source_square, TINY)
    v_col = image - quotient * b_col
    v_row = as_row(v_col)

    squares = [jnp.zeros((1, LANES), F32) for _ in range(3)]
    toward = []
    for own, other, conductance, own_field, _ in faces:
        v_field = jnp.concatenate([jnp.sum(block * v_col, axis=0, keepdims=True) for block in own], axis=0)
        flow_b = conductance * own_field
        flow_v = conductance * v_field
        for n, value in enumerate((flow_b * own_field, flow_b * v_field, flow_v * v_field)):
            squares[n] = squares[n] + jnp.sum(value, axis=0, keepdims=True)
        toward.append((other, flow_b, flow_v))
    for n, (left, right) in enumerate(((b_col, b_row), (b_col, v_row), (v_col, v_row))):
        value = jnp.sum(left * gram, axis=0, keepdims=True) * right
        for start in range(0, wide, LANES):
            squares[n] = squares[n] + value[:, start : start + LANES]
    squares = [jnp.sum(value, axis=1, keepdims=True) for value in squares]

    columns = [b_col, v_col]
    for first, second, odd in ((toward[0], toward[1], odd_x), (toward[2], toward[3], odd_y)):
        for which in (1, 2):
            product = jnp.zeros((k_count, LANES), F32)
            for z in range(len(first[0])):
                block = jnp.where(odd, second[0][z], first[0][z])
                flow = jnp.where(odd, second[which], first[which])
                product = product - block * flow[z : z + 1]
            columns.append(jnp.sum(product, axis=1, keepdims=True))
    lane = iota((k_count, LANES), 1)
    own_lane = lane - iota((k_count, LANES), 0)
    placed = jnp.zeros((k_count, LANES), F32)
    for n, column in enumerate(columns):
        placed = jnp.where(own_lane == n * k_count, column, placed)
    packed = jnp.sum(placed, axis=0, keepdims=True)
    lane = iota((1, LANES), 1)
    base = len(columns) * k_count
    for n, value in enumerate((quotient, *squares, source_square, source_image)):
        packed = jnp.where(lane == base + n, value, packed)
    out_ref[...] = jnp.broadcast_to(packed, out_ref.shape)


def finish_kernel(count_y, gathered_ref, own_ref, basis_ref, correction_ref, solution_ref):
    k_count, cz, cy, cx = basis_ref.shape
    base = 6 * k_count
    every = gathered_ref[...]
    lane = iota(every.shape, 1)

    def total(x):
        return jnp.sum(jnp.sum(x, axis=0, keepdims=True), axis=1, keepdims=True)

    def shifted(x, amount):
        return pltpu.roll(x, LANES - amount, 1)

    def up_rows(x, amount):
        return jnp.concatenate([x[amount:], x[:amount]], axis=0)

    sums = jnp.sum(every, axis=0, keepdims=True)
    energy = sums[:, base + 4 : base + 5]
    step = energy / (sums[:, base + 5 : base + 6] + EPSILON)
    quotient = every[:, base : base + 1]
    beside = shifted(every, k_count)
    remainder = every - step * (quotient * every + beside)
    renewed = total(jnp.where(lane < k_count, remainder * remainder, 0.0))
    ratio = renewed / (energy + EPSILON)
    weight = 1.0 + ratio - step * quotient
    mixed = weight * every - step * beside
    direction = jnp.where(lane < k_count, mixed, 0.0)
    cross = shifted(mixed, 2 * k_count) * up_rows(direction, count_y) + shifted(mixed, 4 * k_count) * up_rows(direction, 1)
    own_part = (
        weight * weight * every[:, base + 1 : base + 2]
        - 2.0 * weight * step * every[:, base + 2 : base + 3]
        + step * step * every[:, base + 3 : base + 4]
    )
    curvature = total(2.0 * cross) + jnp.sum(own_part, axis=0, keepdims=True)
    last_step = renewed / (curvature + EPSILON)

    own = own_ref[0:1, :]
    own_weight = 1.0 + ratio - step * own[:, base : base + 1]
    own_direction = own_weight * own - step * shifted(own, k_count)
    solution = step * own + last_step * own_direction
    solution_ref[...] = solution[:, :k_count]
    spread = iota((k_count, LANES), 0) == iota((k_count, LANES), 1)
    column = jnp.sum(jnp.where(spread, solution, 0.0), axis=1, keepdims=True)
    correction = jnp.zeros((cz, cy, cx), F32)
    for k in range(k_count):
        correction = correction + basis_ref[k].astype(F32) * column[k : k + 1][None]
    correction_ref[...] = correction


def exchange(message, axis, count, second):
    if second:
        pairs = [(i, (i - 1) % count if i % 2 == 0 else (i + 1) % count) for i in range(count)]
    else:
        pairs = [(i, i ^ 1) for i in range(count)]
    return lax.ppermute(message, axis, pairs)


def per_device(counts, basis, mobility, accumulation, residual):
    k_count, cz, cy, cx = basis.shape
    devices = counts[0] * counts[1]
    x_message = jax.ShapeDtypeStruct((k_count + TILE, cz * cy), BF16)
    y_message = jax.ShapeDtypeStruct((cz * k_count + round_up(4 * cz, TILE), cx), BF16)
    x1, x2, y1, y2, b = pl.pallas_call(
        functools.partial(edges_kernel, counts),
        out_shape=(x_message, x_message, y_message, y_message, jax.ShapeDtypeStruct((k_count, LANES), F32)),
        in_specs=[VMEM] * 3,
        out_specs=(VMEM,) * 5,
    )(basis, mobility, residual)
    rx1 = exchange(x1, "gx", counts[0], False)
    rx2 = exchange(x2, "gx", counts[0], True)
    ry1 = exchange(y1, "gy", counts[1], False)
    ry2 = exchange(y2, "gy", counts[1], True)
    gram = pl.pallas_call(
        gram_kernel,
        out_shape=jax.ShapeDtypeStruct((k_count, k_count * TILE), F32),
        in_specs=[VMEM] * 3,
        out_specs=VMEM,
        scratch_shapes=[pltpu.VMEM((2 * k_count * TILE, cz * cy // TILE * cx), BF16)],
        cost_estimate=pl.CostEstimate(flops=2 * 10**9, bytes_accessed=10**6, transcendentals=0),
    )(basis, mobility, accumulation)
    row = pl.pallas_call(
        functools.partial(couple_kernel, cz, counts),
        out_shape=jax.ShapeDtypeStruct((devices, LANES), F32),
        in_specs=[VMEM] * 10,
        out_specs=VMEM,
    )(x1, x2, y1, y2, rx1, rx2, ry1, ry2, b, gram)
    gathered = lax.all_to_all(row, ("gx", "gy"), 0, 0, tiled=True)
    correction, solution = pl.pallas_call(
        functools.partial(finish_kernel, counts[1]),
        out_shape=(jax.ShapeDtypeStruct((cz, cy, cx), F32), jax.ShapeDtypeStruct((1, k_count), F32)),
        in_specs=[VMEM] * 3,
        out_specs=(VMEM, VMEM),
    )(gathered, row, basis)
    return correction, solution.reshape(1, 1, k_count)


def solution(mesh):
    counts = (mesh.shape["gx"], mesh.shape["gy"])
    placed = (
        P(None, None, "gy", "gx"),
        P(None, "gy", "gx"),
        P(None, "gy", "gx"),
        P(None, "gy", "gx"),
    )
    return jax.shard_map(
        functools.partial(per_device, counts),
        mesh=mesh,
        in_specs=placed,
        out_specs=(P(None, "gy", "gx"), P("gx", "gy", None)),
        check_vma=False,
    )
```

```python
import functools

import jax
import jax.numpy as jnp
from jax import lax
from jax.experimental import pallas as pl
from jax.experimental.pallas import tpu as pltpu
from jax.sharding import PartitionSpec as P

ITERS = 2
EPSILON = 1e-6
VERTICAL_RATIO = 0.1
TINY = 1e-30
TILE = 16
LANES = 128

F32 = jnp.float32
BF16 = jnp.bfloat16
VMEM = pl.BlockSpec(memory_space=pltpu.VMEM)
PARAMS = pltpu.CompilerParams(vmem_limit_bytes=8 * 2**20)


def iota(shape, dim):
    return lax.broadcasted_iota(jnp.int32, shape, dim)


def round_up(n, m):
    return (n + m - 1) // m * m


def harmonic(first, second):
    return 2.0 * first * second / jnp.maximum(first + second, TINY)


def dot_nt(a, b):
    return lax.dot_general(a, b, (((1,), (1,)), ((), ())), preferred_element_type=F32)


def three_terms(x):
    high = x.astype(BF16).astype(F32)
    rest = x - high
    middle = rest.astype(BF16).astype(F32)
    return high, middle, rest - middle


def position(axis, count):
    index = lax.axis_index(axis)
    odd = lax.rem(index, 2) == 1
    inner = jnp.logical_and(index > 0, index < count - 1)
    return odd, inner


def edges_kernel(counts, basis_ref, mobility_ref, residual_ref, x1_ref, x2_ref, y1_ref, y2_ref, b_ref):
    k_count, cz, cy, cx = basis_ref.shape
    cells = cz * cy
    odd_x, inner_x = position("gx", counts[0])
    odd_y, inner_y = position("gy", counts[1])

    residual = residual_ref[...]
    row = iota((k_count, cx), 0)
    partial = jnp.zeros((k_count, cx), F32)
    for k in range(k_count):
        product = basis_ref[k].astype(F32) * residual
        total = jnp.sum(jnp.sum(product, axis=0), axis=0, keepdims=True)
        partial = jnp.where(row == k, total, partial)
    b = jnp.broadcast_to(jnp.sum(partial, axis=1, keepdims=True), (k_count, LANES))
    b_ref[...] = b

    first = jnp.where(odd_x, 0, cx - 1)
    second = jnp.where(odd_x, cx - 1, 0)
    pick_row = iota((2 * k_count, cx), 0)
    pick_lane = iota((2 * k_count, cx), 1)
    wanted = pick_lane == jnp.where(pick_row < k_count, first, second)
    pick_k = jnp.where(pick_row < k_count, pick_row, pick_row - k_count)
    columns = jnp.zeros((2 * k_count, cells), F32)
    for k in range(k_count):
        pick = jnp.where(jnp.logical_and(wanted, pick_k == k), 1.0, 0.0).astype(BF16)
        columns = columns + dot_nt(pick, basis_ref[k].reshape(cells, cx))
    pick_row = iota((TILE, cx), 0)
    pick_lane = iota((TILE, cx), 1)
    pick = jnp.where(pick_lane == jnp.where(pick_row == 0, first, second), 1.0, 0.0).astype(BF16)
    edge_mobility = dot_nt(pick, mobility_ref[...].reshape(cells, cx))

    for number, ref in ((0, x1_ref), (1, x2_ref)):
        edge = columns[number * k_count : (number + 1) * k_count]
        ref[0:k_count, :] = edge.astype(BF16)
        field = jnp.sum(edge * b[:, :1], axis=0, keepdims=True)
        mobility = edge_mobility[number : number + 1]
        if number == 1:
            mobility = jnp.where(inner_x, mobility, 0.0)
        row = iota((TILE, cells), 0)
        extra = jnp.zeros((TILE, cells), F32)
        for place, value in enumerate((mobility, *three_terms(field))):
            extra = jnp.where(row == place, value, extra)
        ref[k_count : k_count + TILE, :] = extra.astype(BF16)

    row = iota((k_count, cx), 0)
    extra_rows = round_up(4 * cz, TILE)
    extra_row = iota((extra_rows, cx), 0)
    extras = [jnp.zeros((extra_rows, cx), F32) for _ in range(2)]
    for z in range(cz):
        low = jnp.zeros((k_count, cx), F32)
        high = jnp.zeros((k_count, cx), F32)
        for k in range(k_count):
            low = jnp.where(row == k, basis_ref[k, z, 0:TILE, :].astype(F32)[0:1], low)
            high = jnp.where(row == k, basis_ref[k, z, cy - TILE : cy, :].astype(F32)[TILE - 1 : TILE], high)
        low_mobility = mobility_ref[z, 0:TILE, :].astype(F32)[0:1]
        high_mobility = mobility_ref[z, cy - TILE : cy, :].astype(F32)[TILE - 1 : TILE]
        for number, ref in ((0, y1_ref), (1, y2_ref)):
            use_low = odd_y if number == 0 else jnp.logical_not(odd_y)
            edge = jnp.where(use_low, low, high)
            mobility = jnp.where(use_low, low_mobility, high_mobility)
            if number == 1:
                mobility = jnp.where(inner_y, mobility, 0.0)
            ref[z * k_count : (z + 1) * k_count, :] = edge.astype(BF16)
            field = jnp.sum(edge * b[:, :1], axis=0, keepdims=True)
            for place, value in enumerate((mobility, *three_terms(field))):
                extras[number] = jnp.where(extra_row == place * cz + z, value, extras[number])
    for number, ref in ((0, y1_ref), (1, y2_ref)):
        ref[cz * k_count : cz * k_count + extra_rows, :] = extras[number].astype(BF16)


def gram_kernel(basis_ref, mobility_ref, accumulation_ref, gram_ref, left_ref):
    k_count, cz, cy, cx = basis_ref.shape
    mobility = mobility_ref[...].astype(F32)
    accumulation = accumulation_ref[...]
    shape = mobility.shape
    along_x = jnp.where(iota(shape, 2) < cx - 1, harmonic(mobility, pltpu.roll(mobility, cx - 1, 2)), 0.0)
    along_y = jnp.where(iota(shape, 1) < cy - 1, harmonic(mobility, pltpu.roll(mobility, cy - 1, 1)), 0.0)
    along_z = VERTICAL_RATIO * harmonic(mobility[:-1], mobility[1:])
    rows = k_count * TILE
    strips = [(z, y) for z in range(cz) for y in range(0, cy, TILE)]
    for k in range(k_count):
        field = basis_ref[k].astype(F32)
        flow_x = along_x * (field - pltpu.roll(field, cx - 1, 2))
        image = accumulation * field + flow_x - pltpu.roll(flow_x, 1, 2)
        flow_y = along_y * (field - pltpu.roll(field, cy - 1, 1))
        image = image + flow_y - pltpu.roll(flow_y, 1, 1)
        flow_z = along_z * (field[:-1] - field[1:])
        nothing = jnp.zeros_like(field[:1])
        image = image + jnp.concatenate([flow_z, nothing], axis=0) - jnp.concatenate([nothing, flow_z], axis=0)
        high = image.astype(BF16)
        low = (image - high.astype(F32)).astype(BF16)
        for place, (z, y) in enumerate(strips):
            lanes = slice(place * cx, (place + 1) * cx)
            left_ref[k * TILE : (k + 1) * TILE, lanes] = high[z, y : y + TILE]
            left_ref[rows + k * TILE : rows + (k + 1) * TILE, lanes] = low[z, y : y + TILE]
    total = jnp.zeros((2 * rows, rows), F32)
    for place, (z, y) in enumerate(strips):
        right = basis_ref[:, z, y : y + TILE, :].reshape(rows, cx)
        total = total + dot_nt(left_ref[:, place * cx : (place + 1) * cx], right)
    total = total[:rows] + total[rows:]
    same = lax.rem(iota((rows, rows), 0), TILE) == lax.rem(iota((rows, rows), 1), TILE)
    total = jnp.where(same, total, 0.0)
    gram_ref[...] = jnp.sum(total.reshape(k_count, TILE, rows), axis=1)


def couple_kernel(
    cz, counts, x1_ref, x2_ref, y1_ref, y2_ref, rx1_ref, rx2_ref, ry1_ref, ry2_ref, b_ref, gram_ref, out_ref
):
    k_count = b_ref.shape[0]
    odd_x, _ = position("gx", counts[0])
    odd_y, _ = position("gy", counts[1])
    b = b_ref[...]
    gram = gram_ref[...]
    wide = gram.shape[1]
    spread = iota((k_count, wide), 1) // TILE == iota((k_count, wide), 0)

    def as_row(column):
        return jnp.sum(jnp.where(spread, column[:, :1], 0.0), axis=0, keepdims=True)

    def unpack(ref, layers):
        blocks = [ref[z * k_count : (z + 1) * k_count, :].astype(F32) for z in range(layers)]
        start = layers * k_count
        extra = ref[start : start + round_up(4 * layers, TILE), :].astype(F32)
        mobility, high, middle, low = (extra[n * layers : (n + 1) * layers] for n in range(4))
        return blocks, mobility, high + middle + low

    faces = []
    for own_ref, other_ref, layers in (
        (x1_ref, rx1_ref, 1),
        (x2_ref, rx2_ref, 1),
        (y1_ref, ry1_ref, cz),
        (y2_ref, ry2_ref, cz),
    ):
        own, own_mobility, own_field = unpack(own_ref, layers)
        other, other_mobility, other_field = unpack(other_ref, layers)
        faces.append((own, other, harmonic(own_mobility, other_mobility), own_field, other_field))

    b_row = as_row(b)
    along = jnp.zeros((k_count, LANES), F32)
    for own, _, conductance, own_field, other_field in faces:
        flow = conductance * (own_field - other_field)
        for z, block in enumerate(own):
            along = along + block * flow[z : z + 1]
    image = jnp.sum(along, axis=1, keepdims=True) + jnp.sum(gram * b_row, axis=1, keepdims=True)
    b_col = b[:, :1]
    source_square = jnp.sum(b_col * b_col, axis=0, keepdims=True)
    source_image = jnp.sum(b_col * image, axis=0, keepdims=True)
    quotient = source_image / jnp.maximum(source_square, TINY)
    v_col = image - quotient * b_col
    v_row = as_row(v_col)

    squares = [jnp.zeros((1, LANES), F32) for _ in range(3)]
    toward = []
    for own, other, conductance, own_field, _ in faces:
        v_field = jnp.concatenate([jnp.sum(block * v_col, axis=0, keepdims=True) for block in own], axis=0)
        flow_b = conductance * own_field
        flow_v = conductance * v_field
        for n, value in enumerate((flow_b * own_field, flow_b * v_field, flow_v * v_field)):
            squares[n] = squares[n] + jnp.sum(value, axis=0, keepdims=True)
        toward.append((other, flow_b, flow_v))
    for n, (left, right) in enumerate(((b_col, b_row), (b_col, v_row), (v_col, v_row))):
        value = jnp.sum(left * gram, axis=0, keepdims=True) * right
        for start in range(0, wide, LANES):
            squares[n] = squares[n] + value[:, start : start + LANES]
    squares = [jnp.sum(value, axis=1, keepdims=True) for value in squares]

    columns = [b_col, v_col]
    for first, second, odd in ((toward[0], toward[1], odd_x), (toward[2], toward[3], odd_y)):
        for which in (1, 2):
            product = jnp.zeros((k_count, LANES), F32)
            for z in range(len(first[0])):
                block = jnp.where(odd, second[0][z], first[0][z])
                flow = jnp.where(odd, second[which], first[which])
                product = product - block * flow[z : z + 1]
            columns.append(jnp.sum(product, axis=1, keepdims=True))
    lane = iota((k_count, LANES), 1)
    own_lane = lane - iota((k_count, LANES), 0)
    placed = jnp.zeros((k_count, LANES), F32)
    for n, column in enumerate(columns):
        placed = jnp.where(own_lane == n * k_count, column, placed)
    packed = jnp.sum(placed, axis=0, keepdims=True)
    lane = iota((1, LANES), 1)
    base = len(columns) * k_count
    for n, value in enumerate((quotient, *squares, source_square, source_image)):
        packed = jnp.where(lane == base + n, value, packed)
    out_ref[...] = jnp.broadcast_to(packed, out_ref.shape)


def finish_kernel(count_y, gathered_ref, own_ref, basis_ref, correction_ref, solution_ref):
    k_count, cz, cy, cx = basis_ref.shape
    base = 6 * k_count
    every = gathered_ref[...]
    lane = iota(every.shape, 1)

    def total(x):
        return jnp.sum(jnp.sum(x, axis=0, keepdims=True), axis=1, keepdims=True)

    def shifted(x, amount):
        return pltpu.roll(x, LANES - amount, 1)

    def up_rows(x, amount):
        return jnp.concatenate([x[amount:], x[:amount]], axis=0)

    sums = jnp.sum(every, axis=0, keepdims=True)
    energy = sums[:, base + 4 : base + 5]
    step = energy / (sums[:, base + 5 : base + 6] + EPSILON)
    quotient = every[:, base : base + 1]
    beside = shifted(every, k_count)
    remainder = every - step * (quotient * every + beside)
    renewed = total(jnp.where(lane < k_count, remainder * remainder, 0.0))
    ratio = renewed / (energy + EPSILON)
    weight = 1.0 + ratio - step * quotient
    mixed = weight * every - step * beside
    direction = jnp.where(lane < k_count, mixed, 0.0)
    cross = shifted(mixed, 2 * k_count) * up_rows(direction, count_y) + shifted(mixed, 4 * k_count) * up_rows(direction, 1)
    own_part = (
        weight * weight * every[:, base + 1 : base + 2]
        - 2.0 * weight * step * every[:, base + 2 : base + 3]
        + step * step * every[:, base + 3 : base + 4]
    )
    curvature = total(2.0 * cross) + jnp.sum(own_part, axis=0, keepdims=True)
    last_step = renewed / (curvature + EPSILON)

    own = own_ref[0:1, :]
    own_weight = 1.0 + ratio - step * own[:, base : base + 1]
    own_direction = own_weight * own - step * shifted(own, k_count)
    solution = step * own + last_step * own_direction
    solution_ref[...] = solution[:, :k_count]
    spread = iota((k_count, LANES), 0) == iota((k_count, LANES), 1)
    column = jnp.sum(jnp.where(spread, solution, 0.0), axis=1, keepdims=True)
    correction = jnp.zeros((cz, cy, cx), F32)
    for k in range(k_count):
        correction = correction + basis_ref[k].astype(F32) * column[k : k + 1][None]
    correction_ref[...] = correction


def exchange(message, axis, count, second):
    if second:
        pairs = [(i, (i - 1) % count if i % 2 == 0 else (i + 1) % count) for i in range(count)]
    else:
        pairs = [(i, i ^ 1) for i in range(count)]
    return lax.ppermute(message, axis, pairs)


def per_device(counts, basis, mobility, accumulation, residual):
    k_count, cz, cy, cx = basis.shape
    devices = counts[0] * counts[1]
    x_message = jax.ShapeDtypeStruct((k_count + TILE, cz * cy), BF16)
    y_message = jax.ShapeDtypeStruct((cz * k_count + round_up(4 * cz, TILE), cx), BF16)
    x1, x2, y1, y2, b = pl.pallas_call(
        functools.partial(edges_kernel, counts),
        out_shape=(x_message, x_message, y_message, y_message, jax.ShapeDtypeStruct((k_count, LANES), F32)),
        in_specs=[VMEM] * 3,
        out_specs=(VMEM,) * 5,
        compiler_params=PARAMS,
    )(basis, mobility, residual)
    rx1 = exchange(x1, "gx", counts[0], False)
    rx2 = exchange(x2, "gx", counts[0], True)
    ry1 = exchange(y1, "gy", counts[1], False)
    ry2 = exchange(y2, "gy", counts[1], True)
    gram = pl.pallas_call(
        gram_kernel,
        out_shape=jax.ShapeDtypeStruct((k_count, k_count * TILE), F32),
        in_specs=[VMEM] * 3,
        out_specs=VMEM,
        compiler_params=PARAMS,
        scratch_shapes=[pltpu.VMEM((2 * k_count * TILE, cz * cy // TILE * cx), BF16)],
        cost_estimate=pl.CostEstimate(flops=2 * 10**9, bytes_accessed=10**6, transcendentals=0),
    )(basis, mobility, accumulation)
    row = pl.pallas_call(
        functools.partial(couple_kernel, cz, counts),
        out_shape=jax.ShapeDtypeStruct((devices, LANES), F32),
        in_specs=[VMEM] * 10,
        out_specs=VMEM,
        compiler_params=PARAMS,
    )(x1, x2, y1, y2, rx1, rx2, ry1, ry2, b, gram)
    gathered = lax.all_to_all(row, ("gx", "gy"), 0, 0, tiled=True)
    correction, solution = pl.pallas_call(
        functools.partial(finish_kernel, counts[1]),
        out_shape=(jax.ShapeDtypeStruct((cz, cy, cx), F32), jax.ShapeDtypeStruct((1, k_count), F32)),
        in_specs=[VMEM] * 3,
        out_specs=(VMEM, VMEM),
        compiler_params=PARAMS,
    )(gathered, row, basis)
    return correction, solution.reshape(1, 1, k_count)


def solution(mesh):
    counts = (mesh.shape["gx"], mesh.shape["gy"])
    placed = (
        P(None, None, "gy", "gx"),
        P(None, "gy", "gx"),
        P(None, "gy", "gx"),
        P(None, "gy", "gx"),
    )
    return jax.shard_map(
        functools.partial(per_device, counts),
        mesh=mesh,
        in_specs=placed,
        out_specs=(P(None, "gy", "gx"), P("gx", "gy", None)),
        check_vma=False,
    )
```

```python
import functools

import jax
import jax.numpy as jnp
from jax import lax
from jax.experimental import pallas as pl
from jax.experimental.pallas import tpu as pltpu
from jax.sharding import PartitionSpec as P

ITERS = 2
EPSILON = 1e-6
VERTICAL_RATIO = 0.1
TINY = 1e-30
TILE = 16
LANES = 128

F32 = jnp.float32
BF16 = jnp.bfloat16
VMEM = pl.BlockSpec(memory_space=pltpu.VMEM)
HBM = pl.BlockSpec(memory_space=pltpu.HBM)
PARAMS = pltpu.CompilerParams(vmem_limit_bytes=8 * 2**20)


def iota(shape, dim):
    return lax.broadcasted_iota(jnp.int32, shape, dim)


def round_up(n, m):
    return (n + m - 1) // m * m


def harmonic(first, second):
    return 2.0 * first * second / jnp.maximum(first + second, TINY)


def dot_nt(a, b):
    return lax.dot_general(a, b, (((1,), (1,)), ((), ())), preferred_element_type=F32)


def three_terms(x):
    high = x.astype(BF16).astype(F32)
    rest = x - high
    middle = rest.astype(BF16).astype(F32)
    return high, middle, rest - middle


def position(axis, count):
    index = lax.axis_index(axis)
    odd = lax.rem(index, 2) == 1
    inner = jnp.logical_and(index > 0, index < count - 1)
    return odd, inner


def edges_kernel(
    counts,
    basis_hbm,
    mobility_hbm,
    accumulation_hbm,
    residual_hbm,
    x1_ref,
    x2_ref,
    y1_ref,
    y2_ref,
    b_ref,
    basis_ref,
    mobility_ref,
    accumulation_ref,
    residual_ref,
    chunk_sems,
    sems,
):
    k_count, cz, cy, cx = basis_ref.shape
    chunks = chunk_sems.shape[0]
    size = k_count // chunks
    residual_copy = pltpu.make_async_copy(residual_hbm, residual_ref, sems.at[0])
    residual_copy.start()
    chunk_copies = []
    for n in range(chunks):
        part = slice(n * size, (n + 1) * size)
        copy = pltpu.make_async_copy(basis_hbm.at[part], basis_ref.at[part], chunk_sems.at[n])
        copy.start()
        chunk_copies.append(copy)
    mobility_copy = pltpu.make_async_copy(mobility_hbm, mobility_ref, sems.at[1])
    mobility_copy.start()
    accumulation_copy = pltpu.make_async_copy(accumulation_hbm, accumulation_ref, sems.at[2])
    accumulation_copy.start()
    cells = cz * cy
    odd_x, inner_x = position("gx", counts[0])
    odd_y, inner_y = position("gy", counts[1])

    first = jnp.where(odd_x, 0, cx - 1)
    second = jnp.where(odd_x, cx - 1, 0)
    pick_row = iota((2 * k_count, cx), 0)
    pick_lane = iota((2 * k_count, cx), 1)
    wanted = pick_lane == jnp.where(pick_row < k_count, first, second)
    pick_k = jnp.where(pick_row < k_count, pick_row, pick_row - k_count)
    columns = jnp.zeros((2 * k_count, cells), F32)
    row = iota((k_count, cx), 0)
    partial = jnp.zeros((k_count, cx), F32)
    residual_copy.wait()
    residual = residual_ref[...]
    for k in range(k_count):
        if k % size == 0:
            chunk_copies[k // size].wait()
        pick = jnp.where(jnp.logical_and(wanted, pick_k == k), 1.0, 0.0).astype(BF16)
        columns = columns + dot_nt(pick, basis_ref[k].reshape(cells, cx))
        product = basis_ref[k].astype(F32) * residual
        total = jnp.sum(jnp.sum(product, axis=0), axis=0, keepdims=True)
        partial = jnp.where(row == k, total, partial)
    b = jnp.broadcast_to(jnp.sum(partial, axis=1, keepdims=True), (k_count, LANES))
    b_ref[...] = b
    mobility_copy.wait()
    pick_row = iota((TILE, cx), 0)
    pick_lane = iota((TILE, cx), 1)
    pick = jnp.where(pick_lane == jnp.where(pick_row == 0, first, second), 1.0, 0.0).astype(BF16)
    edge_mobility = dot_nt(pick, mobility_ref[...].reshape(cells, cx))

    for number, ref in ((0, x1_ref), (1, x2_ref)):
        edge = columns[number * k_count : (number + 1) * k_count]
        ref[0:k_count, :] = edge.astype(BF16)
        field = jnp.sum(edge * b[:, :1], axis=0, keepdims=True)
        mobility = edge_mobility[number : number + 1]
        if number == 1:
            mobility = jnp.where(inner_x, mobility, 0.0)
        row = iota((TILE, cells), 0)
        extra = jnp.zeros((TILE, cells), F32)
        for place, value in enumerate((mobility, *three_terms(field))):
            extra = jnp.where(row == place, value, extra)
        ref[k_count : k_count + TILE, :] = extra.astype(BF16)

    row = iota((k_count, cx), 0)
    extra_rows = round_up(4 * cz, TILE)
    extra_row = iota((extra_rows, cx), 0)
    extras = [jnp.zeros((extra_rows, cx), F32) for _ in range(2)]
    for z in range(cz):
        low = jnp.zeros((k_count, cx), F32)
        high = jnp.zeros((k_count, cx), F32)
        for k in range(k_count):
            low = jnp.where(row == k, basis_ref[k, z, 0:TILE, :].astype(F32)[0:1], low)
            high = jnp.where(row == k, basis_ref[k, z, cy - TILE : cy, :].astype(F32)[TILE - 1 : TILE], high)
        low_mobility = mobility_ref[z, 0:TILE, :].astype(F32)[0:1]
        high_mobility = mobility_ref[z, cy - TILE : cy, :].astype(F32)[TILE - 1 : TILE]
        for number, ref in ((0, y1_ref), (1, y2_ref)):
            use_low = odd_y if number == 0 else jnp.logical_not(odd_y)
            edge = jnp.where(use_low, low, high)
            mobility = jnp.where(use_low, low_mobility, high_mobility)
            if number == 1:
                mobility = jnp.where(inner_y, mobility, 0.0)
            ref[z * k_count : (z + 1) * k_count, :] = edge.astype(BF16)
            field = jnp.sum(edge * b[:, :1], axis=0, keepdims=True)
            for place, value in enumerate((mobility, *three_terms(field))):
                extras[number] = jnp.where(extra_row == place * cz + z, value, extras[number])
    for number, ref in ((0, y1_ref), (1, y2_ref)):
        ref[cz * k_count : cz * k_count + extra_rows, :] = extras[number].astype(BF16)
    accumulation_copy.wait()


def gram_kernel(basis_ref, mobility_ref, accumulation_ref, gram_ref, left_ref):
    k_count, cz, cy, cx = basis_ref.shape
    mobility = mobility_ref[...].astype(F32)
    accumulation = accumulation_ref[...]
    shape = mobility.shape
    along_x = jnp.where(iota(shape, 2) < cx - 1, harmonic(mobility, pltpu.roll(mobility, cx - 1, 2)), 0.0)
    along_y = jnp.where(iota(shape, 1) < cy - 1, harmonic(mobility, pltpu.roll(mobility, cy - 1, 1)), 0.0)
    along_z = VERTICAL_RATIO * harmonic(mobility[:-1], mobility[1:])
    rows = k_count * TILE
    strips = [(z, y) for z in range(cz) for y in range(0, cy, TILE)]
    for k in range(k_count):
        field = basis_ref[k].astype(F32)
        flow_x = along_x * (field - pltpu.roll(field, cx - 1, 2))
        image = accumulation * field + flow_x - pltpu.roll(flow_x, 1, 2)
        flow_y = along_y * (field - pltpu.roll(field, cy - 1, 1))
        image = image + flow_y - pltpu.roll(flow_y, 1, 1)
        flow_z = along_z * (field[:-1] - field[1:])
        nothing = jnp.zeros_like(field[:1])
        image = image + jnp.concatenate([flow_z, nothing], axis=0) - jnp.concatenate([nothing, flow_z], axis=0)
        high = image.astype(BF16)
        low = (image - high.astype(F32)).astype(BF16)
        for place, (z, y) in enumerate(strips):
            lanes = slice(place * cx, (place + 1) * cx)
            left_ref[k * TILE : (k + 1) * TILE, lanes] = high[z, y : y + TILE]
            left_ref[rows + k * TILE : rows + (k + 1) * TILE, lanes] = low[z, y : y + TILE]
    total = jnp.zeros((2 * rows, rows), F32)
    for place, (z, y) in enumerate(strips):
        right = basis_ref[:, z, y : y + TILE, :].reshape(rows, cx)
        total = total + dot_nt(left_ref[:, place * cx : (place + 1) * cx], right)
    total = total[:rows] + total[rows:]
    same = lax.rem(iota((rows, rows), 0), TILE) == lax.rem(iota((rows, rows), 1), TILE)
    total = jnp.where(same, total, 0.0)
    gram_ref[...] = jnp.sum(total.reshape(k_count, TILE, rows), axis=1)


def couple_kernel(
    cz, counts, x1_ref, x2_ref, y1_ref, y2_ref, rx1_ref, rx2_ref, ry1_ref, ry2_ref, b_ref, gram_ref, out_ref
):
    k_count = b_ref.shape[0]
    odd_x, _ = position("gx", counts[0])
    odd_y, _ = position("gy", counts[1])
    b = b_ref[...]
    gram = gram_ref[...]
    wide = gram.shape[1]
    spread = iota((k_count, wide), 1) // TILE == iota((k_count, wide), 0)

    def as_row(column):
        return jnp.sum(jnp.where(spread, column[:, :1], 0.0), axis=0, keepdims=True)

    def unpack(ref, layers):
        blocks = [ref[z * k_count : (z + 1) * k_count, :].astype(F32) for z in range(layers)]
        start = layers * k_count
        extra = ref[start : start + round_up(4 * layers, TILE), :].astype(F32)
        mobility, high, middle, low = (extra[n * layers : (n + 1) * layers] for n in range(4))
        return blocks, mobility, high + middle + low

    faces = []
    for own_ref, other_ref, layers in (
        (x1_ref, rx1_ref, 1),
        (x2_ref, rx2_ref, 1),
        (y1_ref, ry1_ref, cz),
        (y2_ref, ry2_ref, cz),
    ):
        own, own_mobility, own_field = unpack(own_ref, layers)
        other, other_mobility, other_field = unpack(other_ref, layers)
        faces.append((own, other, harmonic(own_mobility, other_mobility), own_field, other_field))

    b_row = as_row(b)
    along = jnp.zeros((k_count, LANES), F32)
    for own, _, conductance, own_field, other_field in faces:
        flow = conductance * (own_field - other_field)
        for z, block in enumerate(own):
            along = along + block * flow[z : z + 1]
    image = jnp.sum(along, axis=1, keepdims=True) + jnp.sum(gram * b_row, axis=1, keepdims=True)
    b_col = b[:, :1]
    source_square = jnp.sum(b_col * b_col, axis=0, keepdims=True)
    source_image = jnp.sum(b_col * image, axis=0, keepdims=True)
    quotient = source_image / jnp.maximum(source_square, TINY)
    v_col = image - quotient * b_col
    v_row = as_row(v_col)

    squares = [jnp.zeros((1, LANES), F32) for _ in range(3)]
    toward = []
    for own, other, conductance, own_field, _ in faces:
        v_field = jnp.concatenate([jnp.sum(block * v_col, axis=0, keepdims=True) for block in own], axis=0)
        flow_b = conductance * own_field
        flow_v = conductance * v_field
        for n, value in enumerate((flow_b * own_field, flow_b * v_field, flow_v * v_field)):
            squares[n] = squares[n] + jnp.sum(value, axis=0, keepdims=True)
        toward.append((other, flow_b, flow_v))
    for n, (left, right) in enumerate(((b_col, b_row), (b_col, v_row), (v_col, v_row))):
        value = jnp.sum(left * gram, axis=0, keepdims=True) * right
        for start in range(0, wide, LANES):
            squares[n] = squares[n] + value[:, start : start + LANES]
    squares = [jnp.sum(value, axis=1, keepdims=True) for value in squares]

    columns = [b_col, v_col]
    for first, second, odd in ((toward[0], toward[1], odd_x), (toward[2], toward[3], odd_y)):
        for which in (1, 2):
            product = jnp.zeros((k_count, LANES), F32)
            for z in range(len(first[0])):
                block = jnp.where(odd, second[0][z], first[0][z])
                flow = jnp.where(odd, second[which], first[which])
                product = product - block * flow[z : z + 1]
            columns.append(jnp.sum(product, axis=1, keepdims=True))
    lane = iota((k_count, LANES), 1)
    own_lane = lane - iota((k_count, LANES), 0)
    placed = jnp.zeros((k_count, LANES), F32)
    for n, column in enumerate(columns):
        placed = jnp.where(own_lane == n * k_count, column, placed)
    packed = jnp.sum(placed, axis=0, keepdims=True)
    lane = iota((1, LANES), 1)
    base = len(columns) * k_count
    for n, value in enumerate((quotient, *squares, source_square, source_image)):
        packed = jnp.where(lane == base + n, value, packed)
    out_ref[...] = jnp.broadcast_to(packed, out_ref.shape)


def finish_kernel(count_y, gathered_ref, own_ref, basis_ref, correction_hbm, solution_ref, correction_ref, sems):
    k_count, cz, cy, cx = basis_ref.shape
    base = 6 * k_count
    every = gathered_ref[...]
    lane = iota(every.shape, 1)

    def total(x):
        return jnp.sum(jnp.sum(x, axis=0, keepdims=True), axis=1, keepdims=True)

    def shifted(x, amount):
        return pltpu.roll(x, LANES - amount, 1)

    def up_rows(x, amount):
        return jnp.concatenate([x[amount:], x[:amount]], axis=0)

    sums = jnp.sum(every, axis=0, keepdims=True)
    energy = sums[:, base + 4 : base + 5]
    step = energy / (sums[:, base + 5 : base + 6] + EPSILON)
    quotient = every[:, base : base + 1]
    beside = shifted(every, k_count)
    remainder = every - step * (quotient * every + beside)
    renewed = total(jnp.where(lane < k_count, remainder * remainder, 0.0))
    ratio = renewed / (energy + EPSILON)
    weight = 1.0 + ratio - step * quotient
    mixed = weight * every - step * beside
    direction = jnp.where(lane < k_count, mixed, 0.0)
    cross = shifted(mixed, 2 * k_count) * up_rows(direction, count_y) + shifted(mixed, 4 * k_count) * up_rows(direction, 1)
    own_part = (
        weight * weight * every[:, base + 1 : base + 2]
        - 2.0 * weight * step * every[:, base + 2 : base + 3]
        + step * step * every[:, base + 3 : base + 4]
    )
    curvature = total(2.0 * cross) + jnp.sum(own_part, axis=0, keepdims=True)
    last_step = renewed / (curvature + EPSILON)

    own = own_ref[0:1, :]
    own_weight = 1.0 + ratio - step * own[:, base : base + 1]
    own_direction = own_weight * own - step * shifted(own, k_count)
    solution = step * own + last_step * own_direction
    solution_ref[...] = solution[:, :k_count]
    spread = iota((k_count, LANES), 0) == iota((k_count, LANES), 1)
    column = jnp.sum(jnp.where(spread, solution, 0.0), axis=1, keepdims=True)
    copies = []
    for z in range(cz):
        layer = jnp.zeros((cy, cx), F32)
        for k in range(k_count):
            layer = layer + basis_ref[k, z].astype(F32) * column[k : k + 1]
        correction_ref[z] = layer
        copy = pltpu.make_async_copy(correction_ref.at[z], correction_hbm.at[z], sems.at[z])
        copy.start()
        copies.append(copy)
    for copy in copies:
        copy.wait()


def exchange(message, axis, count, second):
    if second:
        pairs = [(i, (i - 1) % count if i % 2 == 0 else (i + 1) % count) for i in range(count)]
    else:
        pairs = [(i, i ^ 1) for i in range(count)]
    return lax.ppermute(message, axis, pairs)


def per_device(counts, basis, mobility, accumulation, residual):
    k_count, cz, cy, cx = basis.shape
    devices = counts[0] * counts[1]
    x_message = jax.ShapeDtypeStruct((k_count + TILE, cz * cy), BF16)
    y_message = jax.ShapeDtypeStruct((cz * k_count + round_up(4 * cz, TILE), cx), BF16)
    chunks = 8 if k_count % 8 == 0 else 1
    inputs = [pltpu.with_memory_space_constraint(x, pltpu.HBM) for x in (basis, mobility, accumulation, residual)]
    x1, x2, y1, y2, b, basis, mobility, accumulation = pl.pallas_call(
        functools.partial(edges_kernel, counts),
        out_shape=(
            x_message,
            x_message,
            y_message,
            y_message,
            jax.ShapeDtypeStruct((k_count, LANES), F32),
            jax.ShapeDtypeStruct(basis.shape, BF16),
            jax.ShapeDtypeStruct(mobility.shape, BF16),
            jax.ShapeDtypeStruct(accumulation.shape, F32),
        ),
        in_specs=[HBM] * 4,
        out_specs=(VMEM,) * 8,
        scratch_shapes=[
            pltpu.VMEM(residual.shape, F32),
            pltpu.SemaphoreType.DMA((chunks,)),
            pltpu.SemaphoreType.DMA((3,)),
        ],
        compiler_params=PARAMS,
    )(*inputs)
    rx1 = exchange(x1, "gx", counts[0], False)
    rx2 = exchange(x2, "gx", counts[0], True)
    ry1 = exchange(y1, "gy", counts[1], False)
    ry2 = exchange(y2, "gy", counts[1], True)
    gram = pl.pallas_call(
        gram_kernel,
        out_shape=jax.ShapeDtypeStruct((k_count, k_count * TILE), F32),
        in_specs=[VMEM] * 3,
        out_specs=VMEM,
        compiler_params=PARAMS,
        scratch_shapes=[pltpu.VMEM((2 * k_count * TILE, cz * cy // TILE * cx), BF16)],
        cost_estimate=pl.CostEstimate(flops=2 * 10**9, bytes_accessed=10**6, transcendentals=0),
    )(basis, mobility, accumulation)
    row = pl.pallas_call(
        functools.partial(couple_kernel, cz, counts),
        out_shape=jax.ShapeDtypeStruct((devices, LANES), F32),
        in_specs=[VMEM] * 10,
        out_specs=VMEM,
        compiler_params=PARAMS,
    )(x1, x2, y1, y2, rx1, rx2, ry1, ry2, b, gram)
    gathered = lax.all_to_all(row, ("gx", "gy"), 0, 0, tiled=True)
    correction, solution = pl.pallas_call(
        functools.partial(finish_kernel, counts[1]),
        out_shape=(jax.ShapeDtypeStruct((cz, cy, cx), F32), jax.ShapeDtypeStruct((1, k_count), F32)),
        in_specs=[VMEM] * 3,
        out_specs=(HBM, VMEM),
        scratch_shapes=[pltpu.VMEM((cz, cy, cx), F32), pltpu.SemaphoreType.DMA((cz,))],
        compiler_params=PARAMS,
    )(gathered, row, basis)
    return correction, solution.reshape(1, 1, k_count)


def solution(mesh):
    counts = (mesh.shape["gx"], mesh.shape["gy"])
    placed = (
        P(None, None, "gy", "gx"),
        P(None, "gy", "gx"),
        P(None, "gy", "gx"),
        P(None, "gy", "gx"),
    )
    return jax.shard_map(
        functools.partial(per_device, counts),
        mesh=mesh,
        in_specs=placed,
        out_specs=(P(None, "gy", "gx"), P("gx", "gy", None)),
        check_vma=False,
    )
```

```python
import functools

import jax
import jax.numpy as jnp
from jax import lax
from jax.experimental import pallas as pl
from jax.experimental.pallas import tpu as pltpu
from jax.sharding import PartitionSpec as P

ITERS = 2
EPSILON = 1e-6
VERTICAL_RATIO = 0.1
TINY = 1e-30
TILE = 16
LANES = 128

F32 = jnp.float32
BF16 = jnp.bfloat16
VMEM = pl.BlockSpec(memory_space=pltpu.VMEM)
HBM = pl.BlockSpec(memory_space=pltpu.HBM)
PARAMS = pltpu.CompilerParams(vmem_limit_bytes=8 * 2**20)


def iota(shape, dim):
    return lax.broadcasted_iota(jnp.int32, shape, dim)


def round_up(n, m):
    return (n + m - 1) // m * m


def harmonic(first, second):
    return 2.0 * first * second / jnp.maximum(first + second, TINY)


def dot_nt(a, b):
    return lax.dot_general(a, b, (((1,), (1,)), ((), ())), preferred_element_type=F32)


def three_terms(x):
    high = x.astype(BF16).astype(F32)
    rest = x - high
    middle = rest.astype(BF16).astype(F32)
    return high, middle, rest - middle


def position(axis, count):
    index = lax.axis_index(axis)
    odd = lax.rem(index, 2) == 1
    inner = jnp.logical_and(index > 0, index < count - 1)
    return odd, inner


def edges_kernel(
    counts,
    basis_hbm,
    mobility_hbm,
    accumulation_hbm,
    residual_hbm,
    x1_ref,
    x2_ref,
    y1_ref,
    y2_ref,
    b_ref,
    basis_ref,
    mobility_ref,
    accumulation_ref,
    residual_ref,
    chunk_sems,
    sems,
):
    k_count, cz, cy, cx = basis_ref.shape
    chunks = chunk_sems.shape[0]
    size = k_count // chunks
    residual_copy = pltpu.make_async_copy(residual_hbm, residual_ref, sems.at[0])
    residual_copy.start()
    chunk_copies = []
    for n in range(chunks):
        part = slice(n * size, (n + 1) * size)
        copy = pltpu.make_async_copy(basis_hbm.at[part], basis_ref.at[part], chunk_sems.at[n])
        copy.start()
        chunk_copies.append(copy)
    mobility_copy = pltpu.make_async_copy(mobility_hbm, mobility_ref, sems.at[1])
    mobility_copy.start()
    accumulation_copy = pltpu.make_async_copy(accumulation_hbm, accumulation_ref, sems.at[2])
    accumulation_copy.start()
    cells = cz * cy
    odd_x, inner_x = position("gx", counts[0])
    odd_y, inner_y = position("gy", counts[1])

    first = jnp.where(odd_x, 0, cx - 1)
    second = jnp.where(odd_x, cx - 1, 0)
    pick_row = iota((2 * k_count, cx), 0)
    pick_lane = iota((2 * k_count, cx), 1)
    wanted = pick_lane == jnp.where(pick_row < k_count, first, second)
    pick_k = jnp.where(pick_row < k_count, pick_row, pick_row - k_count)
    columns = jnp.zeros((2 * k_count, cells), F32)
    row = iota((k_count, cx), 0)
    partial = jnp.zeros((k_count, cx), F32)
    residual_copy.wait()
    residual = residual_ref[...]
    for k in range(k_count):
        if k % size == 0:
            chunk_copies[k // size].wait()
        pick = jnp.where(jnp.logical_and(wanted, pick_k == k), 1.0, 0.0).astype(BF16)
        columns = columns + dot_nt(pick, basis_ref[k].reshape(cells, cx))
        product = basis_ref[k].astype(F32) * residual
        total = jnp.sum(jnp.sum(product, axis=0), axis=0, keepdims=True)
        partial = jnp.where(row == k, total, partial)
    b = jnp.broadcast_to(jnp.sum(partial, axis=1, keepdims=True), (k_count, LANES))
    b_ref[...] = b
    mobility_copy.wait()
    pick_row = iota((TILE, cx), 0)
    pick_lane = iota((TILE, cx), 1)
    pick = jnp.where(pick_lane == jnp.where(pick_row == 0, first, second), 1.0, 0.0).astype(BF16)
    edge_mobility = dot_nt(pick, mobility_ref[...].reshape(cells, cx))

    for number, ref in ((0, x1_ref), (1, x2_ref)):
        edge = columns[number * k_count : (number + 1) * k_count]
        ref[0:k_count, :] = edge.astype(BF16)
        field = jnp.sum(edge * b[:, :1], axis=0, keepdims=True)
        mobility = edge_mobility[number : number + 1]
        if number == 1:
            mobility = jnp.where(inner_x, mobility, 0.0)
        row = iota((TILE, cells), 0)
        extra = jnp.zeros((TILE, cells), F32)
        for place, value in enumerate((mobility, *three_terms(field))):
            extra = jnp.where(row == place, value, extra)
        ref[k_count : k_count + TILE, :] = extra.astype(BF16)

    row = iota((k_count, cx), 0)
    extra_rows = round_up(4 * cz, TILE)
    extra_row = iota((extra_rows, cx), 0)
    extras = [jnp.zeros((extra_rows, cx), F32) for _ in range(2)]
    for z in range(cz):
        low = jnp.zeros((k_count, cx), F32)
        high = jnp.zeros((k_count, cx), F32)
        for k in range(k_count):
            low = jnp.where(row == k, basis_ref[k, z, 0:TILE, :].astype(F32)[0:1], low)
            high = jnp.where(row == k, basis_ref[k, z, cy - TILE : cy, :].astype(F32)[TILE - 1 : TILE], high)
        low_mobility = mobility_ref[z, 0:TILE, :].astype(F32)[0:1]
        high_mobility = mobility_ref[z, cy - TILE : cy, :].astype(F32)[TILE - 1 : TILE]
        for number, ref in ((0, y1_ref), (1, y2_ref)):
            use_low = odd_y if number == 0 else jnp.logical_not(odd_y)
            edge = jnp.where(use_low, low, high)
            mobility = jnp.where(use_low, low_mobility, high_mobility)
            if number == 1:
                mobility = jnp.where(inner_y, mobility, 0.0)
            ref[z * k_count : (z + 1) * k_count, :] = edge.astype(BF16)
            field = jnp.sum(edge * b[:, :1], axis=0, keepdims=True)
            for place, value in enumerate((mobility, *three_terms(field))):
                extras[number] = jnp.where(extra_row == place * cz + z, value, extras[number])
    for number, ref in ((0, y1_ref), (1, y2_ref)):
        ref[cz * k_count : cz * k_count + extra_rows, :] = extras[number].astype(BF16)
    accumulation_copy.wait()


def gram_kernel(basis_ref, mobility_ref, accumulation_ref, gram_ref, left_ref):
    k_count, cz, cy, cx = basis_ref.shape
    mobility = mobility_ref[...].astype(F32)
    accumulation = accumulation_ref[...]
    shape = mobility.shape
    along_x = jnp.where(iota(shape, 2) < cx - 1, harmonic(mobility, pltpu.roll(mobility, cx - 1, 2)), 0.0)
    along_y = jnp.where(iota(shape, 1) < cy - 1, harmonic(mobility, pltpu.roll(mobility, cy - 1, 1)), 0.0)
    along_z = VERTICAL_RATIO * harmonic(mobility[:-1], mobility[1:])
    rows = k_count * TILE
    strips = [(z, y) for z in range(cz) for y in range(0, cy, TILE)]
    for k in range(k_count):
        field = basis_ref[k].astype(F32)
        flow_x = along_x * (field - pltpu.roll(field, cx - 1, 2))
        image = accumulation * field + flow_x - pltpu.roll(flow_x, 1, 2)
        flow_y = along_y * (field - pltpu.roll(field, cy - 1, 1))
        image = image + flow_y - pltpu.roll(flow_y, 1, 1)
        flow_z = along_z * (field[:-1] - field[1:])
        nothing = jnp.zeros_like(field[:1])
        image = image + jnp.concatenate([flow_z, nothing], axis=0) - jnp.concatenate([nothing, flow_z], axis=0)
        high = image.astype(BF16)
        low = (image - high.astype(F32)).astype(BF16)
        for place, (z, y) in enumerate(strips):
            lanes = slice(place * cx, (place + 1) * cx)
            left_ref[k * TILE : (k + 1) * TILE, lanes] = high[z, y : y + TILE]
            left_ref[rows + k * TILE : rows + (k + 1) * TILE, lanes] = low[z, y : y + TILE]
    total = jnp.zeros((2 * rows, rows), F32)
    for place, (z, y) in enumerate(strips):
        right = basis_ref[:, z, y : y + TILE, :].reshape(rows, cx)
        total = total + dot_nt(left_ref[:, place * cx : (place + 1) * cx], right)
    total = total[:rows] + total[rows:]
    same = lax.rem(iota((rows, rows), 0), TILE) == lax.rem(iota((rows, rows), 1), TILE)
    total = jnp.where(same, total, 0.0)
    gram_ref[...] = jnp.sum(total.reshape(k_count, TILE, rows), axis=1)


def couple_kernel(
    cz, counts, x1_ref, x2_ref, y1_ref, y2_ref, rx1_ref, rx2_ref, ry1_ref, ry2_ref, b_ref, gram_ref, out_ref
):
    k_count = b_ref.shape[0]
    odd_x, _ = position("gx", counts[0])
    odd_y, _ = position("gy", counts[1])
    b = b_ref[...]
    gram = gram_ref[...]
    wide = gram.shape[1]
    spread = iota((k_count, wide), 1) // TILE == iota((k_count, wide), 0)

    def as_row(column):
        return jnp.sum(jnp.where(spread, column[:, :1], 0.0), axis=0, keepdims=True)

    def unpack(ref, layers):
        blocks = [ref[z * k_count : (z + 1) * k_count, :].astype(F32) for z in range(layers)]
        start = layers * k_count
        extra = ref[start : start + round_up(4 * layers, TILE), :].astype(F32)
        mobility, high, middle, low = (extra[n * layers : (n + 1) * layers] for n in range(4))
        return blocks, mobility, high + middle + low

    faces = []
    for own_ref, other_ref, layers in (
        (x1_ref, rx1_ref, 1),
        (x2_ref, rx2_ref, 1),
        (y1_ref, ry1_ref, cz),
        (y2_ref, ry2_ref, cz),
    ):
        own, own_mobility, own_field = unpack(own_ref, layers)
        other, other_mobility, other_field = unpack(other_ref, layers)
        faces.append((own, other, harmonic(own_mobility, other_mobility), own_field, other_field))

    b_row = as_row(b)
    along = jnp.zeros((k_count, LANES), F32)
    for own, _, conductance, own_field, other_field in faces:
        flow = conductance * (own_field - other_field)
        for z, block in enumerate(own):
            along = along + block * flow[z : z + 1]
    image = jnp.sum(along, axis=1, keepdims=True) + jnp.sum(gram * b_row, axis=1, keepdims=True)
    b_col = b[:, :1]
    source_square = jnp.sum(b_col * b_col, axis=0, keepdims=True)
    source_image = jnp.sum(b_col * image, axis=0, keepdims=True)
    quotient = source_image / jnp.maximum(source_square, TINY)
    v_col = image - quotient * b_col
    v_row = as_row(v_col)

    squares = [jnp.zeros((1, LANES), F32) for _ in range(3)]
    toward = []
    for own, other, conductance, own_field, _ in faces:
        v_field = jnp.concatenate([jnp.sum(block * v_col, axis=0, keepdims=True) for block in own], axis=0)
        flow_b = conductance * own_field
        flow_v = conductance * v_field
        for n, value in enumerate((flow_b * own_field, flow_b * v_field, flow_v * v_field)):
            squares[n] = squares[n] + jnp.sum(value, axis=0, keepdims=True)
        toward.append((other, flow_b, flow_v))
    for n, (left, right) in enumerate(((b_col, b_row), (b_col, v_row), (v_col, v_row))):
        value = jnp.sum(left * gram, axis=0, keepdims=True) * right
        for start in range(0, wide, LANES):
            squares[n] = squares[n] + value[:, start : start + LANES]
    squares = [jnp.sum(value, axis=1, keepdims=True) for value in squares]

    columns = [b_col, v_col]
    for first, second, odd in ((toward[0], toward[1], odd_x), (toward[2], toward[3], odd_y)):
        for which in (1, 2):
            product = jnp.zeros((k_count, LANES), F32)
            for z in range(len(first[0])):
                block = jnp.where(odd, second[0][z], first[0][z])
                flow = jnp.where(odd, second[which], first[which])
                product = product - block * flow[z : z + 1]
            columns.append(jnp.sum(product, axis=1, keepdims=True))
    lane = iota((k_count, LANES), 1)
    own_lane = lane - iota((k_count, LANES), 0)
    placed = jnp.zeros((k_count, LANES), F32)
    for n, column in enumerate(columns):
        placed = jnp.where(own_lane == n * k_count, column, placed)
    packed = jnp.sum(placed, axis=0, keepdims=True)
    lane = iota((1, LANES), 1)
    base = len(columns) * k_count
    for n, value in enumerate((quotient, *squares, source_square, source_image)):
        packed = jnp.where(lane == base + n, value, packed)
    out_ref[...] = jnp.broadcast_to(packed, out_ref.shape)


def finish_kernel(count_y, gathered_ref, own_ref, basis_ref, correction_hbm, solution_hbm, correction_ref, solution_ref, sems):
    k_count, cz, cy, cx = basis_ref.shape
    base = 6 * k_count
    every = gathered_ref[...]
    lane = iota(every.shape, 1)

    def total(x):
        return jnp.sum(jnp.sum(x, axis=0, keepdims=True), axis=1, keepdims=True)

    def shifted(x, amount):
        return pltpu.roll(x, LANES - amount, 1)

    def up_rows(x, amount):
        return jnp.concatenate([x[amount:], x[:amount]], axis=0)

    sums = jnp.sum(every, axis=0, keepdims=True)
    energy = sums[:, base + 4 : base + 5]
    step = energy / (sums[:, base + 5 : base + 6] + EPSILON)
    quotient = every[:, base : base + 1]
    beside = shifted(every, k_count)
    remainder = every - step * (quotient * every + beside)
    renewed = total(jnp.where(lane < k_count, remainder * remainder, 0.0))
    ratio = renewed / (energy + EPSILON)
    weight = 1.0 + ratio - step * quotient
    mixed = weight * every - step * beside
    direction = jnp.where(lane < k_count, mixed, 0.0)
    cross = shifted(mixed, 2 * k_count) * up_rows(direction, count_y) + shifted(mixed, 4 * k_count) * up_rows(direction, 1)
    own_part = (
        weight * weight * every[:, base + 1 : base + 2]
        - 2.0 * weight * step * every[:, base + 2 : base + 3]
        + step * step * every[:, base + 3 : base + 4]
    )
    curvature = total(2.0 * cross) + jnp.sum(own_part, axis=0, keepdims=True)
    last_step = renewed / (curvature + EPSILON)

    own = own_ref[0:1, :]
    own_weight = 1.0 + ratio - step * own[:, base : base + 1]
    own_direction = own_weight * own - step * shifted(own, k_count)
    solution = step * own + last_step * own_direction
    solution_ref[...] = solution[:, :k_count]
    copies = [pltpu.make_async_copy(solution_ref, solution_hbm, sems.at[cz])]
    copies[0].start()
    spread = iota((k_count, LANES), 0) == iota((k_count, LANES), 1)
    column = jnp.sum(jnp.where(spread, solution, 0.0), axis=1, keepdims=True)
    for z in range(cz):
        layer = jnp.zeros((cy, cx), F32)
        for k in range(k_count):
            layer = layer + basis_ref[k, z].astype(F32) * column[k : k + 1]
        correction_ref[z] = layer
        copy = pltpu.make_async_copy(correction_ref.at[z], correction_hbm.at[z], sems.at[z])
        copy.start()
        copies.append(copy)
    for copy in copies:
        copy.wait()


def exchange(message, axis, counts, second):
    count_x, count_y = counts
    pairs = []
    for x in range(count_x):
        for y in range(count_y):
            i, count = (x, count_x) if axis == "gx" else (y, count_y)
            j = i ^ 1
            if second:
                j = i - 1 if i % 2 == 0 else i + 1
            if 0 <= j < count:
                partner = (j, y) if axis == "gx" else (x, j)
            else:
                partner = (x, y ^ 1) if axis == "gx" else (x ^ 1, y)
            pairs.append((x * count_y + y, partner[0] * count_y + partner[1]))
    return lax.ppermute(message, ("gx", "gy"), pairs)


def per_device(counts, basis, mobility, accumulation, residual):
    k_count, cz, cy, cx = basis.shape
    devices = counts[0] * counts[1]
    x_message = jax.ShapeDtypeStruct((k_count + TILE, cz * cy), BF16)
    y_message = jax.ShapeDtypeStruct((cz * k_count + round_up(4 * cz, TILE), cx), BF16)
    chunks = 8 if k_count % 8 == 0 else 1
    inputs = [pltpu.with_memory_space_constraint(x, pltpu.HBM) for x in (basis, mobility, accumulation, residual)]
    x1, x2, y1, y2, b, basis, mobility, accumulation = pl.pallas_call(
        functools.partial(edges_kernel, counts),
        out_shape=(
            x_message,
            x_message,
            y_message,
            y_message,
            jax.ShapeDtypeStruct((k_count, LANES), F32),
            jax.ShapeDtypeStruct(basis.shape, BF16),
            jax.ShapeDtypeStruct(mobility.shape, BF16),
            jax.ShapeDtypeStruct(accumulation.shape, F32),
        ),
        in_specs=[HBM] * 4,
        out_specs=(VMEM,) * 8,
        scratch_shapes=[
            pltpu.VMEM(residual.shape, F32),
            pltpu.SemaphoreType.DMA((chunks,)),
            pltpu.SemaphoreType.DMA((3,)),
        ],
        compiler_params=PARAMS,
    )(*inputs)
    rx1 = exchange(x1, "gx", counts, False)
    rx2 = exchange(x2, "gx", counts, True)
    ry1 = exchange(y1, "gy", counts, False)
    ry2 = exchange(y2, "gy", counts, True)
    gram = pl.pallas_call(
        gram_kernel,
        out_shape=jax.ShapeDtypeStruct((k_count, k_count * TILE), F32),
        in_specs=[VMEM] * 3,
        out_specs=VMEM,
        compiler_params=PARAMS,
        scratch_shapes=[pltpu.VMEM((2 * k_count * TILE, cz * cy // TILE * cx), BF16)],
        cost_estimate=pl.CostEstimate(flops=2 * 10**9, bytes_accessed=10**6, transcendentals=0),
    )(basis, mobility, accumulation)
    row = pl.pallas_call(
        functools.partial(couple_kernel, cz, counts),
        out_shape=jax.ShapeDtypeStruct((devices, LANES), F32),
        in_specs=[VMEM] * 10,
        out_specs=VMEM,
        compiler_params=PARAMS,
    )(x1, x2, y1, y2, rx1, rx2, ry1, ry2, b, gram)
    gathered = lax.all_to_all(row, ("gx", "gy"), 0, 0, tiled=True)
    correction, solution = pl.pallas_call(
        functools.partial(finish_kernel, counts[1]),
        out_shape=(jax.ShapeDtypeStruct((cz, cy, cx), F32), jax.ShapeDtypeStruct((1, k_count), F32)),
        in_specs=[VMEM] * 3,
        out_specs=(HBM, HBM),
        scratch_shapes=[
            pltpu.VMEM((cz, cy, cx), F32),
            pltpu.VMEM((1, k_count), F32),
            pltpu.SemaphoreType.DMA((cz + 1,)),
        ],
        compiler_params=PARAMS,
    )(gathered, row, basis)
    return correction, solution.reshape(1, 1, k_count)


def solution(mesh):
    counts = (mesh.shape["gx"], mesh.shape["gy"])
    placed = (
        P(None, None, "gy", "gx"),
        P(None, "gy", "gx"),
        P(None, "gy", "gx"),
        P(None, "gy", "gx"),
    )
    return jax.shard_map(
        functools.partial(per_device, counts),
        mesh=mesh,
        in_specs=placed,
        out_specs=(P(None, "gy", "gx"), P("gx", "gy", None)),
        check_vma=False,
    )
```

```python
import functools

import jax
import jax.numpy as jnp
from jax import lax
from jax.experimental import pallas as pl
from jax.experimental.pallas import tpu as pltpu
from jax.sharding import PartitionSpec as P

ITERS = 2
EPSILON = 1e-6
VERTICAL_RATIO = 0.1
TINY = 1e-30
TILE = 16
LANES = 128

F32 = jnp.float32
BF16 = jnp.bfloat16
VMEM = pl.BlockSpec(memory_space=pltpu.VMEM)
HBM = pl.BlockSpec(memory_space=pltpu.HBM)
PARAMS = pltpu.CompilerParams(vmem_limit_bytes=8 * 2**20)


def iota(shape, dim):
    return lax.broadcasted_iota(jnp.int32, shape, dim)


def round_up(n, m):
    return (n + m - 1) // m * m


def harmonic(first, second):
    return 2.0 * first * second / jnp.maximum(first + second, TINY)


def dot_nt(a, b):
    return lax.dot_general(a, b, (((1,), (1,)), ((), ())), preferred_element_type=F32)


def three_terms(x):
    high = x.astype(BF16).astype(F32)
    rest = x - high
    middle = rest.astype(BF16).astype(F32)
    return high, middle, rest - middle


def expand(basis_ref, column):
    field = basis_ref[0].astype(F32) * column[0:1][None]
    for k in range(1, basis_ref.shape[0]):
        field = field + basis_ref[k].astype(F32) * column[k : k + 1][None]
    return field


def position(axis, count):
    index = lax.axis_index(axis)
    odd = lax.rem(index, 2) == 1
    inner = jnp.logical_and(index > 0, index < count - 1)
    return odd, inner


def edges_kernel(
    counts,
    basis_hbm,
    mobility_hbm,
    accumulation_hbm,
    residual_hbm,
    x1_ref,
    x2_ref,
    y1_ref,
    y2_ref,
    b_ref,
    basis_ref,
    mobility_ref,
    accumulation_ref,
    residual_ref,
    chunk_sems,
    sems,
):
    k_count, cz, cy, cx = basis_ref.shape
    chunks = chunk_sems.shape[0]
    size = k_count // chunks
    residual_copy = pltpu.make_async_copy(residual_hbm, residual_ref, sems.at[0])
    residual_copy.start()
    chunk_copies = []
    for n in range(chunks):
        part = slice(n * size, (n + 1) * size)
        copy = pltpu.make_async_copy(basis_hbm.at[part], basis_ref.at[part], chunk_sems.at[n])
        copy.start()
        chunk_copies.append(copy)
    mobility_copy = pltpu.make_async_copy(mobility_hbm, mobility_ref, sems.at[1])
    mobility_copy.start()
    accumulation_copy = pltpu.make_async_copy(accumulation_hbm, accumulation_ref, sems.at[2])
    accumulation_copy.start()
    cells = cz * cy
    odd_x, inner_x = position("gx", counts[0])
    odd_y, inner_y = position("gy", counts[1])

    first = jnp.where(odd_x, 0, cx - 1)
    second = jnp.where(odd_x, cx - 1, 0)
    pick_row = iota((2 * k_count, cx), 0)
    pick_lane = iota((2 * k_count, cx), 1)
    wanted = pick_lane == jnp.where(pick_row < k_count, first, second)
    pick_k = jnp.where(pick_row < k_count, pick_row, pick_row - k_count)
    picks = [jnp.where(jnp.logical_and(wanted, pick_k == k), 1.0, 0.0).astype(BF16) for k in range(k_count)]
    pick_row = iota((TILE, cx), 0)
    pick_lane = iota((TILE, cx), 1)
    pick = jnp.where(pick_lane == jnp.where(pick_row == 0, first, second), 1.0, 0.0).astype(BF16)
    mobility_copy.wait()
    edge_mobility = dot_nt(pick, mobility_ref[...].reshape(cells, cx))
    residual_copy.wait()
    residual = residual_ref[...]

    row = iota((k_count, cx), 0)
    partial = jnp.zeros((k_count, cx), F32)
    for copy in chunk_copies:
        copy.wait()
    columns = dot_nt(
        jnp.concatenate(picks, axis=1), jnp.concatenate([basis_ref[k].reshape(cells, cx) for k in range(k_count)], axis=1)
    )
    for k in range(k_count):
        product = basis_ref[k].astype(F32) * residual
        total = jnp.sum(jnp.sum(product, axis=0), axis=0, keepdims=True)
        partial = jnp.where(row == k, total, partial)
    b = jnp.broadcast_to(jnp.sum(partial, axis=1, keepdims=True), (k_count, LANES))
    b_ref[...] = b

    for number, ref in ((0, x1_ref), (1, x2_ref)):
        edge = columns[number * k_count : (number + 1) * k_count]
        ref[0:k_count, :] = edge.astype(BF16)
        field = jnp.sum(edge * b[:, :1], axis=0, keepdims=True)
        mobility = edge_mobility[number : number + 1]
        if number == 1:
            mobility = jnp.where(inner_x, mobility, 0.0)
        row = iota((TILE, cells), 0)
        extra = jnp.zeros((TILE, cells), F32)
        for place, value in enumerate((mobility, *three_terms(field))):
            extra = jnp.where(row == place, value, extra)
        ref[k_count : k_count + TILE, :] = extra.astype(BF16)

    row = iota((k_count, cx), 0)
    extra_rows = round_up(4 * cz, TILE)
    extra_row = iota((extra_rows, cx), 0)
    extras = [jnp.zeros((extra_rows, cx), F32) for _ in range(2)]
    for z in range(cz):
        low = jnp.zeros((k_count, cx), F32)
        high = jnp.zeros((k_count, cx), F32)
        for k in range(k_count):
            low = jnp.where(row == k, basis_ref[k, z, 0:TILE, :].astype(F32)[0:1], low)
            high = jnp.where(row == k, basis_ref[k, z, cy - TILE : cy, :].astype(F32)[TILE - 1 : TILE], high)
        low_mobility = mobility_ref[z, 0:TILE, :].astype(F32)[0:1]
        high_mobility = mobility_ref[z, cy - TILE : cy, :].astype(F32)[TILE - 1 : TILE]
        for number, ref in ((0, y1_ref), (1, y2_ref)):
            use_low = odd_y if number == 0 else jnp.logical_not(odd_y)
            edge = jnp.where(use_low, low, high)
            mobility = jnp.where(use_low, low_mobility, high_mobility)
            if number == 1:
                mobility = jnp.where(inner_y, mobility, 0.0)
            ref[z * k_count : (z + 1) * k_count, :] = edge.astype(BF16)
            field = jnp.sum(edge * b[:, :1], axis=0, keepdims=True)
            for place, value in enumerate((mobility, *three_terms(field))):
                extras[number] = jnp.where(extra_row == place * cz + z, value, extras[number])
    for number, ref in ((0, y1_ref), (1, y2_ref)):
        ref[cz * k_count : cz * k_count + extra_rows, :] = extras[number].astype(BF16)
    accumulation_copy.wait()


def image_kernel(basis_ref, mobility_ref, accumulation_ref, b_ref, along_x_ref, along_y_ref, along_z_ref, image_ref):
    k_count, cz, cy, cx = basis_ref.shape
    mobility = mobility_ref[...].astype(F32)
    shape = mobility.shape
    along_x = jnp.where(iota(shape, 2) < cx - 1, harmonic(mobility, pltpu.roll(mobility, cx - 1, 2)), 0.0)
    along_y = jnp.where(iota(shape, 1) < cy - 1, harmonic(mobility, pltpu.roll(mobility, cy - 1, 1)), 0.0)
    along_z = VERTICAL_RATIO * harmonic(mobility[:-1], mobility[1:])
    along_x_ref[...] = along_x
    along_y_ref[...] = along_y
    along_z_ref[...] = along_z
    field = expand(basis_ref, b_ref[...])
    flow_x = along_x * (field - pltpu.roll(field, cx - 1, 2))
    image = accumulation_ref[...] * field + flow_x - pltpu.roll(flow_x, 1, 2)
    flow_y = along_y * (field - pltpu.roll(field, cy - 1, 1))
    image = image + flow_y - pltpu.roll(flow_y, 1, 1)
    flow_z = along_z * (field[:-1] - field[1:])
    nothing = jnp.zeros_like(field[:1])
    image = image + jnp.concatenate([flow_z, nothing], axis=0) - jnp.concatenate([nothing, flow_z], axis=0)
    row = iota((k_count, cx), 0)
    partial = jnp.zeros((k_count, cx), F32)
    for k in range(k_count):
        total = jnp.sum(jnp.sum(basis_ref[k].astype(F32) * image, axis=0), axis=0, keepdims=True)
        partial = jnp.where(row == k, total, partial)
    image_ref[...] = partial


def energy(field, accumulation, along_x, along_y, along_z):
    _, cy, cx = field.shape
    change_x = field - pltpu.roll(field, cx - 1, 2)
    change_y = field - pltpu.roll(field, cy - 1, 1)
    change_z = field[:-1] - field[1:]
    square = accumulation * field * field + along_x * change_x * change_x + along_y * change_y * change_y
    square = jnp.sum(square, axis=0) + jnp.sum(along_z * change_z * change_z, axis=0)
    return jnp.sum(square, axis=0, keepdims=True)


def couple_kernel(
    counts,
    x1_ref,
    x2_ref,
    y1_ref,
    y2_ref,
    rx2_ref,
    ry2_ref,
    ry1_ref,
    rx1_ref,
    b_ref,
    image_ref,
    basis_ref,
    accumulation_ref,
    along_x_ref,
    along_y_ref,
    along_z_ref,
    out_ref,
):
    k_count, cz, _, _ = basis_ref.shape
    odd_x, _ = position("gx", counts[0])
    odd_y, _ = position("gy", counts[1])
    b_col = b_ref[...]

    def unpack(ref, layers):
        blocks = [ref[z * k_count : (z + 1) * k_count, :].astype(F32) for z in range(layers)]
        start = layers * k_count
        extra = ref[start : start + round_up(4 * layers, TILE), :].astype(F32)
        mobility, high, middle, low = (extra[n * layers : (n + 1) * layers] for n in range(4))
        return blocks, mobility, high + middle + low

    faces = []
    for own_ref, other_ref, layers in (
        (x1_ref, rx1_ref, 1),
        (x2_ref, rx2_ref, 1),
        (y1_ref, ry1_ref, cz),
        (y2_ref, ry2_ref, cz),
    ):
        own, own_mobility, own_field = unpack(own_ref, layers)
        other, other_mobility, other_field = unpack(other_ref, layers)
        faces.append((own, other, harmonic(own_mobility, other_mobility), own_field, other_field))

    own_image = image_ref[...]
    along = own_image
    for own, _, conductance, own_field, other_field in faces:
        flow = conductance * (own_field - other_field)
        for z, block in enumerate(own):
            along = along + block * flow[z : z + 1]
    image = jnp.sum(along, axis=1, keepdims=True)
    source_square = jnp.sum(b_col * b_col, axis=0, keepdims=True)[:, :1]
    source_image = jnp.sum(b_col * image, axis=0, keepdims=True)[:, :1]
    quotient = source_image / jnp.maximum(source_square, TINY)
    v_col = image - quotient * b_col

    field = expand(basis_ref, v_col)
    squares = [
        jnp.sum(b_col * own_image, axis=0, keepdims=True),
        jnp.sum(v_col * own_image, axis=0, keepdims=True),
        energy(field, accumulation_ref[...], along_x_ref[...], along_y_ref[...], along_z_ref[...]),
    ]
    toward = []
    for own, other, conductance, own_field, _ in faces:
        v_field = jnp.concatenate([jnp.sum(block * v_col, axis=0, keepdims=True) for block in own], axis=0)
        flow_b = conductance * own_field
        flow_v = conductance * v_field
        for n, value in enumerate((flow_b * own_field, flow_b * v_field, flow_v * v_field)):
            squares[n] = squares[n] + jnp.sum(value, axis=0, keepdims=True)
        toward.append((other, flow_b, flow_v))
    squares = [jnp.sum(value, axis=1, keepdims=True) for value in squares]

    columns = [b_col, v_col]
    for first, second, odd in ((toward[0], toward[1], odd_x), (toward[2], toward[3], odd_y)):
        for which in (1, 2):
            product = jnp.zeros((k_count, LANES), F32)
            for z in range(len(first[0])):
                block = jnp.where(odd, second[0][z], first[0][z])
                flow = jnp.where(odd, second[which], first[which])
                product = product - block * flow[z : z + 1]
            columns.append(jnp.sum(product, axis=1, keepdims=True))
    lane = iota((k_count, LANES), 1)
    own_lane = lane - iota((k_count, LANES), 0)
    placed = jnp.zeros((k_count, LANES), F32)
    for n, column in enumerate(columns):
        placed = jnp.where(own_lane == n * k_count, column, placed)
    packed = jnp.sum(placed, axis=0, keepdims=True)
    lane = iota((1, LANES), 1)
    base = len(columns) * k_count
    for n, value in enumerate((quotient, *squares, source_square, source_image)):
        packed = jnp.where(lane == base + n, value, packed)
    out_ref[...] = jnp.broadcast_to(packed, out_ref.shape)


def finish_kernel(count_y, gathered_ref, own_ref, basis_ref, correction_hbm, solution_hbm, correction_ref, solution_ref, sems):
    k_count, cz, cy, cx = basis_ref.shape
    base = 6 * k_count
    every = gathered_ref[...]
    lane = iota(every.shape, 1)

    def total(x):
        return jnp.sum(jnp.sum(x, axis=0, keepdims=True), axis=1, keepdims=True)

    def shifted(x, amount):
        return pltpu.roll(x, LANES - amount, 1)

    def up_rows(x, amount):
        return jnp.concatenate([x[amount:], x[:amount]], axis=0)

    sums = jnp.sum(every, axis=0, keepdims=True)
    energy = sums[:, base + 4 : base + 5]
    step = energy / (sums[:, base + 5 : base + 6] + EPSILON)
    quotient = every[:, base : base + 1]
    beside = shifted(every, k_count)
    remainder = every - step * (quotient * every + beside)
    renewed = total(jnp.where(lane < k_count, remainder * remainder, 0.0))
    ratio = renewed / (energy + EPSILON)
    weight = 1.0 + ratio - step * quotient
    mixed = weight * every - step * beside
    direction = jnp.where(lane < k_count, mixed, 0.0)
    cross = shifted(mixed, 2 * k_count) * up_rows(direction, count_y) + shifted(mixed, 4 * k_count) * up_rows(direction, 1)
    own_part = (
        weight * weight * every[:, base + 1 : base + 2]
        - 2.0 * weight * step * every[:, base + 2 : base + 3]
        + step * step * every[:, base + 3 : base + 4]
    )
    curvature = total(2.0 * cross) + jnp.sum(own_part, axis=0, keepdims=True)
    last_step = renewed / (curvature + EPSILON)

    own = own_ref[0:1, :]
    own_weight = 1.0 + ratio - step * own[:, base : base + 1]
    own_direction = own_weight * own - step * shifted(own, k_count)
    solution = step * own + last_step * own_direction
    solution_ref[...] = solution[:, :k_count]
    copies = [pltpu.make_async_copy(solution_ref, solution_hbm, sems.at[cz])]
    copies[0].start()
    spread = iota((k_count, LANES), 0) == iota((k_count, LANES), 1)
    column = jnp.sum(jnp.where(spread, solution, 0.0), axis=1, keepdims=True)
    for z in range(cz):
        layer = jnp.zeros((cy, cx), F32)
        for k in range(k_count):
            layer = layer + basis_ref[k, z].astype(F32) * column[k : k + 1]
        correction_ref[z] = layer
        copy = pltpu.make_async_copy(correction_ref.at[z], correction_hbm.at[z], sems.at[z])
        copy.start()
        copies.append(copy)
    for copy in copies:
        copy.wait()


def exchange(message, axis, counts, second):
    count_x, count_y = counts
    pairs = []
    for x in range(count_x):
        for y in range(count_y):
            i, count = (x, count_x) if axis == "gx" else (y, count_y)
            j = i ^ 1
            if second:
                j = i - 1 if i % 2 == 0 else i + 1
            if 0 <= j < count:
                partner = (j, y) if axis == "gx" else (x, j)
            else:
                partner = (x, y ^ 1) if axis == "gx" else (x ^ 1, y)
            pairs.append((x * count_y + y, partner[0] * count_y + partner[1]))
    return lax.ppermute(message, ("gx", "gy"), pairs)


def per_device(counts, basis, mobility, accumulation, residual):
    k_count, cz, cy, cx = basis.shape
    devices = counts[0] * counts[1]
    x_message = jax.ShapeDtypeStruct((k_count + TILE, cz * cy), BF16)
    y_message = jax.ShapeDtypeStruct((cz * k_count + round_up(4 * cz, TILE), cx), BF16)
    chunks = 1
    inputs = [pltpu.with_memory_space_constraint(x, pltpu.HBM) for x in (basis, mobility, accumulation, residual)]
    x1, x2, y1, y2, b, basis, mobility, accumulation = pl.pallas_call(
        functools.partial(edges_kernel, counts),
        out_shape=(
            x_message,
            x_message,
            y_message,
            y_message,
            jax.ShapeDtypeStruct((k_count, LANES), F32),
            jax.ShapeDtypeStruct(basis.shape, BF16),
            jax.ShapeDtypeStruct(mobility.shape, BF16),
            jax.ShapeDtypeStruct(accumulation.shape, F32),
        ),
        in_specs=[HBM] * 4,
        out_specs=(VMEM,) * 8,
        scratch_shapes=[
            pltpu.VMEM(residual.shape, F32),
            pltpu.SemaphoreType.DMA((chunks,)),
            pltpu.SemaphoreType.DMA((3,)),
        ],
        compiler_params=PARAMS,
    )(*inputs)
    rx1 = exchange(x1, "gx", counts, False)
    rx2 = exchange(x2, "gx", counts, True)
    ry1 = exchange(y1, "gy", counts, False)
    ry2 = exchange(y2, "gy", counts, True)
    conductance = jax.ShapeDtypeStruct((cz, cy, cx), F32)
    layered = jax.ShapeDtypeStruct((cz - 1, cy, cx), F32)
    along_x, along_y, along_z, image = pl.pallas_call(
        image_kernel,
        out_shape=(conductance, conductance, layered, jax.ShapeDtypeStruct((k_count, cx), F32)),
        in_specs=[VMEM] * 4,
        out_specs=(VMEM,) * 4,
        compiler_params=PARAMS,
        cost_estimate=pl.CostEstimate(flops=10**8, bytes_accessed=10**6, transcendentals=0),
    )(basis, mobility, accumulation, b)
    row = pl.pallas_call(
        functools.partial(couple_kernel, counts),
        out_shape=jax.ShapeDtypeStruct((devices, LANES), F32),
        in_specs=[VMEM] * 15,
        out_specs=VMEM,
        compiler_params=PARAMS,
    )(x1, x2, y1, y2, rx2, ry2, ry1, rx1, b, image, basis, accumulation, along_x, along_y, along_z)
    gathered = lax.all_to_all(row, ("gx", "gy"), 0, 0, tiled=True)
    correction, solution = pl.pallas_call(
        functools.partial(finish_kernel, counts[1]),
        out_shape=(jax.ShapeDtypeStruct((cz, cy, cx), F32), jax.ShapeDtypeStruct((1, k_count), F32)),
        in_specs=[VMEM] * 3,
        out_specs=(HBM, HBM),
        scratch_shapes=[
            pltpu.VMEM((cz, cy, cx), F32),
            pltpu.VMEM((1, k_count), F32),
            pltpu.SemaphoreType.DMA((cz + 1,)),
        ],
        compiler_params=PARAMS,
    )(gathered, row, basis)
    return correction, solution.reshape(1, 1, k_count)


def solution(mesh):
    counts = (mesh.shape["gx"], mesh.shape["gy"])
    placed = (
        P(None, None, "gy", "gx"),
        P(None, "gy", "gx"),
        P(None, "gy", "gx"),
        P(None, "gy", "gx"),
    )
    return jax.shard_map(
        functools.partial(per_device, counts),
        mesh=mesh,
        in_specs=placed,
        out_specs=(P(None, "gy", "gx"), P("gx", "gy", None)),
        check_vma=False,
    )
```

```python
import functools

import jax
import jax.numpy as jnp
from jax import lax
from jax.experimental import pallas as pl
from jax.experimental.pallas import tpu as pltpu
from jax.sharding import PartitionSpec as P

ITERS = 2
EPSILON = 1e-6
VERTICAL_RATIO = 0.1
TINY = 1e-30
TILE = 16
LANES = 128

F32 = jnp.float32
BF16 = jnp.bfloat16
VMEM = pl.BlockSpec(memory_space=pltpu.VMEM)
HBM = pl.BlockSpec(memory_space=pltpu.HBM)
PARAMS = pltpu.CompilerParams(vmem_limit_bytes=8 * 2**20)


def iota(shape, dim):
    return lax.broadcasted_iota(jnp.int32, shape, dim)


def round_up(n, m):
    return (n + m - 1) // m * m


def harmonic(first, second):
    return 2.0 * first * second / jnp.maximum(first + second, TINY)


def dot_nt(a, b):
    return lax.dot_general(a, b, (((1,), (1,)), ((), ())), preferred_element_type=F32)


def three_terms(x):
    high = x.astype(BF16).astype(F32)
    rest = x - high
    middle = rest.astype(BF16).astype(F32)
    return high, middle, rest - middle


def expand(basis_ref, column):
    field = basis_ref[0].astype(F32) * column[0:1][None]
    for k in range(1, basis_ref.shape[0]):
        field = field + basis_ref[k].astype(F32) * column[k : k + 1][None]
    return field


def position(axis, count):
    index = lax.axis_index(axis)
    odd = lax.rem(index, 2) == 1
    inner = jnp.logical_and(index > 0, index < count - 1)
    return odd, inner


def edges_kernel(
    counts,
    basis_hbm,
    mobility_hbm,
    accumulation_hbm,
    residual_hbm,
    x1_ref,
    x2_ref,
    y1_ref,
    y2_ref,
    b_ref,
    basis_ref,
    mobility_ref,
    accumulation_ref,
    residual_ref,
    chunk_sems,
    sems,
):
    k_count, cz, cy, cx = basis_ref.shape
    chunks = chunk_sems.shape[0]
    size = k_count // chunks
    residual_copy = pltpu.make_async_copy(residual_hbm, residual_ref, sems.at[0])
    residual_copy.start()
    chunk_copies = []
    for n in range(chunks):
        part = slice(n * size, (n + 1) * size)
        copy = pltpu.make_async_copy(basis_hbm.at[part], basis_ref.at[part], chunk_sems.at[n])
        copy.start()
        chunk_copies.append(copy)
    mobility_copy = pltpu.make_async_copy(mobility_hbm, mobility_ref, sems.at[1])
    mobility_copy.start()
    accumulation_copy = pltpu.make_async_copy(accumulation_hbm, accumulation_ref, sems.at[2])
    accumulation_copy.start()
    cells = cz * cy
    odd_x, inner_x = position("gx", counts[0])
    odd_y, inner_y = position("gy", counts[1])

    first = jnp.where(odd_x, 0, cx - 1)
    second = jnp.where(odd_x, cx - 1, 0)
    pick_row = iota((2 * k_count, cx), 0)
    pick_lane = iota((2 * k_count, cx), 1)
    wanted = pick_lane == jnp.where(pick_row < k_count, first, second)
    pick_k = jnp.where(pick_row < k_count, pick_row, pick_row - k_count)
    picks = [jnp.where(jnp.logical_and(wanted, pick_k == k), 1.0, 0.0).astype(BF16) for k in range(k_count)]
    pick_row = iota((TILE, cx), 0)
    pick_lane = iota((TILE, cx), 1)
    pick = jnp.where(pick_lane == jnp.where(pick_row == 0, first, second), 1.0, 0.0).astype(BF16)
    mobility_copy.wait()
    edge_mobility = dot_nt(pick, mobility_ref[...].reshape(cells, cx))
    residual_copy.wait()
    residual = residual_ref[...]

    row = iota((k_count, cx), 0)
    partial = jnp.zeros((k_count, cx), F32)
    for copy in chunk_copies:
        copy.wait()
    columns = dot_nt(
        jnp.concatenate(picks, axis=1), jnp.concatenate([basis_ref[k].reshape(cells, cx) for k in range(k_count)], axis=1)
    )
    for k in range(k_count):
        product = basis_ref[k].astype(F32) * residual
        total = jnp.sum(jnp.sum(product, axis=0), axis=0, keepdims=True)
        partial = jnp.where(row == k, total, partial)
    b = jnp.broadcast_to(jnp.sum(partial, axis=1, keepdims=True), (k_count, LANES))
    b_ref[...] = b

    for number, ref in ((0, x1_ref), (1, x2_ref)):
        edge = columns[number * k_count : (number + 1) * k_count]
        ref[0:k_count, :] = edge.astype(BF16)
        field = jnp.sum(edge * b[:, :1], axis=0, keepdims=True)
        mobility = edge_mobility[number : number + 1]
        if number == 1:
            mobility = jnp.where(inner_x, mobility, 0.0)
        row = iota((TILE, cells), 0)
        extra = jnp.zeros((TILE, cells), F32)
        for place, value in enumerate((mobility, *three_terms(field))):
            extra = jnp.where(row == place, value, extra)
        ref[k_count : k_count + TILE, :] = extra.astype(BF16)

    row = iota((k_count, cx), 0)
    extra_rows = round_up(4 * cz, TILE)
    extra_row = iota((extra_rows, cx), 0)
    extras = [jnp.zeros((extra_rows, cx), F32) for _ in range(2)]
    for z in range(cz):
        low = jnp.zeros((k_count, cx), F32)
        high = jnp.zeros((k_count, cx), F32)
        for k in range(k_count):
            low = jnp.where(row == k, basis_ref[k, z, 0:TILE, :].astype(F32)[0:1], low)
            high = jnp.where(row == k, basis_ref[k, z, cy - TILE : cy, :].astype(F32)[TILE - 1 : TILE], high)
        low_mobility = mobility_ref[z, 0:TILE, :].astype(F32)[0:1]
        high_mobility = mobility_ref[z, cy - TILE : cy, :].astype(F32)[TILE - 1 : TILE]
        for number, ref in ((0, y1_ref), (1, y2_ref)):
            use_low = odd_y if number == 0 else jnp.logical_not(odd_y)
            edge = jnp.where(use_low, low, high)
            mobility = jnp.where(use_low, low_mobility, high_mobility)
            if number == 1:
                mobility = jnp.where(inner_y, mobility, 0.0)
            ref[z * k_count : (z + 1) * k_count, :] = edge.astype(BF16)
            field = jnp.sum(edge * b[:, :1], axis=0, keepdims=True)
            for place, value in enumerate((mobility, *three_terms(field))):
                extras[number] = jnp.where(extra_row == place * cz + z, value, extras[number])
    for number, ref in ((0, y1_ref), (1, y2_ref)):
        ref[cz * k_count : cz * k_count + extra_rows, :] = extras[number].astype(BF16)
    accumulation_copy.wait()


def image_kernel(basis_ref, mobility_ref, accumulation_ref, b_ref, along_x_ref, along_y_ref, along_z_ref, image_ref):
    k_count, cz, cy, cx = basis_ref.shape
    mobility = mobility_ref[...].astype(F32)
    shape = mobility.shape
    along_x = jnp.where(iota(shape, 2) < cx - 1, harmonic(mobility, pltpu.roll(mobility, cx - 1, 2)), 0.0)
    along_y = jnp.where(iota(shape, 1) < cy - 1, harmonic(mobility, pltpu.roll(mobility, cy - 1, 1)), 0.0)
    along_z = VERTICAL_RATIO * harmonic(mobility[:-1], mobility[1:])
    along_x_ref[...] = along_x
    along_y_ref[...] = along_y
    along_z_ref[...] = along_z
    field = expand(basis_ref, b_ref[...])
    flow_x = along_x * (field - pltpu.roll(field, cx - 1, 2))
    image = accumulation_ref[...] * field + flow_x - pltpu.roll(flow_x, 1, 2)
    flow_y = along_y * (field - pltpu.roll(field, cy - 1, 1))
    image = image + flow_y - pltpu.roll(flow_y, 1, 1)
    flow_z = along_z * (field[:-1] - field[1:])
    nothing = jnp.zeros_like(field[:1])
    image = image + jnp.concatenate([flow_z, nothing], axis=0) - jnp.concatenate([nothing, flow_z], axis=0)
    row = iota((k_count, cx), 0)
    partial = jnp.zeros((k_count, cx), F32)
    for k in range(k_count):
        total = jnp.sum(jnp.sum(basis_ref[k].astype(F32) * image, axis=0), axis=0, keepdims=True)
        partial = jnp.where(row == k, total, partial)
    image_ref[...] = partial


def energy(field, accumulation, along_x, along_y, along_z):
    _, cy, cx = field.shape
    change_x = field - pltpu.roll(field, cx - 1, 2)
    change_y = field - pltpu.roll(field, cy - 1, 1)
    change_z = field[:-1] - field[1:]
    square = accumulation * field * field + along_x * change_x * change_x + along_y * change_y * change_y
    square = jnp.sum(square, axis=0) + jnp.sum(along_z * change_z * change_z, axis=0)
    return jnp.sum(square, axis=0, keepdims=True)


def couple_kernel(
    counts,
    x1_ref,
    x2_ref,
    y1_ref,
    y2_ref,
    rx2_ref,
    ry2_ref,
    ry1_ref,
    rx1_ref,
    b_ref,
    image_ref,
    basis_ref,
    accumulation_ref,
    along_x_ref,
    along_y_ref,
    along_z_ref,
    out_ref,
    v_ref,
):
    k_count, cz, _, _ = basis_ref.shape
    odd_x, _ = position("gx", counts[0])
    odd_y, _ = position("gy", counts[1])
    b_col = b_ref[...]

    def unpack(ref, layers):
        blocks = [ref[z * k_count : (z + 1) * k_count, :].astype(F32) for z in range(layers)]
        start = layers * k_count
        extra = ref[start : start + round_up(4 * layers, TILE), :].astype(F32)
        mobility, high, middle, low = (extra[n * layers : (n + 1) * layers] for n in range(4))
        return blocks, mobility, high + middle + low

    faces = []
    for own_ref, other_ref, layers in (
        (x1_ref, rx1_ref, 1),
        (x2_ref, rx2_ref, 1),
        (y1_ref, ry1_ref, cz),
        (y2_ref, ry2_ref, cz),
    ):
        own, own_mobility, own_field = unpack(own_ref, layers)
        other, other_mobility, other_field = unpack(other_ref, layers)
        faces.append((own, other, harmonic(own_mobility, other_mobility), own_field, other_field))

    own_image = image_ref[...]
    along = own_image
    for own, _, conductance, own_field, other_field in faces:
        flow = conductance * (own_field - other_field)
        for z, block in enumerate(own):
            along = along + block * flow[z : z + 1]
    image = jnp.sum(along, axis=1, keepdims=True)
    source_square = jnp.sum(b_col * b_col, axis=0, keepdims=True)
    source_image = jnp.sum(b_col * image, axis=0, keepdims=True)
    quotient = source_image / jnp.maximum(source_square, TINY)
    v_col = image - quotient * b_col
    v_ref[0:k_count, :] = v_col
    v_ref[k_count : k_count + 8, :] = jnp.broadcast_to(quotient, (8, LANES))

    field = expand(basis_ref, v_col)
    squares = [
        jnp.sum(b_col * own_image, axis=0, keepdims=True),
        jnp.sum(v_col * own_image, axis=0, keepdims=True),
        energy(field, accumulation_ref[...], along_x_ref[...], along_y_ref[...], along_z_ref[...]),
    ]
    toward = []
    for own, other, conductance, own_field, other_field in faces:
        v_field = jnp.concatenate([jnp.sum(block * v_col, axis=0, keepdims=True) for block in own], axis=0)
        flow_b = conductance * own_field
        flow_v = conductance * v_field
        for n, value in enumerate((flow_b * own_field, flow_b * v_field, flow_v * v_field)):
            squares[n] = squares[n] + jnp.sum(value, axis=0, keepdims=True)
        toward.append(
            (
                other,
                flow_v,
                jnp.sum(-flow_b * other_field, axis=0, keepdims=True),
                jnp.sum(-flow_v * other_field, axis=0, keepdims=True),
            )
        )

    columns = [v_col]
    source_pairs = []
    image_pairs = []
    for first, second, odd in ((toward[0], toward[1], odd_x), (toward[2], toward[3], odd_y)):
        product = jnp.zeros((k_count, LANES), F32)
        for z in range(len(first[0])):
            block = jnp.where(odd, second[0][z], first[0][z])
            flow = jnp.where(odd, second[1], first[1])
            product = product - block * flow[z : z + 1]
        columns.append(jnp.sum(product, axis=1, keepdims=True))
        source_pairs.append(jnp.where(odd, second[2], first[2]))
        image_pairs.append(jnp.where(odd, second[3], first[3]))
        image_pairs.append(jnp.where(odd, first[3], second[3]))
    row = iota((TILE, LANES), 0)
    sums = jnp.zeros((TILE, LANES), F32)
    for n, value in enumerate((*squares, *source_pairs, *image_pairs)):
        sums = jnp.where(row == n, value, sums)
    scalars = jnp.broadcast_to(jnp.sum(sums, axis=1, keepdims=True), (TILE, LANES))
    v_square = jnp.sum(v_col * v_col, axis=0, keepdims=True)
    source_v = jnp.sum(v_col * b_col, axis=0, keepdims=True)
    for n, value in enumerate((quotient, source_square, source_image, source_v, v_square)):
        scalars = jnp.where(row == 9 + n, value, scalars)
    packed = jnp.zeros((1, LANES), F32)
    for n, column in enumerate((*columns, scalars)):
        size = column.shape[0]
        place = iota((size, LANES), 1) - iota((size, LANES), 0) == n * k_count
        packed = packed + jnp.sum(jnp.where(place, column, 0.0), axis=0, keepdims=True)
    out_ref[...] = jnp.broadcast_to(packed, out_ref.shape)


def finish_kernel(
    count_y,
    gathered_ref,
    b_ref,
    v_ref,
    basis_ref,
    correction_hbm,
    solution_hbm,
    correction_ref,
    solution_ref,
    sems,
):
    k_count, cz, cy, cx = basis_ref.shape
    base = 3 * k_count
    every = gathered_ref[...]

    def rows(x, amount):
        amount = amount % x.shape[0]
        return jnp.concatenate([x[amount:], x[:amount]], axis=0)

    def column(n):
        return jnp.broadcast_to(every[:, base + n : base + n + 1], every.shape)

    def total(x):
        return jnp.sum(x, axis=0, keepdims=True)

    sums = total(every)
    energy_sum = jnp.broadcast_to(sums[:, base + 10 : base + 11], sums.shape)
    image_sum = jnp.broadcast_to(sums[:, base + 11 : base + 12], sums.shape)
    lane = iota(every.shape, 1)
    vectors = pltpu.roll(every, LANES - k_count, 1) * rows(every, count_y)
    vectors = vectors + pltpu.roll(every, LANES - 2 * k_count, 1) * rows(every, 1)
    v_image_v = jnp.where(lane < k_count, 2.0 * vectors, jnp.where(lane == base + 2, every, 0.0))
    v_image_v = jnp.sum(total(v_image_v), axis=1, keepdims=True)
    quotient = column(9)
    quotient_x = rows(quotient, count_y)
    quotient_y = rows(quotient, 1)
    square_b, b_v, square_v = column(10), column(12), column(13)
    b_image_b, pair_x, pair_y = column(0), 2.0 * column(3), 2.0 * column(4)
    b_image_v = column(1) + rows(column(5), -count_y) + rows(column(6), count_y) + rows(column(7), -1) + rows(column(8), 1)

    step = energy_sum / (image_sum + EPSILON)
    left = 1.0 - step * quotient
    renewed = total(left * (left * square_b - 2.0 * step * b_v) + step * step * square_v)
    ratio = renewed / (energy_sum + EPSILON)
    weight = left + ratio
    weight_x = 1.0 + ratio - step * quotient_x
    weight_y = 1.0 + ratio - step * quotient_y
    curvature = total(weight * (weight * b_image_b + weight_x * pair_x + weight_y * pair_y - 2.0 * step * b_image_v))
    curvature = curvature + step * step * v_image_v
    last_step = renewed / (curvature + EPSILON)

    own_weight = 1.0 + ratio - step * v_ref[k_count : k_count + 1, :]
    solution = (step + last_step * own_weight) * b_ref[...] - last_step * step * v_ref[0:k_count, :]
    place = iota(solution.shape, 0) == iota(solution.shape, 1)
    solution_ref[...] = total(jnp.where(place, solution, 0.0))[:, :k_count]
    copies = [pltpu.make_async_copy(solution_ref, solution_hbm, sems.at[cz])]
    copies[0].start()
    for z in range(cz):
        layer = jnp.zeros((cy, cx), F32)
        for k in range(k_count):
            layer = layer + basis_ref[k, z].astype(F32) * solution[k : k + 1]
        correction_ref[z] = layer
        copy = pltpu.make_async_copy(correction_ref.at[z], correction_hbm.at[z], sems.at[z])
        copy.start()
        copies.append(copy)
    for copy in copies:
        copy.wait()


def exchange(message, axis, counts, second):
    count_x, count_y = counts
    pairs = []
    for x in range(count_x):
        for y in range(count_y):
            i, count = (x, count_x) if axis == "gx" else (y, count_y)
            j = i ^ 1
            if second:
                j = i - 1 if i % 2 == 0 else i + 1
            if 0 <= j < count:
                partner = (j, y) if axis == "gx" else (x, j)
            else:
                partner = (x, y ^ 1) if axis == "gx" else (x ^ 1, y)
            pairs.append((x * count_y + y, partner[0] * count_y + partner[1]))
    return lax.ppermute(message, ("gx", "gy"), pairs)


def per_device(counts, basis, mobility, accumulation, residual):
    k_count, cz, cy, cx = basis.shape
    devices = counts[0] * counts[1]
    x_message = jax.ShapeDtypeStruct((k_count + TILE, cz * cy), BF16)
    y_message = jax.ShapeDtypeStruct((cz * k_count + round_up(4 * cz, TILE), cx), BF16)
    chunks = 1
    inputs = [pltpu.with_memory_space_constraint(x, pltpu.HBM) for x in (basis, mobility, accumulation, residual)]
    x1, x2, y1, y2, b, basis, mobility, accumulation = pl.pallas_call(
        functools.partial(edges_kernel, counts),
        out_shape=(
            x_message,
            x_message,
            y_message,
            y_message,
            jax.ShapeDtypeStruct((k_count, LANES), F32),
            jax.ShapeDtypeStruct(basis.shape, BF16),
            jax.ShapeDtypeStruct(mobility.shape, BF16),
            jax.ShapeDtypeStruct(accumulation.shape, F32),
        ),
        in_specs=[HBM] * 4,
        out_specs=(VMEM,) * 8,
        scratch_shapes=[
            pltpu.VMEM(residual.shape, F32),
            pltpu.SemaphoreType.DMA((chunks,)),
            pltpu.SemaphoreType.DMA((3,)),
        ],
        compiler_params=PARAMS,
    )(*inputs)
    rx1 = exchange(x1, "gx", counts, False)
    rx2 = exchange(x2, "gx", counts, True)
    ry1 = exchange(y1, "gy", counts, False)
    ry2 = exchange(y2, "gy", counts, True)
    conductance = jax.ShapeDtypeStruct((cz, cy, cx), F32)
    layered = jax.ShapeDtypeStruct((cz - 1, cy, cx), F32)
    along_x, along_y, along_z, image = pl.pallas_call(
        image_kernel,
        out_shape=(conductance, conductance, layered, jax.ShapeDtypeStruct((k_count, cx), F32)),
        in_specs=[VMEM] * 4,
        out_specs=(VMEM,) * 4,
        compiler_params=PARAMS,
        cost_estimate=pl.CostEstimate(flops=10**8, bytes_accessed=10**6, transcendentals=0),
    )(basis, mobility, accumulation, b)
    row, v = pl.pallas_call(
        functools.partial(couple_kernel, counts),
        out_shape=(jax.ShapeDtypeStruct((devices, LANES), F32), jax.ShapeDtypeStruct((k_count + 8, LANES), F32)),
        in_specs=[VMEM] * 15,
        out_specs=(VMEM, VMEM),
        compiler_params=PARAMS,
    )(x1, x2, y1, y2, rx2, ry2, ry1, rx1, b, image, basis, accumulation, along_x, along_y, along_z)
    gathered = lax.all_to_all(row, ("gx", "gy"), 0, 0, tiled=True)
    correction, solution = pl.pallas_call(
        functools.partial(finish_kernel, counts[1]),
        out_shape=(jax.ShapeDtypeStruct((cz, cy, cx), F32), jax.ShapeDtypeStruct((1, k_count), F32)),
        in_specs=[VMEM] * 4,
        out_specs=(HBM, HBM),
        scratch_shapes=[
            pltpu.VMEM((cz, cy, cx), F32),
            pltpu.VMEM((1, k_count), F32),
            pltpu.SemaphoreType.DMA((cz + 1,)),
        ],
        compiler_params=PARAMS,
    )(gathered, b, v, basis)
    return correction, solution.reshape(1, 1, k_count)


def solution(mesh):
    counts = (mesh.shape["gx"], mesh.shape["gy"])
    placed = (
        P(None, None, "gy", "gx"),
        P(None, "gy", "gx"),
        P(None, "gy", "gx"),
        P(None, "gy", "gx"),
    )
    return jax.shard_map(
        functools.partial(per_device, counts),
        mesh=mesh,
        in_specs=placed,
        out_specs=(P(None, "gy", "gx"), P("gx", "gy", None)),
        check_vma=False,
    )
```

```python
import functools

import jax
import jax.numpy as jnp
from jax import lax
from jax.experimental import pallas as pl
from jax.experimental.pallas import tpu as pltpu
from jax.sharding import PartitionSpec as P

ITERS = 2
EPSILON = 1e-6
VERTICAL_RATIO = 0.1
TINY = 1e-30
TILE = 16
LANES = 128

F32 = jnp.float32
BF16 = jnp.bfloat16
VMEM = pl.BlockSpec(memory_space=pltpu.VMEM)
HBM = pl.BlockSpec(memory_space=pltpu.HBM)
PARAMS = pltpu.CompilerParams(vmem_limit_bytes=8 * 2**20)


def iota(shape, dim):
    return lax.broadcasted_iota(jnp.int32, shape, dim)


def round_up(n, m):
    return (n + m - 1) // m * m


def harmonic(first, second):
    return 2.0 * first * second / jnp.maximum(first + second, TINY)


def dot_nt(a, b):
    return lax.dot_general(a, b, (((1,), (1,)), ((), ())), preferred_element_type=F32)


def three_terms(x):
    high = x.astype(BF16).astype(F32)
    rest = x - high
    middle = rest.astype(BF16).astype(F32)
    return high, middle, rest - middle


def expand(basis_ref, column):
    field = basis_ref[0].astype(F32) * column[0:1][None]
    for k in range(1, basis_ref.shape[0]):
        field = field + basis_ref[k].astype(F32) * column[k : k + 1][None]
    return field


def position(axis, count):
    index = lax.axis_index(axis)
    odd = lax.rem(index, 2) == 1
    inner = jnp.logical_and(index > 0, index < count - 1)
    return odd, inner


def edges_kernel(
    counts,
    basis_hbm,
    mobility_hbm,
    accumulation_hbm,
    residual_hbm,
    x1_ref,
    x2_ref,
    y1_ref,
    y2_ref,
    b_ref,
    basis_ref,
    mobility_ref,
    accumulation_ref,
    residual_ref,
    sems,
):
    k_count, cz, cy, cx = basis_ref.shape
    mobility_copy = pltpu.make_async_copy(mobility_hbm, mobility_ref, sems.at[1])
    mobility_copy.start()
    residual_copy = pltpu.make_async_copy(residual_hbm, residual_ref, sems.at[0])
    residual_copy.start()
    basis_copy = pltpu.make_async_copy(basis_hbm, basis_ref, sems.at[3])
    basis_copy.start()
    accumulation_copy = pltpu.make_async_copy(accumulation_hbm, accumulation_ref, sems.at[2])
    accumulation_copy.start()
    cells = cz * cy
    odd_x, inner_x = position("gx", counts[0])
    odd_y, inner_y = position("gy", counts[1])

    first = jnp.where(odd_x, 0, cx - 1)
    second = jnp.where(odd_x, cx - 1, 0)
    pick_row = iota((2 * k_count, cx), 0)
    pick_lane = iota((2 * k_count, cx), 1)
    wanted = pick_lane == jnp.where(pick_row < k_count, first, second)
    pick_k = jnp.where(pick_row < k_count, pick_row, pick_row - k_count)
    picks = [jnp.where(jnp.logical_and(wanted, pick_k == k), 1.0, 0.0).astype(BF16) for k in range(k_count)]
    pick_row = iota((TILE, cx), 0)
    pick_lane = iota((TILE, cx), 1)
    pick = jnp.where(pick_lane == jnp.where(pick_row == 0, first, second), 1.0, 0.0).astype(BF16)
    mobility_copy.wait()
    edge_mobility = dot_nt(pick, mobility_ref[...].reshape(cells, cx))
    residual_copy.wait()
    residual = residual_ref[...]

    row = iota((k_count, cx), 0)
    partial = jnp.zeros((k_count, cx), F32)
    basis_copy.wait()
    columns = dot_nt(
        jnp.concatenate(picks, axis=1), jnp.concatenate([basis_ref[k].reshape(cells, cx) for k in range(k_count)], axis=1)
    )
    for k in range(k_count):
        product = basis_ref[k].astype(F32) * residual
        total = jnp.sum(jnp.sum(product, axis=0), axis=0, keepdims=True)
        partial = jnp.where(row == k, total, partial)
    b = jnp.broadcast_to(jnp.sum(partial, axis=1, keepdims=True), (k_count, LANES))
    b_ref[...] = b

    for number, ref in ((0, x1_ref), (1, x2_ref)):
        edge = columns[number * k_count : (number + 1) * k_count]
        ref[0:k_count, :] = edge.astype(BF16)
        field = jnp.sum(edge * b[:, :1], axis=0, keepdims=True)
        mobility = edge_mobility[number : number + 1]
        if number == 1:
            mobility = jnp.where(inner_x, mobility, 0.0)
        row = iota((TILE, cells), 0)
        extra = jnp.zeros((TILE, cells), F32)
        for place, value in enumerate((mobility, *three_terms(field))):
            extra = jnp.where(row == place, value, extra)
        ref[k_count : k_count + TILE, :] = extra.astype(BF16)

    row = iota((k_count, cx), 0)
    extra_rows = round_up(4 * cz, TILE)
    extra_row = iota((extra_rows, cx), 0)
    extras = [jnp.zeros((extra_rows, cx), F32) for _ in range(2)]
    for z in range(cz):
        low = jnp.zeros((k_count, cx), F32)
        high = jnp.zeros((k_count, cx), F32)
        for k in range(k_count):
            low = jnp.where(row == k, basis_ref[k, z, 0:TILE, :].astype(F32)[0:1], low)
            high = jnp.where(row == k, basis_ref[k, z, cy - TILE : cy, :].astype(F32)[TILE - 1 : TILE], high)
        low_mobility = mobility_ref[z, 0:TILE, :].astype(F32)[0:1]
        high_mobility = mobility_ref[z, cy - TILE : cy, :].astype(F32)[TILE - 1 : TILE]
        for number, ref in ((0, y1_ref), (1, y2_ref)):
            use_low = odd_y if number == 0 else jnp.logical_not(odd_y)
            edge = jnp.where(use_low, low, high)
            mobility = jnp.where(use_low, low_mobility, high_mobility)
            if number == 1:
                mobility = jnp.where(inner_y, mobility, 0.0)
            ref[z * k_count : (z + 1) * k_count, :] = edge.astype(BF16)
            field = jnp.sum(edge * b[:, :1], axis=0, keepdims=True)
            for place, value in enumerate((mobility, *three_terms(field))):
                extras[number] = jnp.where(extra_row == place * cz + z, value, extras[number])
    for number, ref in ((0, y1_ref), (1, y2_ref)):
        ref[cz * k_count : cz * k_count + extra_rows, :] = extras[number].astype(BF16)
    accumulation_copy.wait()


def image_kernel(
    basis_ref, mobility_ref, accumulation_ref, b_ref, along_x_ref, along_y_ref, along_z_ref, image_ref, field_ref
):
    k_count, cz, cy, cx = basis_ref.shape
    mobility = mobility_ref[...].astype(F32)
    shape = mobility.shape
    along_x = jnp.where(iota(shape, 2) < cx - 1, harmonic(mobility, pltpu.roll(mobility, cx - 1, 2)), 0.0)
    along_y = jnp.where(iota(shape, 1) < cy - 1, harmonic(mobility, pltpu.roll(mobility, cy - 1, 1)), 0.0)
    along_z = VERTICAL_RATIO * harmonic(mobility[:-1], mobility[1:])
    along_x_ref[...] = along_x
    along_y_ref[...] = along_y
    along_z_ref[...] = along_z
    field = expand(basis_ref, b_ref[...])
    field_ref[...] = field
    flow_x = along_x * (field - pltpu.roll(field, cx - 1, 2))
    image = accumulation_ref[...] * field + flow_x - pltpu.roll(flow_x, 1, 2)
    flow_y = along_y * (field - pltpu.roll(field, cy - 1, 1))
    image = image + flow_y - pltpu.roll(flow_y, 1, 1)
    flow_z = along_z * (field[:-1] - field[1:])
    nothing = jnp.zeros_like(field[:1])
    image = image + jnp.concatenate([flow_z, nothing], axis=0) - jnp.concatenate([nothing, flow_z], axis=0)
    row = iota((k_count, cx), 0)
    partial = jnp.zeros((k_count, cx), F32)
    for k in range(k_count):
        total = jnp.sum(jnp.sum(basis_ref[k].astype(F32) * image, axis=0), axis=0, keepdims=True)
        partial = jnp.where(row == k, total, partial)
    image_ref[...] = partial


def energy(field, accumulation, along_x, along_y, along_z):
    _, cy, cx = field.shape
    change_x = field - pltpu.roll(field, cx - 1, 2)
    change_y = field - pltpu.roll(field, cy - 1, 1)
    change_z = field[:-1] - field[1:]
    square = accumulation * field * field + along_x * change_x * change_x + along_y * change_y * change_y
    square = jnp.sum(square, axis=0) + jnp.sum(along_z * change_z * change_z, axis=0)
    return jnp.sum(square, axis=0, keepdims=True)


def couple_kernel(
    counts,
    y2_ref,
    y1_ref,
    x2_ref,
    x1_ref,
    rx2_ref,
    ry2_ref,
    ry1_ref,
    rx1_ref,
    b_ref,
    image_ref,
    basis_ref,
    accumulation_ref,
    along_x_ref,
    along_y_ref,
    along_z_ref,
    out_ref,
    v_ref,
    field_ref,
):
    k_count, cz, _, _ = basis_ref.shape
    odd_x, _ = position("gx", counts[0])
    odd_y, _ = position("gy", counts[1])
    b_col = b_ref[...]

    def unpack(ref, layers):
        blocks = [ref[z * k_count : (z + 1) * k_count, :].astype(F32) for z in range(layers)]
        start = layers * k_count
        extra = ref[start : start + round_up(4 * layers, TILE), :].astype(F32)
        mobility, high, middle, low = (extra[n * layers : (n + 1) * layers] for n in range(4))
        return blocks, mobility, high + middle + low

    faces = []
    for own_ref, other_ref, layers in (
        (x1_ref, rx1_ref, 1),
        (x2_ref, rx2_ref, 1),
        (y1_ref, ry1_ref, cz),
        (y2_ref, ry2_ref, cz),
    ):
        own, own_mobility, own_field = unpack(own_ref, layers)
        other, other_mobility, other_field = unpack(other_ref, layers)
        faces.append((own, other, harmonic(own_mobility, other_mobility), own_field, other_field))

    own_image = image_ref[...]
    along = own_image
    for own, _, conductance, own_field, other_field in faces:
        flow = conductance * (own_field - other_field)
        for z, block in enumerate(own):
            along = along + block * flow[z : z + 1]
    image = jnp.sum(along, axis=1, keepdims=True)
    source_square = jnp.sum(b_col * b_col, axis=0, keepdims=True)
    source_image = jnp.sum(b_col * image, axis=0, keepdims=True)
    quotient = source_image / jnp.maximum(source_square, TINY)
    v_col = image - quotient * b_col
    v_ref[0:k_count, :] = v_col
    v_ref[k_count : k_count + 8, :] = jnp.broadcast_to(quotient, (8, LANES))

    field = expand(basis_ref, v_col)
    field_ref[...] = field
    squares = [
        jnp.sum(b_col * own_image, axis=0, keepdims=True),
        jnp.sum(v_col * own_image, axis=0, keepdims=True),
        energy(field, accumulation_ref[...], along_x_ref[...], along_y_ref[...], along_z_ref[...]),
    ]
    toward = []
    for own, other, conductance, own_field, other_field in faces:
        v_field = jnp.concatenate([jnp.sum(block * v_col, axis=0, keepdims=True) for block in own], axis=0)
        flow_b = conductance * own_field
        flow_v = conductance * v_field
        for n, value in enumerate((flow_b * own_field, flow_b * v_field, flow_v * v_field)):
            squares[n] = squares[n] + jnp.sum(value, axis=0, keepdims=True)
        toward.append(
            (
                other,
                flow_v,
                jnp.sum(-flow_b * other_field, axis=0, keepdims=True),
                jnp.sum(-flow_v * other_field, axis=0, keepdims=True),
            )
        )

    columns = [v_col]
    source_pairs = []
    image_pairs = []
    for first, second, odd in ((toward[0], toward[1], odd_x), (toward[2], toward[3], odd_y)):
        product = jnp.zeros((k_count, LANES), F32)
        for z in range(len(first[0])):
            block = jnp.where(odd, second[0][z], first[0][z])
            flow = jnp.where(odd, second[1], first[1])
            product = product - block * flow[z : z + 1]
        columns.append(jnp.sum(product, axis=1, keepdims=True))
        source_pairs.append(jnp.where(odd, second[2], first[2]))
        image_pairs.append(jnp.where(odd, second[3], first[3]))
        image_pairs.append(jnp.where(odd, first[3], second[3]))
    row = iota((TILE, LANES), 0)
    sums = jnp.zeros((TILE, LANES), F32)
    for n, value in enumerate((*squares, *source_pairs, *image_pairs)):
        sums = jnp.where(row == n, value, sums)
    scalars = jnp.broadcast_to(jnp.sum(sums, axis=1, keepdims=True), (TILE, LANES))
    v_square = jnp.sum(v_col * v_col, axis=0, keepdims=True)
    source_v = jnp.sum(v_col * b_col, axis=0, keepdims=True)
    for n, value in enumerate((quotient, source_square, source_image, source_v, v_square)):
        scalars = jnp.where(row == 9 + n, value, scalars)
    packed = jnp.zeros((1, LANES), F32)
    for n, column in enumerate((*columns, scalars)):
        size = column.shape[0]
        place = iota((size, LANES), 1) - iota((size, LANES), 0) == n * k_count
        packed = packed + jnp.sum(jnp.where(place, column, 0.0), axis=0, keepdims=True)
    out_ref[...] = jnp.broadcast_to(packed, out_ref.shape)


def finish_kernel(
    count_y,
    gathered_ref,
    b_ref,
    v_ref,
    b_field_ref,
    v_field_ref,
    correction_hbm,
    solution_hbm,
    correction_ref,
    solution_ref,
    sems,
):
    k_count = b_ref.shape[0]
    cz = correction_ref.shape[0]
    base = 3 * k_count
    every = gathered_ref[...]

    def rows(x, amount):
        amount = amount % x.shape[0]
        return jnp.concatenate([x[amount:], x[:amount]], axis=0)

    def column(n):
        return jnp.broadcast_to(every[:, base + n : base + n + 1], every.shape)

    def total(x):
        return jnp.sum(x, axis=0, keepdims=True)

    sums = total(every)
    energy_sum = jnp.broadcast_to(sums[:, base + 10 : base + 11], sums.shape)
    image_sum = jnp.broadcast_to(sums[:, base + 11 : base + 12], sums.shape)
    lane = iota(every.shape, 1)
    vectors = pltpu.roll(every, LANES - k_count, 1) * rows(every, count_y)
    vectors = vectors + pltpu.roll(every, LANES - 2 * k_count, 1) * rows(every, 1)
    v_image_v = jnp.where(lane < k_count, 2.0 * vectors, jnp.where(lane == base + 2, every, 0.0))
    v_image_v = jnp.sum(total(v_image_v), axis=1, keepdims=True)
    quotient = column(9)
    quotient_x = rows(quotient, count_y)
    quotient_y = rows(quotient, 1)
    square_b, b_v, square_v = column(10), column(12), column(13)
    b_image_b, pair_x, pair_y = column(0), 2.0 * column(3), 2.0 * column(4)
    b_image_v = column(1) + rows(column(5), -count_y) + rows(column(6), count_y) + rows(column(7), -1) + rows(column(8), 1)

    step = energy_sum / (image_sum + EPSILON)
    left = 1.0 - step * quotient
    renewed = total(left * (left * square_b - 2.0 * step * b_v) + step * step * square_v)
    ratio = renewed / (energy_sum + EPSILON)
    weight = left + ratio
    weight_x = 1.0 + ratio - step * quotient_x
    weight_y = 1.0 + ratio - step * quotient_y
    curvature = total(weight * (weight * b_image_b + weight_x * pair_x + weight_y * pair_y - 2.0 * step * b_image_v))
    curvature = curvature + step * step * v_image_v
    last_step = renewed / (curvature + EPSILON)

    own_weight = 1.0 + ratio - step * v_ref[k_count : k_count + 1, :]
    b_part = step + last_step * own_weight
    v_part = -last_step * step
    solution = b_part * b_ref[...] + v_part * v_ref[0:k_count, :]
    place = iota(solution.shape, 0) == iota(solution.shape, 1)
    solution_ref[...] = total(jnp.where(place, solution, 0.0))[:, :k_count]
    copies = [pltpu.make_async_copy(solution_ref, solution_hbm, sems.at[cz])]
    copies[0].start()
    for z in range(cz):
        correction_ref[z] = b_part * b_field_ref[z] + v_part * v_field_ref[z]
        copy = pltpu.make_async_copy(correction_ref.at[z], correction_hbm.at[z], sems.at[z])
        copy.start()
        copies.append(copy)
    for copy in copies:
        copy.wait()


def exchange(message, axis, counts, second):
    count_x, count_y = counts
    pairs = []
    for x in range(count_x):
        for y in range(count_y):
            i, count = (x, count_x) if axis == "gx" else (y, count_y)
            j = i ^ 1
            if second:
                j = i - 1 if i % 2 == 0 else i + 1
            if 0 <= j < count:
                partner = (j, y) if axis == "gx" else (x, j)
            else:
                partner = (x, y ^ 1) if axis == "gx" else (x ^ 1, y)
            pairs.append((x * count_y + y, partner[0] * count_y + partner[1]))
    return lax.ppermute(message, ("gx", "gy"), pairs)


def per_device(counts, basis, mobility, accumulation, residual):
    k_count, cz, cy, cx = basis.shape
    devices = counts[0] * counts[1]
    x_message = jax.ShapeDtypeStruct((k_count + TILE, cz * cy), BF16)
    y_message = jax.ShapeDtypeStruct((cz * k_count + round_up(4 * cz, TILE), cx), BF16)
    inputs = [pltpu.with_memory_space_constraint(x, pltpu.HBM) for x in (basis, mobility, accumulation, residual)]
    x1, x2, y1, y2, b, basis, mobility, accumulation = pl.pallas_call(
        functools.partial(edges_kernel, counts),
        out_shape=(
            x_message,
            x_message,
            y_message,
            y_message,
            jax.ShapeDtypeStruct((k_count, LANES), F32),
            jax.ShapeDtypeStruct(basis.shape, BF16),
            jax.ShapeDtypeStruct(mobility.shape, BF16),
            jax.ShapeDtypeStruct(accumulation.shape, F32),
        ),
        in_specs=[HBM] * 4,
        out_specs=(VMEM,) * 8,
        scratch_shapes=[
            pltpu.VMEM(residual.shape, F32),
            pltpu.SemaphoreType.DMA((4,)),
        ],
        compiler_params=PARAMS,
    )(*inputs)
    rx1 = exchange(x1, "gx", counts, False)
    rx2 = exchange(x2, "gx", counts, True)
    ry1 = exchange(y1, "gy", counts, False)
    ry2 = exchange(y2, "gy", counts, True)
    conductance = jax.ShapeDtypeStruct((cz, cy, cx), F32)
    layered = jax.ShapeDtypeStruct((cz - 1, cy, cx), F32)
    along_x, along_y, along_z, image, b_field = pl.pallas_call(
        image_kernel,
        out_shape=(conductance, conductance, layered, jax.ShapeDtypeStruct((k_count, cx), F32), conductance),
        in_specs=[VMEM] * 4,
        out_specs=(VMEM,) * 5,
        compiler_params=PARAMS,
        cost_estimate=pl.CostEstimate(flops=10**8, bytes_accessed=10**6, transcendentals=0),
    )(basis, mobility, accumulation, b)
    row, v, v_field = pl.pallas_call(
        functools.partial(couple_kernel, counts),
        out_shape=(
            jax.ShapeDtypeStruct((devices, LANES), F32),
            jax.ShapeDtypeStruct((k_count + 8, LANES), F32),
            conductance,
        ),
        in_specs=[VMEM] * 15,
        out_specs=(VMEM,) * 3,
        compiler_params=PARAMS,
    )(y2, y1, x2, x1, rx2, ry2, ry1, rx1, b, image, basis, accumulation, along_x, along_y, along_z)
    gathered = lax.all_to_all(row, ("gx", "gy"), 0, 0, tiled=True)
    correction, solution = pl.pallas_call(
        functools.partial(finish_kernel, counts[1]),
        out_shape=(jax.ShapeDtypeStruct((cz, cy, cx), F32), jax.ShapeDtypeStruct((1, k_count), F32)),
        in_specs=[VMEM] * 5,
        out_specs=(HBM, HBM),
        scratch_shapes=[
            pltpu.VMEM((cz, cy, cx), F32),
            pltpu.VMEM((1, k_count), F32),
            pltpu.SemaphoreType.DMA((cz + 1,)),
        ],
        compiler_params=PARAMS,
    )(gathered, b, v, b_field, v_field)
    return correction, solution.reshape(1, 1, k_count)


def solution(mesh):
    counts = (mesh.shape["gx"], mesh.shape["gy"])
    placed = (
        P(None, None, "gy", "gx"),
        P(None, "gy", "gx"),
        P(None, "gy", "gx"),
        P(None, "gy", "gx"),
    )
    return jax.shard_map(
        functools.partial(per_device, counts),
        mesh=mesh,
        in_specs=placed,
        out_specs=(P(None, "gy", "gx"), P("gx", "gy", None)),
        check_vma=False,
    )
```

```python
import functools

import jax
import jax.numpy as jnp
from jax import lax
from jax.experimental import pallas as pl
from jax.experimental.pallas import tpu as pltpu
from jax.sharding import PartitionSpec as P

ITERS = 2
EPSILON = 1e-6
VERTICAL_RATIO = 0.1
TINY = 1e-30
TILE = 16
LANES = 128

F32 = jnp.float32
BF16 = jnp.bfloat16
VMEM = pl.BlockSpec(memory_space=pltpu.VMEM)
HBM = pl.BlockSpec(memory_space=pltpu.HBM)
PARAMS = pltpu.CompilerParams(vmem_limit_bytes=8 * 2**20)


def iota(shape, dim):
    return lax.broadcasted_iota(jnp.int32, shape, dim)


def round_up(n, m):
    return (n + m - 1) // m * m


def harmonic(first, second):
    return 2.0 * first * second / jnp.maximum(first + second, TINY)


def dot_nt(a, b):
    return lax.dot_general(a, b, (((1,), (1,)), ((), ())), preferred_element_type=F32)


def three_terms(x):
    high = x.astype(BF16).astype(F32)
    rest = x - high
    middle = rest.astype(BF16).astype(F32)
    return high, middle, rest - middle


def expand(basis_ref, column):
    field = basis_ref[0].astype(F32) * column[0:1][None]
    for k in range(1, basis_ref.shape[0]):
        field = field + basis_ref[k].astype(F32) * column[k : k + 1][None]
    return field


def position(axis, count):
    index = lax.axis_index(axis)
    odd = lax.rem(index, 2) == 1
    inner = jnp.logical_and(index > 0, index < count - 1)
    return odd, inner


def edges_kernel(
    counts,
    basis_hbm,
    mobility_hbm,
    accumulation_hbm,
    residual_hbm,
    x1_ref,
    x2_ref,
    y1_ref,
    y2_ref,
    b_ref,
    basis_ref,
    mobility_ref,
    accumulation_ref,
    residual_ref,
    sems,
):
    k_count, cz, cy, cx = basis_ref.shape
    mobility_copy = pltpu.make_async_copy(mobility_hbm, mobility_ref, sems.at[1])
    mobility_copy.start()
    residual_copy = pltpu.make_async_copy(residual_hbm, residual_ref, sems.at[0])
    residual_copy.start()
    basis_copy = pltpu.make_async_copy(basis_hbm, basis_ref, sems.at[3])
    basis_copy.start()
    accumulation_copy = pltpu.make_async_copy(accumulation_hbm, accumulation_ref, sems.at[2])
    accumulation_copy.start()
    cells = cz * cy
    odd_x, inner_x = position("gx", counts[0])
    odd_y, inner_y = position("gy", counts[1])

    first = jnp.where(odd_x, 0, cx - 1)
    second = jnp.where(odd_x, cx - 1, 0)
    pick_row = iota((2 * k_count, cx), 0)
    pick_lane = iota((2 * k_count, cx), 1)
    wanted = pick_lane == jnp.where(pick_row < k_count, first, second)
    pick_k = jnp.where(pick_row < k_count, pick_row, pick_row - k_count)
    picks = [jnp.where(jnp.logical_and(wanted, pick_k == k), 1.0, 0.0).astype(BF16) for k in range(k_count)]
    pick_row = iota((TILE, cx), 0)
    pick_lane = iota((TILE, cx), 1)
    pick = jnp.where(pick_lane == jnp.where(pick_row == 0, first, second), 1.0, 0.0).astype(BF16)
    mobility_copy.wait()
    edge_mobility = dot_nt(pick, mobility_ref[...].reshape(cells, cx))
    residual_copy.wait()
    residual = residual_ref[...]

    row = iota((k_count, cx), 0)
    partial = jnp.zeros((k_count, cx), F32)
    basis_copy.wait()
    columns = dot_nt(
        jnp.concatenate(picks, axis=1), jnp.concatenate([basis_ref[k].reshape(cells, cx) for k in range(k_count)], axis=1)
    )
    for k in range(k_count):
        product = basis_ref[k].astype(F32) * residual
        total = jnp.sum(jnp.sum(product, axis=0), axis=0, keepdims=True)
        partial = jnp.where(row == k, total, partial)
    b = jnp.broadcast_to(jnp.sum(partial, axis=1, keepdims=True), (k_count, LANES))
    b_ref[...] = b

    for number, ref in ((0, x1_ref), (1, x2_ref)):
        edge = columns[number * k_count : (number + 1) * k_count]
        ref[0:k_count, :] = edge.astype(BF16)
        field = jnp.sum(edge * b[:, :1], axis=0, keepdims=True)
        mobility = edge_mobility[number : number + 1]
        if number == 1:
            mobility = jnp.where(inner_x, mobility, 0.0)
        row = iota((TILE, cells), 0)
        extra = jnp.zeros((TILE, cells), F32)
        for place, value in enumerate((mobility, *three_terms(field))):
            extra = jnp.where(row == place, value, extra)
        ref[k_count : k_count + TILE, :] = extra.astype(BF16)

    row = iota((k_count, cx), 0)
    extra_rows = round_up(4 * cz, TILE)
    extra_row = iota((extra_rows, cx), 0)
    extras = [jnp.zeros((extra_rows, cx), F32) for _ in range(2)]
    for z in range(cz):
        low = jnp.zeros((k_count, cx), F32)
        high = jnp.zeros((k_count, cx), F32)
        for k in range(k_count):
            low = jnp.where(row == k, basis_ref[k, z, 0:TILE, :].astype(F32)[0:1], low)
            high = jnp.where(row == k, basis_ref[k, z, cy - TILE : cy, :].astype(F32)[TILE - 1 : TILE], high)
        low_mobility = mobility_ref[z, 0:TILE, :].astype(F32)[0:1]
        high_mobility = mobility_ref[z, cy - TILE : cy, :].astype(F32)[TILE - 1 : TILE]
        for number, ref in ((0, y1_ref), (1, y2_ref)):
            use_low = odd_y if number == 0 else jnp.logical_not(odd_y)
            edge = jnp.where(use_low, low, high)
            mobility = jnp.where(use_low, low_mobility, high_mobility)
            if number == 1:
                mobility = jnp.where(inner_y, mobility, 0.0)
            ref[z * k_count : (z + 1) * k_count, :] = edge.astype(BF16)
            field = jnp.sum(edge * b[:, :1], axis=0, keepdims=True)
            for place, value in enumerate((mobility, *three_terms(field))):
                extras[number] = jnp.where(extra_row == place * cz + z, value, extras[number])
    for number, ref in ((0, y1_ref), (1, y2_ref)):
        ref[cz * k_count : cz * k_count + extra_rows, :] = extras[number].astype(BF16)
    accumulation_copy.wait()


def gram_kernel(basis_ref, mobility_ref, accumulation_ref, b_ref, gram_ref, field_ref, left_ref):
    k_count, cz, cy, cx = basis_ref.shape
    mobility = mobility_ref[...].astype(F32)
    accumulation = accumulation_ref[...]
    shape = mobility.shape
    along_x = jnp.where(iota(shape, 2) < cx - 1, harmonic(mobility, pltpu.roll(mobility, cx - 1, 2)), 0.0)
    along_y = jnp.where(iota(shape, 1) < cy - 1, harmonic(mobility, pltpu.roll(mobility, cy - 1, 1)), 0.0)
    along_z = VERTICAL_RATIO * harmonic(mobility[:-1], mobility[1:])
    rows = k_count * TILE
    strips = [(z, y) for z in range(cz) for y in range(0, cy, TILE)]
    for k in range(k_count):
        field = basis_ref[k].astype(F32)
        flow_x = along_x * (field - pltpu.roll(field, cx - 1, 2))
        image = accumulation * field + flow_x - pltpu.roll(flow_x, 1, 2)
        flow_y = along_y * (field - pltpu.roll(field, cy - 1, 1))
        image = image + flow_y - pltpu.roll(flow_y, 1, 1)
        flow_z = along_z * (field[:-1] - field[1:])
        nothing = jnp.zeros_like(field[:1])
        image = image + jnp.concatenate([flow_z, nothing], axis=0) - jnp.concatenate([nothing, flow_z], axis=0)
        high = image.astype(BF16)
        low = (image - high.astype(F32)).astype(BF16)
        for place, (z, y) in enumerate(strips):
            lanes = slice(place * cx, (place + 1) * cx)
            left_ref[k * TILE : (k + 1) * TILE, lanes] = high[z, y : y + TILE]
            left_ref[rows + k * TILE : rows + (k + 1) * TILE, lanes] = low[z, y : y + TILE]
    total = jnp.zeros((2 * rows, rows), F32)
    for place, (z, y) in enumerate(strips):
        right = basis_ref[:, z, y : y + TILE, :].reshape(rows, cx)
        total = total + dot_nt(left_ref[:, place * cx : (place + 1) * cx], right)
    total = total[:rows] + total[rows:]
    same = lax.rem(iota((rows, rows), 0), TILE) == lax.rem(iota((rows, rows), 1), TILE)
    total = jnp.where(same, total, 0.0)
    gram_ref[...] = jnp.sum(total.reshape(k_count, TILE, rows), axis=1)
    field_ref[...] = expand(basis_ref, b_ref[...])


def unpack(ref, k_count, layers):
    blocks = [ref[z * k_count : (z + 1) * k_count, :].astype(F32) for z in range(layers)]
    start = layers * k_count
    extra = ref[start : start + round_up(4 * layers, TILE), :].astype(F32)
    mobility, high, middle, low = (extra[n * layers : (n + 1) * layers] for n in range(4))
    return blocks, mobility, high + middle + low


def as_row(column, width):
    k_count = column.shape[0]
    shape = (k_count, max(k_count * width, LANES))
    place = iota(shape, 1) // width == iota(shape, 0)
    return jnp.sum(jnp.where(place, column[:, :1], 0.0), axis=0, keepdims=True)


def fold_lanes(x):
    return sum(x[:, start : start + LANES] for start in range(0, x.shape[1], LANES))


def rows_kernel(counts, y2_ref, y1_ref, ry2_ref, ry1_ref, b_ref, gram_ref, own_ref, pull_ref, edge_ref, cross_ref):
    k_count = b_ref.shape[0]
    cz = (y1_ref.shape[0] - TILE) // k_count
    odd_y, _ = position("gy", counts[1])
    own_image = fold_lanes(gram_ref[...] * as_row(b_ref[...], TILE))
    weighted, plain, others = [], [], []
    for n, (own_ref_, other_ref) in enumerate(((y1_ref, ry1_ref), (y2_ref, ry2_ref))):
        own, own_mobility, own_field = unpack(own_ref_, k_count, cz)
        other, other_mobility, other_field = unpack(other_ref, k_count, cz)
        conductance = harmonic(own_mobility, other_mobility)
        heavy = [block * conductance[z : z + 1] for z, block in enumerate(own)]
        pull = jnp.zeros((k_count, LANES), F32)
        for z, block in enumerate(heavy):
            own_image = own_image + block * own_field[z : z + 1]
            pull = pull + block * other_field[z : z + 1]
        pull_ref[n * k_count : (n + 1) * k_count, :] = pull
        weighted.append(jnp.concatenate(heavy, axis=1))
        plain.append(jnp.concatenate(own, axis=1))
        others.append(jnp.concatenate(other, axis=1))
    own_ref[...] = own_image

    def product(left, right):
        right = jnp.concatenate([right, jnp.zeros((LANES - k_count, right.shape[1]), F32)], axis=0)
        high = right.astype(BF16)
        low = (right - high.astype(F32)).astype(BF16)
        left = left.astype(BF16)
        return dot_nt(left, high) + dot_nt(left, low)

    edge_ref[...] = product(jnp.concatenate(plain, axis=1), jnp.concatenate(weighted, axis=1))
    cross_ref[...] = product(jnp.where(odd_y, others[1], others[0]), jnp.where(odd_y, weighted[1], weighted[0]))


def couple_kernel(
    counts,
    x2_ref,
    x1_ref,
    rx2_ref,
    rx1_ref,
    b_ref,
    gram_ref,
    own_ref,
    pull_ref,
    edge_ref,
    cross_ref,
    out_ref,
    v_ref,
):
    k_count = b_ref.shape[0]
    odd_x, _ = position("gx", counts[0])
    odd_y, _ = position("gy", counts[1])
    b_col = b_ref[...]
    pulls = [pull_ref[0:k_count, :], pull_ref[k_count : 2 * k_count, :]]
    faces = []
    own_image = own_ref[...]
    along = -pulls[0] - pulls[1]
    for own_ref_, other_ref in ((x1_ref, rx1_ref), (x2_ref, rx2_ref)):
        (own,), own_mobility, own_field = unpack(own_ref_, k_count, 1)
        (other,), other_mobility, other_field = unpack(other_ref, k_count, 1)
        conductance = harmonic(own_mobility, other_mobility)
        own_image = own_image + own * (conductance * own_field)
        pull = own * (conductance * other_field)
        along = along - pull
        pulls.append(pull)
        faces.append((own, other, conductance))
    image = jnp.sum(along + own_image, axis=1, keepdims=True)
    source_square = jnp.sum(b_col * b_col, axis=0, keepdims=True)
    source_image = jnp.sum(b_col * image, axis=0, keepdims=True)
    quotient = source_image / jnp.maximum(source_square, TINY)
    v_col = image - quotient * b_col
    v_ref[0:k_count, :] = v_col
    v_ref[k_count : k_count + 8, :] = jnp.broadcast_to(quotient, (8, LANES))

    v_row = as_row(v_col, 1)
    v_image = fold_lanes(gram_ref[...] * as_row(v_col, TILE)) + edge_ref[...] * v_row
    squares = [
        jnp.sum(b_col * own_image, axis=0, keepdims=True),
        jnp.sum(v_col * own_image, axis=0, keepdims=True),
        jnp.sum(v_col * v_image, axis=0, keepdims=True),
    ]
    flows = []
    for own, _, conductance in faces:
        v_field = jnp.sum(own * v_col, axis=0, keepdims=True)
        flows.append(conductance * v_field)
        squares[2] = squares[2] + flows[-1] * v_field
    beside = -jnp.where(odd_x, faces[1][1], faces[0][1]) * jnp.where(odd_x, flows[1], flows[0])
    columns = [v_col]
    for product in (beside, -cross_ref[...] * v_row):
        columns.append(jnp.sum(product, axis=1, keepdims=True))
    source_pairs = []
    image_pairs = []
    for first, second, odd in ((pulls[2], pulls[3], odd_x), (pulls[0], pulls[1], odd_y)):
        right, left = jnp.where(odd, second, first), jnp.where(odd, first, second)
        source_pairs.append(-jnp.sum(b_col * right, axis=0, keepdims=True))
        image_pairs.append(-jnp.sum(v_col * right, axis=0, keepdims=True))
        image_pairs.append(-jnp.sum(v_col * left, axis=0, keepdims=True))
    row = iota((TILE, LANES), 0)
    sums = jnp.zeros((TILE, LANES), F32)
    for n, value in enumerate((*squares, *source_pairs, *image_pairs)):
        sums = jnp.where(row == n, value, sums)
    scalars = jnp.broadcast_to(jnp.sum(sums, axis=1, keepdims=True), (TILE, LANES))
    v_square = jnp.sum(v_col * v_col, axis=0, keepdims=True)
    source_v = jnp.sum(v_col * b_col, axis=0, keepdims=True)
    for n, value in enumerate((quotient, source_square, source_image, source_v, v_square)):
        scalars = jnp.where(row == 9 + n, value, scalars)
    packed = jnp.zeros((1, LANES), F32)
    for n, column in enumerate((*columns, scalars)):
        size = column.shape[0]
        place = iota((size, LANES), 1) - iota((size, LANES), 0) == n * k_count
        packed = packed + jnp.sum(jnp.where(place, column, 0.0), axis=0, keepdims=True)
    out_ref[...] = jnp.broadcast_to(packed, out_ref.shape)


def finish_kernel(
    count_y,
    gathered_ref,
    b_ref,
    v_ref,
    b_field_ref,
    basis_ref,
    correction_hbm,
    solution_hbm,
    correction_ref,
    solution_ref,
    sems,
):
    k_count = b_ref.shape[0]
    cz = correction_ref.shape[0]
    base = 3 * k_count
    every = gathered_ref[...]
    v_field = expand(basis_ref, v_ref[0:k_count, :])

    def rows(x, amount):
        amount = amount % x.shape[0]
        return jnp.concatenate([x[amount:], x[:amount]], axis=0)

    def column(n):
        return jnp.broadcast_to(every[:, base + n : base + n + 1], every.shape)

    def total(x):
        return jnp.sum(x, axis=0, keepdims=True)

    sums = total(every)
    energy_sum = jnp.broadcast_to(sums[:, base + 10 : base + 11], sums.shape)
    image_sum = jnp.broadcast_to(sums[:, base + 11 : base + 12], sums.shape)
    lane = iota(every.shape, 1)
    vectors = pltpu.roll(every, LANES - k_count, 1) * rows(every, count_y)
    vectors = vectors + pltpu.roll(every, LANES - 2 * k_count, 1) * rows(every, 1)
    v_image_v = jnp.where(lane < k_count, 2.0 * vectors, jnp.where(lane == base + 2, every, 0.0))
    v_image_v = jnp.sum(total(v_image_v), axis=1, keepdims=True)
    quotient = column(9)
    quotient_x = rows(quotient, count_y)
    quotient_y = rows(quotient, 1)
    square_b, b_v, square_v = column(10), column(12), column(13)
    b_image_b, pair_x, pair_y = column(0), 2.0 * column(3), 2.0 * column(4)
    b_image_v = column(1) + rows(column(5), -count_y) + rows(column(6), count_y) + rows(column(7), -1) + rows(column(8), 1)

    step = energy_sum / (image_sum + EPSILON)
    left = 1.0 - step * quotient
    renewed = total(left * (left * square_b - 2.0 * step * b_v) + step * step * square_v)
    ratio = renewed / (energy_sum + EPSILON)
    weight = left + ratio
    weight_x = 1.0 + ratio - step * quotient_x
    weight_y = 1.0 + ratio - step * quotient_y
    curvature = total(weight * (weight * b_image_b + weight_x * pair_x + weight_y * pair_y - 2.0 * step * b_image_v))
    curvature = curvature + step * step * v_image_v
    last_step = renewed / (curvature + EPSILON)

    own_weight = 1.0 + ratio - step * v_ref[k_count : k_count + 1, :]
    b_part = step + last_step * own_weight
    v_part = -last_step * step
    solution = b_part * b_ref[...] + v_part * v_ref[0:k_count, :]
    place = iota(solution.shape, 0) == iota(solution.shape, 1)
    solution_ref[...] = total(jnp.where(place, solution, 0.0))[:, :k_count]
    copies = [pltpu.make_async_copy(solution_ref, solution_hbm, sems.at[cz])]
    copies[0].start()
    for z in range(cz):
        correction_ref[z] = b_part * b_field_ref[z] + v_part * v_field[z]
        copy = pltpu.make_async_copy(correction_ref.at[z], correction_hbm.at[z], sems.at[z])
        copy.start()
        copies.append(copy)
    for copy in copies:
        copy.wait()


def exchange(message, axis, counts, second):
    count_x, count_y = counts
    pairs = []
    for x in range(count_x):
        for y in range(count_y):
            i, count = (x, count_x) if axis == "gx" else (y, count_y)
            j = i ^ 1
            if second:
                j = i - 1 if i % 2 == 0 else i + 1
            if 0 <= j < count:
                partner = (j, y) if axis == "gx" else (x, j)
            else:
                partner = (x, y ^ 1) if axis == "gx" else (x ^ 1, y)
            pairs.append((x * count_y + y, partner[0] * count_y + partner[1]))
    return lax.ppermute(message, ("gx", "gy"), pairs)


def per_device(counts, basis, mobility, accumulation, residual):
    k_count, cz, cy, cx = basis.shape
    devices = counts[0] * counts[1]
    x_message = jax.ShapeDtypeStruct((k_count + TILE, cz * cy), BF16)
    y_message = jax.ShapeDtypeStruct((cz * k_count + round_up(4 * cz, TILE), cx), BF16)
    inputs = [pltpu.with_memory_space_constraint(x, pltpu.HBM) for x in (basis, mobility, accumulation, residual)]
    x1, x2, y1, y2, b, basis, mobility, accumulation = pl.pallas_call(
        functools.partial(edges_kernel, counts),
        out_shape=(
            x_message,
            x_message,
            y_message,
            y_message,
            jax.ShapeDtypeStruct((k_count, LANES), F32),
            jax.ShapeDtypeStruct(basis.shape, BF16),
            jax.ShapeDtypeStruct(mobility.shape, BF16),
            jax.ShapeDtypeStruct(accumulation.shape, F32),
        ),
        in_specs=[HBM] * 4,
        out_specs=(VMEM,) * 8,
        scratch_shapes=[
            pltpu.VMEM(residual.shape, F32),
            pltpu.SemaphoreType.DMA((4,)),
        ],
        compiler_params=PARAMS,
    )(*inputs)
    rx1 = exchange(x1, "gx", counts, False)
    rx2 = exchange(x2, "gx", counts, True)
    ry1 = exchange(y1, "gy", counts, False)
    ry2 = exchange(y2, "gy", counts, True)
    conductance = jax.ShapeDtypeStruct((cz, cy, cx), F32)
    gram, b_field = pl.pallas_call(
        gram_kernel,
        out_shape=(jax.ShapeDtypeStruct((k_count, k_count * TILE), F32), conductance),
        in_specs=[VMEM] * 4,
        out_specs=(VMEM,) * 2,
        compiler_params=PARAMS,
        scratch_shapes=[pltpu.VMEM((2 * k_count * TILE, cz * cy // TILE * cx), BF16)],
        cost_estimate=pl.CostEstimate(flops=10**8, bytes_accessed=10**6, transcendentals=0),
    )(basis, mobility, accumulation, b)
    square = jax.ShapeDtypeStruct((k_count, LANES), F32)
    own, pull, edge, cross = pl.pallas_call(
        functools.partial(rows_kernel, counts),
        out_shape=(square, jax.ShapeDtypeStruct((2 * k_count, LANES), F32), square, square),
        in_specs=[VMEM] * 6,
        out_specs=(VMEM,) * 4,
        compiler_params=PARAMS,
        cost_estimate=pl.CostEstimate(flops=10**7, bytes_accessed=10**6, transcendentals=0),
    )(y2, y1, ry2, ry1, b, gram)
    row, v = pl.pallas_call(
        functools.partial(couple_kernel, counts),
        out_shape=(
            jax.ShapeDtypeStruct((devices, LANES), F32),
            jax.ShapeDtypeStruct((k_count + 8, LANES), F32),
        ),
        in_specs=[VMEM] * 10,
        out_specs=(VMEM,) * 2,
        compiler_params=PARAMS,
    )(x2, x1, rx2, rx1, b, gram, own, pull, edge, cross)
    gathered = lax.all_to_all(row, ("gx", "gy"), 0, 0, tiled=True)
    correction, solution = pl.pallas_call(
        functools.partial(finish_kernel, counts[1]),
        out_shape=(jax.ShapeDtypeStruct((cz, cy, cx), F32), jax.ShapeDtypeStruct((1, k_count), F32)),
        in_specs=[VMEM] * 5,
        out_specs=(HBM, HBM),
        scratch_shapes=[
            pltpu.VMEM((cz, cy, cx), F32),
            pltpu.VMEM((1, k_count), F32),
            pltpu.SemaphoreType.DMA((cz + 1,)),
        ],
        compiler_params=PARAMS,
    )(gathered, b, v, b_field, basis)
    return correction, solution.reshape(1, 1, k_count)


def solution(mesh):
    counts = (mesh.shape["gx"], mesh.shape["gy"])
    placed = (
        P(None, None, "gy", "gx"),
        P(None, "gy", "gx"),
        P(None, "gy", "gx"),
        P(None, "gy", "gx"),
    )
    return jax.shard_map(
        functools.partial(per_device, counts),
        mesh=mesh,
        in_specs=placed,
        out_specs=(P(None, "gy", "gx"), P("gx", "gy", None)),
        check_vma=False,
    )
```

```python
import functools

import jax
import jax.numpy as jnp
from jax import lax
from jax.experimental import pallas as pl
from jax.experimental.pallas import tpu as pltpu
from jax.sharding import PartitionSpec as P

ITERS = 2
EPSILON = 1e-6
VERTICAL_RATIO = 0.1
TINY = 1e-30
TILE = 16
LANES = 128

F32 = jnp.float32
BF16 = jnp.bfloat16
VMEM = pl.BlockSpec(memory_space=pltpu.VMEM)
HBM = pl.BlockSpec(memory_space=pltpu.HBM)
PARAMS = pltpu.CompilerParams(vmem_limit_bytes=8 * 2**20)


def iota(shape, dim):
    return lax.broadcasted_iota(jnp.int32, shape, dim)


def round_up(n, m):
    return (n + m - 1) // m * m


def harmonic(first, second):
    return 2.0 * first * second / jnp.maximum(first + second, TINY)


def dot_nt(a, b):
    return lax.dot_general(a, b, (((1,), (1,)), ((), ())), preferred_element_type=F32)


def three_terms(x):
    high = x.astype(BF16).astype(F32)
    rest = x - high
    middle = rest.astype(BF16).astype(F32)
    return high, middle, rest - middle


def expand(basis_ref, column):
    field = basis_ref[0].astype(F32) * column[0:1][None]
    for k in range(1, basis_ref.shape[0]):
        field = field + basis_ref[k].astype(F32) * column[k : k + 1][None]
    return field


def position(axis, count):
    index = lax.axis_index(axis)
    odd = lax.rem(index, 2) == 1
    inner = jnp.logical_and(index > 0, index < count - 1)
    return odd, inner


def edges_kernel(
    counts,
    basis_hbm,
    mobility_hbm,
    accumulation_hbm,
    residual_hbm,
    x1_ref,
    x2_ref,
    y1_ref,
    y2_ref,
    b_ref,
    basis_ref,
    mobility_ref,
    accumulation_ref,
    residual_ref,
    sems,
):
    k_count, cz, cy, cx = basis_ref.shape
    mobility_copy = pltpu.make_async_copy(mobility_hbm, mobility_ref, sems.at[1])
    mobility_copy.start()
    residual_copy = pltpu.make_async_copy(residual_hbm, residual_ref, sems.at[0])
    residual_copy.start()
    basis_copy = pltpu.make_async_copy(basis_hbm, basis_ref, sems.at[3])
    basis_copy.start()
    accumulation_copy = pltpu.make_async_copy(accumulation_hbm, accumulation_ref, sems.at[2])
    accumulation_copy.start()
    cells = cz * cy
    odd_x, inner_x = position("gx", counts[0])
    odd_y, inner_y = position("gy", counts[1])

    first = jnp.where(odd_x, 0, cx - 1)
    second = jnp.where(odd_x, cx - 1, 0)
    pick_row = iota((TILE, cx), 0)
    pick_lane = iota((TILE, cx), 1)
    pick = jnp.where(pick_lane == jnp.where(pick_row == 0, first, second), 1.0, 0.0).astype(BF16)
    mobility_copy.wait()
    edge_mobility = dot_nt(pick, mobility_ref[...].reshape(cells, cx))
    residual_copy.wait()
    residual = residual_ref[...]

    row = iota((k_count, cx), 0)
    partial = jnp.zeros((k_count, cx), F32)
    basis_copy.wait()
    flat = dot_nt(pick, basis_ref[...].reshape(k_count * cells, cx))
    columns = [jnp.zeros((k_count, cells), F32) for _ in range(2)]
    for k in range(k_count):
        for number in range(2):
            value = flat[number : number + 1, k * cells : (k + 1) * cells]
            columns[number] = jnp.where(row == k, value, columns[number])
    for k in range(k_count):
        product = basis_ref[k].astype(F32) * residual
        total = jnp.sum(jnp.sum(product, axis=0), axis=0, keepdims=True)
        partial = jnp.where(row == k, total, partial)
    b = jnp.broadcast_to(jnp.sum(partial, axis=1, keepdims=True), (k_count, LANES))
    b_ref[...] = b

    for number, ref in ((0, x1_ref), (1, x2_ref)):
        edge = columns[number]
        ref[0:k_count, :] = edge.astype(BF16)
        field = jnp.sum(edge * b[:, :1], axis=0, keepdims=True)
        mobility = edge_mobility[number : number + 1]
        if number == 1:
            mobility = jnp.where(inner_x, mobility, 0.0)
        row = iota((TILE, cells), 0)
        extra = jnp.zeros((TILE, cells), F32)
        for place, value in enumerate((mobility, *three_terms(field))):
            extra = jnp.where(row == place, value, extra)
        ref[k_count : k_count + TILE, :] = extra.astype(BF16)

    row = iota((k_count, cx), 0)
    extra_rows = round_up(4 * cz, TILE)
    extra_row = iota((extra_rows, cx), 0)
    extras = [jnp.zeros((extra_rows, cx), F32) for _ in range(2)]
    for z in range(cz):
        low = jnp.zeros((k_count, cx), F32)
        high = jnp.zeros((k_count, cx), F32)
        for k in range(k_count):
            low = jnp.where(row == k, basis_ref[k, z, 0:TILE, :].astype(F32)[0:1], low)
            high = jnp.where(row == k, basis_ref[k, z, cy - TILE : cy, :].astype(F32)[TILE - 1 : TILE], high)
        low_mobility = mobility_ref[z, 0:TILE, :].astype(F32)[0:1]
        high_mobility = mobility_ref[z, cy - TILE : cy, :].astype(F32)[TILE - 1 : TILE]
        for number, ref in ((0, y1_ref), (1, y2_ref)):
            use_low = odd_y if number == 0 else jnp.logical_not(odd_y)
            edge = jnp.where(use_low, low, high)
            mobility = jnp.where(use_low, low_mobility, high_mobility)
            if number == 1:
                mobility = jnp.where(inner_y, mobility, 0.0)
            ref[z * k_count : (z + 1) * k_count, :] = edge.astype(BF16)
            field = jnp.sum(edge * b[:, :1], axis=0, keepdims=True)
            for place, value in enumerate((mobility, *three_terms(field))):
                extras[number] = jnp.where(extra_row == place * cz + z, value, extras[number])
    for number, ref in ((0, y1_ref), (1, y2_ref)):
        ref[cz * k_count : cz * k_count + extra_rows, :] = extras[number].astype(BF16)
    accumulation_copy.wait()


def gram_kernel(basis_ref, mobility_ref, accumulation_ref, b_ref, gram_ref, field_ref, left_ref):
    k_count, cz, cy, cx = basis_ref.shape
    mobility = mobility_ref[...].astype(F32)
    accumulation = accumulation_ref[...]
    shape = mobility.shape
    along_x = jnp.where(iota(shape, 2) < cx - 1, harmonic(mobility, pltpu.roll(mobility, cx - 1, 2)), 0.0)
    along_y = jnp.where(iota(shape, 1) < cy - 1, harmonic(mobility, pltpu.roll(mobility, cy - 1, 1)), 0.0)
    along_z = VERTICAL_RATIO * harmonic(mobility[:-1], mobility[1:])
    rows = k_count * TILE
    strips = [(z, y) for z in range(cz) for y in range(0, cy, TILE)]
    for k in range(k_count):
        field = basis_ref[k].astype(F32)
        flow_x = along_x * (field - pltpu.roll(field, cx - 1, 2))
        image = accumulation * field + flow_x - pltpu.roll(flow_x, 1, 2)
        flow_y = along_y * (field - pltpu.roll(field, cy - 1, 1))
        image = image + flow_y - pltpu.roll(flow_y, 1, 1)
        flow_z = along_z * (field[:-1] - field[1:])
        nothing = jnp.zeros_like(field[:1])
        image = image + jnp.concatenate([flow_z, nothing], axis=0) - jnp.concatenate([nothing, flow_z], axis=0)
        high = image.astype(BF16)
        low = (image - high.astype(F32)).astype(BF16)
        for place, (z, y) in enumerate(strips):
            lanes = slice(place * cx, (place + 1) * cx)
            left_ref[k * TILE : (k + 1) * TILE, lanes] = high[z, y : y + TILE]
            left_ref[rows + k * TILE : rows + (k + 1) * TILE, lanes] = low[z, y : y + TILE]
    total = jnp.zeros((2 * rows, rows), F32)
    for place, (z, y) in enumerate(strips):
        right = basis_ref[:, z, y : y + TILE, :].reshape(rows, cx)
        total = total + dot_nt(left_ref[:, place * cx : (place + 1) * cx], right)
    total = total[:rows] + total[rows:]
    same = lax.rem(iota((rows, rows), 0), TILE) == lax.rem(iota((rows, rows), 1), TILE)
    total = jnp.where(same, total, 0.0)
    gram_ref[...] = jnp.sum(total.reshape(k_count, TILE, rows), axis=1)
    field_ref[...] = expand(basis_ref, b_ref[...])


def couple_kernel(
    counts,
    y2_ref,
    y1_ref,
    x2_ref,
    x1_ref,
    rx2_ref,
    ry2_ref,
    ry1_ref,
    rx1_ref,
    b_ref,
    gram_ref,
    out_ref,
    v_ref,
):
    k_count = b_ref.shape[0]
    cz = (y1_ref.shape[0] - TILE) // k_count
    odd_x, _ = position("gx", counts[0])
    odd_y, _ = position("gy", counts[1])
    b_col = b_ref[...]

    def unpack(ref, layers):
        blocks = [ref[z * k_count : (z + 1) * k_count, :].astype(F32) for z in range(layers)]
        start = layers * k_count
        extra = ref[start : start + round_up(4 * layers, TILE), :].astype(F32)
        mobility, high, middle, low = (extra[n * layers : (n + 1) * layers] for n in range(4))
        return blocks, mobility, high + middle + low

    faces = []
    for own_ref, other_ref, layers in (
        (x1_ref, rx1_ref, 1),
        (x2_ref, rx2_ref, 1),
        (y1_ref, ry1_ref, cz),
        (y2_ref, ry2_ref, cz),
    ):
        own, own_mobility, own_field = unpack(own_ref, layers)
        other, other_mobility, other_field = unpack(other_ref, layers)
        faces.append((own, other, harmonic(own_mobility, other_mobility), own_field, other_field))

    gram = gram_ref[...]
    wide = gram.shape[1]
    spread = iota((k_count, wide), 1) // TILE == iota((k_count, wide), 0)

    def as_row(column):
        return jnp.sum(jnp.where(spread, column[:, :1], 0.0), axis=0, keepdims=True)

    def fold(x):
        return sum(x[:, start : start + LANES] for start in range(0, wide, LANES))

    own_image = fold(gram * as_row(b_col))
    along = own_image
    for own, _, conductance, own_field, other_field in faces:
        flow = conductance * (own_field - other_field)
        for z, block in enumerate(own):
            along = along + block * flow[z : z + 1]
    image = jnp.sum(along, axis=1, keepdims=True)
    source_square = jnp.sum(b_col * b_col, axis=0, keepdims=True)
    source_image = jnp.sum(b_col * image, axis=0, keepdims=True)
    quotient = source_image / jnp.maximum(source_square, TINY)
    v_col = image - quotient * b_col
    v_ref[0:k_count, :] = v_col
    v_ref[k_count : k_count + 8, :] = jnp.broadcast_to(quotient, (8, LANES))

    squares = [
        jnp.sum(b_col * own_image, axis=0, keepdims=True),
        jnp.sum(v_col * own_image, axis=0, keepdims=True),
        jnp.sum(v_col * fold(gram * as_row(v_col)), axis=0, keepdims=True),
    ]
    toward = []
    for own, other, conductance, own_field, other_field in faces:
        v_field = jnp.concatenate([jnp.sum(block * v_col, axis=0, keepdims=True) for block in own], axis=0)
        flow_b = conductance * own_field
        flow_v = conductance * v_field
        for n, value in enumerate((flow_b * own_field, flow_b * v_field, flow_v * v_field)):
            squares[n] = squares[n] + jnp.sum(value, axis=0, keepdims=True)
        toward.append(
            (
                other,
                flow_v,
                jnp.sum(-flow_b * other_field, axis=0, keepdims=True),
                jnp.sum(-flow_v * other_field, axis=0, keepdims=True),
            )
        )

    columns = [v_col]
    source_pairs = []
    image_pairs = []
    for first, second, odd in ((toward[0], toward[1], odd_x), (toward[2], toward[3], odd_y)):
        product = jnp.zeros((k_count, LANES), F32)
        for z in range(len(first[0])):
            block = jnp.where(odd, second[0][z], first[0][z])
            flow = jnp.where(odd, second[1], first[1])
            product = product - block * flow[z : z + 1]
        columns.append(jnp.sum(product, axis=1, keepdims=True))
        source_pairs.append(jnp.where(odd, second[2], first[2]))
        image_pairs.append(jnp.where(odd, second[3], first[3]))
        image_pairs.append(jnp.where(odd, first[3], second[3]))
    row = iota((TILE, LANES), 0)
    sums = jnp.zeros((TILE, LANES), F32)
    for n, value in enumerate((*squares, *source_pairs, *image_pairs)):
        sums = jnp.where(row == n, value, sums)
    scalars = jnp.broadcast_to(jnp.sum(sums, axis=1, keepdims=True), (TILE, LANES))
    v_square = jnp.sum(v_col * v_col, axis=0, keepdims=True)
    source_v = jnp.sum(v_col * b_col, axis=0, keepdims=True)
    for n, value in enumerate((quotient, source_square, source_image, source_v, v_square)):
        scalars = jnp.where(row == 9 + n, value, scalars)
    packed = jnp.zeros((1, LANES), F32)
    for n, column in enumerate((*columns, scalars)):
        size = column.shape[0]
        place = iota((size, LANES), 1) - iota((size, LANES), 0) == n * k_count
        packed = packed + jnp.sum(jnp.where(place, column, 0.0), axis=0, keepdims=True)
    out_ref[...] = jnp.broadcast_to(packed, out_ref.shape)


def finish_kernel(
    count_y,
    gathered_ref,
    b_ref,
    v_ref,
    b_field_ref,
    basis_ref,
    correction_hbm,
    solution_hbm,
    correction_ref,
    solution_ref,
    sems,
):
    k_count = b_ref.shape[0]
    cz = correction_ref.shape[0]
    base = 3 * k_count
    every = gathered_ref[...]
    v_field = expand(basis_ref, v_ref[0:k_count, :])

    def rows(x, amount):
        amount = amount % x.shape[0]
        return jnp.concatenate([x[amount:], x[:amount]], axis=0)

    def column(n):
        return jnp.broadcast_to(every[:, base + n : base + n + 1], every.shape)

    def total(x):
        return jnp.sum(x, axis=0, keepdims=True)

    sums = total(every)
    energy_sum = jnp.broadcast_to(sums[:, base + 10 : base + 11], sums.shape)
    image_sum = jnp.broadcast_to(sums[:, base + 11 : base + 12], sums.shape)
    lane = iota(every.shape, 1)
    vectors = pltpu.roll(every, LANES - k_count, 1) * rows(every, count_y)
    vectors = vectors + pltpu.roll(every, LANES - 2 * k_count, 1) * rows(every, 1)
    v_image_v = jnp.where(lane < k_count, 2.0 * vectors, jnp.where(lane == base + 2, every, 0.0))
    v_image_v = jnp.sum(total(v_image_v), axis=1, keepdims=True)
    quotient = column(9)
    quotient_x = rows(quotient, count_y)
    quotient_y = rows(quotient, 1)
    square_b, b_v, square_v = column(10), column(12), column(13)
    b_image_b, pair_x, pair_y = column(0), 2.0 * column(3), 2.0 * column(4)
    b_image_v = column(1) + rows(column(5), -count_y) + rows(column(6), count_y) + rows(column(7), -1) + rows(column(8), 1)

    step = energy_sum / (image_sum + EPSILON)
    left = 1.0 - step * quotient
    renewed = total(left * (left * square_b - 2.0 * step * b_v) + step * step * square_v)
    ratio = renewed / (energy_sum + EPSILON)
    weight = left + ratio
    weight_x = 1.0 + ratio - step * quotient_x
    weight_y = 1.0 + ratio - step * quotient_y
    curvature = total(weight * (weight * b_image_b + weight_x * pair_x + weight_y * pair_y - 2.0 * step * b_image_v))
    curvature = curvature + step * step * v_image_v
    last_step = renewed / (curvature + EPSILON)

    own_weight = 1.0 + ratio - step * v_ref[k_count : k_count + 1, :]
    b_part = step + last_step * own_weight
    v_part = -last_step * step
    solution = b_part * b_ref[...] + v_part * v_ref[0:k_count, :]
    place = iota(solution.shape, 0) == iota(solution.shape, 1)
    solution_ref[...] = total(jnp.where(place, solution, 0.0))[:, :k_count]
    copies = [pltpu.make_async_copy(solution_ref, solution_hbm, sems.at[cz])]
    copies[0].start()
    for z in range(cz):
        correction_ref[z] = b_part * b_field_ref[z] + v_part * v_field[z]
        copy = pltpu.make_async_copy(correction_ref.at[z], correction_hbm.at[z], sems.at[z])
        copy.start()
        copies.append(copy)
    for copy in copies:
        copy.wait()


def exchange(message, axis, counts, second):
    count_x, count_y = counts
    pairs = []
    for x in range(count_x):
        for y in range(count_y):
            i, count = (x, count_x) if axis == "gx" else (y, count_y)
            j = i ^ 1
            if second:
                j = i - 1 if i % 2 == 0 else i + 1
            if 0 <= j < count:
                partner = (j, y) if axis == "gx" else (x, j)
            else:
                partner = (x, y ^ 1) if axis == "gx" else (x ^ 1, y)
            pairs.append((x * count_y + y, partner[0] * count_y + partner[1]))
    return lax.ppermute(message, ("gx", "gy"), pairs)


def per_device(counts, basis, mobility, accumulation, residual):
    k_count, cz, cy, cx = basis.shape
    devices = counts[0] * counts[1]
    x_message = jax.ShapeDtypeStruct((k_count + TILE, cz * cy), BF16)
    y_message = jax.ShapeDtypeStruct((cz * k_count + round_up(4 * cz, TILE), cx), BF16)
    inputs = [pltpu.with_memory_space_constraint(x, pltpu.HBM) for x in (basis, mobility, accumulation, residual)]
    x1, x2, y1, y2, b, basis, mobility, accumulation = pl.pallas_call(
        functools.partial(edges_kernel, counts),
        out_shape=(
            x_message,
            x_message,
            y_message,
            y_message,
            jax.ShapeDtypeStruct((k_count, LANES), F32),
            jax.ShapeDtypeStruct(basis.shape, BF16),
            jax.ShapeDtypeStruct(mobility.shape, BF16),
            jax.ShapeDtypeStruct(accumulation.shape, F32),
        ),
        in_specs=[HBM] * 4,
        out_specs=(VMEM,) * 8,
        scratch_shapes=[
            pltpu.VMEM(residual.shape, F32),
            pltpu.SemaphoreType.DMA((4,)),
        ],
        compiler_params=PARAMS,
    )(*inputs)
    rx1 = exchange(x1, "gx", counts, False)
    rx2 = exchange(x2, "gx", counts, True)
    ry1 = exchange(y1, "gy", counts, False)
    ry2 = exchange(y2, "gy", counts, True)
    conductance = jax.ShapeDtypeStruct((cz, cy, cx), F32)
    gram, b_field = pl.pallas_call(
        gram_kernel,
        out_shape=(jax.ShapeDtypeStruct((k_count, k_count * TILE), F32), conductance),
        in_specs=[VMEM] * 4,
        out_specs=(VMEM,) * 2,
        compiler_params=PARAMS,
        scratch_shapes=[pltpu.VMEM((2 * k_count * TILE, cz * cy // TILE * cx), BF16)],
        cost_estimate=pl.CostEstimate(flops=10**8, bytes_accessed=10**6, transcendentals=0),
    )(basis, mobility, accumulation, b)
    row, v = pl.pallas_call(
        functools.partial(couple_kernel, counts),
        out_shape=(
            jax.ShapeDtypeStruct((devices, LANES), F32),
            jax.ShapeDtypeStruct((k_count + 8, LANES), F32),
        ),
        in_specs=[VMEM] * 10,
        out_specs=(VMEM,) * 2,
        compiler_params=PARAMS,
    )(y2, y1, x2, x1, rx2, ry2, ry1, rx1, b, gram)
    gathered = lax.all_to_all(row, ("gx", "gy"), 0, 0, tiled=True)
    correction, solution = pl.pallas_call(
        functools.partial(finish_kernel, counts[1]),
        out_shape=(jax.ShapeDtypeStruct((cz, cy, cx), F32), jax.ShapeDtypeStruct((1, k_count), F32)),
        in_specs=[VMEM] * 5,
        out_specs=(HBM, HBM),
        scratch_shapes=[
            pltpu.VMEM((cz, cy, cx), F32),
            pltpu.VMEM((1, k_count), F32),
            pltpu.SemaphoreType.DMA((cz + 1,)),
        ],
        compiler_params=PARAMS,
    )(gathered, b, v, b_field, basis)
    return correction, solution.reshape(1, 1, k_count)


def solution(mesh):
    counts = (mesh.shape["gx"], mesh.shape["gy"])
    placed = (
        P(None, None, "gy", "gx"),
        P(None, "gy", "gx"),
        P(None, "gy", "gx"),
        P(None, "gy", "gx"),
    )
    return jax.shard_map(
        functools.partial(per_device, counts),
        mesh=mesh,
        in_specs=placed,
        out_specs=(P(None, "gy", "gx"), P("gx", "gy", None)),
        check_vma=False,
    )
```

```python
import functools

import jax
import jax.numpy as jnp
from jax import lax
from jax.experimental import pallas as pl
from jax.experimental.pallas import tpu as pltpu
from jax.sharding import PartitionSpec as P

ITERS = 2
EPSILON = 1e-6
VERTICAL_RATIO = 0.1
TINY = 1e-30
TILE = 16
LANES = 128

F32 = jnp.float32
BF16 = jnp.bfloat16
VMEM = pl.BlockSpec(memory_space=pltpu.VMEM)
HBM = pl.BlockSpec(memory_space=pltpu.HBM)
PARAMS = pltpu.CompilerParams(vmem_limit_bytes=8 * 2**20)


def iota(shape, dim):
    return lax.broadcasted_iota(jnp.int32, shape, dim)


def round_up(n, m):
    return (n + m - 1) // m * m


def harmonic(first, second):
    return 2.0 * first * second / jnp.maximum(first + second, TINY)


def dot_nt(a, b):
    return lax.dot_general(a, b, (((1,), (1,)), ((), ())), preferred_element_type=F32)


def three_terms(x):
    high = x.astype(BF16).astype(F32)
    rest = x - high
    middle = rest.astype(BF16).astype(F32)
    return high, middle, rest - middle


def expand(basis_ref, column):
    field = basis_ref[0].astype(F32) * column[0:1][None]
    for k in range(1, basis_ref.shape[0]):
        field = field + basis_ref[k].astype(F32) * column[k : k + 1][None]
    return field


def position(axis, count):
    index = lax.axis_index(axis)
    odd = lax.rem(index, 2) == 1
    inner = jnp.logical_and(index > 0, index < count - 1)
    return odd, inner


def edges_kernel(
    counts,
    basis_hbm,
    mobility_hbm,
    accumulation_hbm,
    residual_hbm,
    x1_ref,
    x2_ref,
    y1_ref,
    y2_ref,
    b_ref,
    basis_ref,
    mobility_ref,
    accumulation_ref,
    residual_ref,
    sems,
):
    k_count, cz, cy, cx = basis_ref.shape
    mobility_copy = pltpu.make_async_copy(mobility_hbm, mobility_ref, sems.at[1])
    mobility_copy.start()
    residual_copy = pltpu.make_async_copy(residual_hbm, residual_ref, sems.at[0])
    residual_copy.start()
    basis_copy = pltpu.make_async_copy(basis_hbm, basis_ref, sems.at[3])
    basis_copy.start()
    accumulation_copy = pltpu.make_async_copy(accumulation_hbm, accumulation_ref, sems.at[2])
    accumulation_copy.start()
    cells = cz * cy
    odd_x, inner_x = position("gx", counts[0])
    odd_y, inner_y = position("gy", counts[1])

    first = jnp.where(odd_x, 0, cx - 1)
    second = jnp.where(odd_x, cx - 1, 0)
    pick_row = iota((TILE, cx), 0)
    pick_lane = iota((TILE, cx), 1)
    pick = jnp.where(pick_lane == jnp.where(pick_row == 0, first, second), 1.0, 0.0).astype(BF16)
    mobility_copy.wait()
    edge_mobility = dot_nt(pick, mobility_ref[...].reshape(cells, cx))
    residual_copy.wait()
    residual = residual_ref[...]

    row = iota((k_count, cx), 0)
    partial = jnp.zeros((k_count, cx), F32)
    basis_copy.wait()
    flat = dot_nt(pick, basis_ref[...].reshape(k_count * cells, cx))
    columns = [jnp.zeros((k_count, cells), F32) for _ in range(2)]
    for k in range(k_count):
        for number in range(2):
            value = flat[number : number + 1, k * cells : (k + 1) * cells]
            columns[number] = jnp.where(row == k, value, columns[number])
    for k in range(k_count):
        product = basis_ref[k].astype(F32) * residual
        total = jnp.sum(jnp.sum(product, axis=0), axis=0, keepdims=True)
        partial = jnp.where(row == k, total, partial)
    b = jnp.broadcast_to(jnp.sum(partial, axis=1, keepdims=True), (k_count, LANES))
    b_ref[...] = b

    for number, ref in ((0, x1_ref), (1, x2_ref)):
        edge = columns[number]
        ref[0:k_count, :] = edge.astype(BF16)
        field = jnp.sum(edge * b[:, :1], axis=0, keepdims=True)
        mobility = edge_mobility[number : number + 1]
        if number == 1:
            mobility = jnp.where(inner_x, mobility, 0.0)
        row = iota((TILE, cells), 0)
        extra = jnp.zeros((TILE, cells), F32)
        for place, value in enumerate((mobility, *three_terms(field))):
            extra = jnp.where(row == place, value, extra)
        ref[k_count : k_count + TILE, :] = extra.astype(BF16)

    row = iota((k_count, cx), 0)
    extra_rows = round_up(4 * cz, TILE)
    extra_row = iota((extra_rows, cx), 0)
    extras = [jnp.zeros((extra_rows, cx), F32) for _ in range(2)]
    for z in range(cz):
        low = jnp.zeros((k_count, cx), F32)
        high = jnp.zeros((k_count, cx), F32)
        for k in range(k_count):
            low = jnp.where(row == k, basis_ref[k, z, 0:TILE, :].astype(F32)[0:1], low)
            high = jnp.where(row == k, basis_ref[k, z, cy - TILE : cy, :].astype(F32)[TILE - 1 : TILE], high)
        low_mobility = mobility_ref[z, 0:TILE, :].astype(F32)[0:1]
        high_mobility = mobility_ref[z, cy - TILE : cy, :].astype(F32)[TILE - 1 : TILE]
        for number, ref in ((0, y1_ref), (1, y2_ref)):
            use_low = odd_y if number == 0 else jnp.logical_not(odd_y)
            edge = jnp.where(use_low, low, high)
            mobility = jnp.where(use_low, low_mobility, high_mobility)
            if number == 1:
                mobility = jnp.where(inner_y, mobility, 0.0)
            ref[z * k_count : (z + 1) * k_count, :] = edge.astype(BF16)
            field = jnp.sum(edge * b[:, :1], axis=0, keepdims=True)
            for place, value in enumerate((mobility, *three_terms(field))):
                extras[number] = jnp.where(extra_row == place * cz + z, value, extras[number])
    for number, ref in ((0, y1_ref), (1, y2_ref)):
        ref[cz * k_count : cz * k_count + extra_rows, :] = extras[number].astype(BF16)
    accumulation_copy.wait()


def gram_kernel(basis_ref, mobility_ref, accumulation_ref, b_ref, gram_ref, image_ref, field_ref, left_ref):
    k_count, cz, cy, cx = basis_ref.shape
    mobility = mobility_ref[...].astype(F32)
    accumulation = accumulation_ref[...]
    shape = mobility.shape
    along_x = jnp.where(iota(shape, 2) < cx - 1, harmonic(mobility, pltpu.roll(mobility, cx - 1, 2)), 0.0)
    along_y = jnp.where(iota(shape, 1) < cy - 1, harmonic(mobility, pltpu.roll(mobility, cy - 1, 1)), 0.0)
    along_z = VERTICAL_RATIO * harmonic(mobility[:-1], mobility[1:])
    rows = k_count * TILE
    strips = [(z, y) for z in range(cz) for y in range(0, cy, TILE)]
    for k in range(k_count):
        field = basis_ref[k].astype(F32)
        flow_x = along_x * (field - pltpu.roll(field, cx - 1, 2))
        image = accumulation * field + flow_x - pltpu.roll(flow_x, 1, 2)
        flow_y = along_y * (field - pltpu.roll(field, cy - 1, 1))
        image = image + flow_y - pltpu.roll(flow_y, 1, 1)
        flow_z = along_z * (field[:-1] - field[1:])
        nothing = jnp.zeros_like(field[:1])
        image = image + jnp.concatenate([flow_z, nothing], axis=0) - jnp.concatenate([nothing, flow_z], axis=0)
        high = image.astype(BF16)
        low = (image - high.astype(F32)).astype(BF16)
        for place, (z, y) in enumerate(strips):
            lanes = slice(place * cx, (place + 1) * cx)
            left_ref[k * TILE : (k + 1) * TILE, lanes] = high[z, y : y + TILE]
            left_ref[rows + k * TILE : rows + (k + 1) * TILE, lanes] = low[z, y : y + TILE]
    total = jnp.zeros((2 * rows, rows), F32)
    for place, (z, y) in enumerate(strips):
        right = basis_ref[:, z, y : y + TILE, :].reshape(rows, cx)
        total = total + dot_nt(left_ref[:, place * cx : (place + 1) * cx], right)
    total = total[:rows] + total[rows:]
    same = lax.rem(iota((rows, rows), 0), TILE) == lax.rem(iota((rows, rows), 1), TILE)
    total = jnp.where(same, total, 0.0)
    gram = jnp.sum(total.reshape(k_count, TILE, rows), axis=1)
    gram_ref[...] = gram
    place = iota((k_count, rows), 1) // TILE == iota((k_count, rows), 0)
    b_row = jnp.sum(jnp.where(place, b_ref[:, :1], 0.0), axis=0, keepdims=True)
    image_ref[...] = sum((gram * b_row)[:, start : start + LANES] for start in range(0, rows, LANES))
    field_ref[...] = expand(basis_ref, b_ref[...])


def couple_kernel(
    counts,
    y2_ref,
    y1_ref,
    x2_ref,
    x1_ref,
    rx2_ref,
    ry2_ref,
    ry1_ref,
    rx1_ref,
    b_ref,
    gram_ref,
    image_ref,
    out_ref,
    v_ref,
):
    k_count = b_ref.shape[0]
    cz = (y1_ref.shape[0] - TILE) // k_count
    odd_x, _ = position("gx", counts[0])
    odd_y, _ = position("gy", counts[1])
    b_col = b_ref[...]

    def unpack(ref, layers):
        blocks = [ref[z * k_count : (z + 1) * k_count, :].astype(F32) for z in range(layers)]
        start = layers * k_count
        extra = ref[start : start + round_up(4 * layers, TILE), :].astype(F32)
        mobility, high, middle, low = (extra[n * layers : (n + 1) * layers] for n in range(4))
        return blocks, mobility, high + middle + low

    faces = []
    for own_ref, other_ref, layers in (
        (x1_ref, rx1_ref, 1),
        (x2_ref, rx2_ref, 1),
        (y1_ref, ry1_ref, cz),
        (y2_ref, ry2_ref, cz),
    ):
        own, own_mobility, own_field = unpack(own_ref, layers)
        other, other_mobility, other_field = unpack(other_ref, layers)
        faces.append((own, other, harmonic(own_mobility, other_mobility), own_field, other_field))

    gram = gram_ref[...]
    wide = gram.shape[1]
    spread = iota((k_count, wide), 1) // TILE == iota((k_count, wide), 0)

    def as_row(column):
        return jnp.sum(jnp.where(spread, column[:, :1], 0.0), axis=0, keepdims=True)

    def fold(x):
        return sum(x[:, start : start + LANES] for start in range(0, wide, LANES))

    own_image = image_ref[...]
    along = own_image
    for own, _, conductance, own_field, other_field in faces:
        flow = conductance * (own_field - other_field)
        for z, block in enumerate(own):
            along = along + block * flow[z : z + 1]
    image = jnp.sum(along, axis=1, keepdims=True)
    source_square = jnp.sum(b_col * b_col, axis=0, keepdims=True)
    source_image = jnp.sum(b_col * image, axis=0, keepdims=True)
    quotient = source_image / jnp.maximum(source_square, TINY)
    v_col = image - quotient * b_col
    v_ref[0:k_count, :] = v_col
    v_ref[k_count : k_count + 8, :] = jnp.broadcast_to(quotient, (8, LANES))

    squares = [
        jnp.sum(b_col * own_image, axis=0, keepdims=True),
        jnp.sum(v_col * own_image, axis=0, keepdims=True),
        jnp.sum(v_col * fold(gram * as_row(v_col)), axis=0, keepdims=True),
    ]
    toward = []
    for own, other, conductance, own_field, other_field in faces:
        v_field = jnp.concatenate([jnp.sum(block * v_col, axis=0, keepdims=True) for block in own], axis=0)
        flow_b = conductance * own_field
        flow_v = conductance * v_field
        for n, value in enumerate((flow_b * own_field, flow_b * v_field, flow_v * v_field)):
            squares[n] = squares[n] + jnp.sum(value, axis=0, keepdims=True)
        toward.append(
            (
                other,
                flow_v,
                jnp.sum(-flow_b * other_field, axis=0, keepdims=True),
                jnp.sum(-flow_v * other_field, axis=0, keepdims=True),
            )
        )

    columns = [v_col]
    source_pairs = []
    image_pairs = []
    for first, second, odd in ((toward[0], toward[1], odd_x), (toward[2], toward[3], odd_y)):
        product = jnp.zeros((k_count, LANES), F32)
        for z in range(len(first[0])):
            block = jnp.where(odd, second[0][z], first[0][z])
            flow = jnp.where(odd, second[1], first[1])
            product = product - block * flow[z : z + 1]
        columns.append(jnp.sum(product, axis=1, keepdims=True))
        source_pairs.append(jnp.where(odd, second[2], first[2]))
        image_pairs.append(jnp.where(odd, second[3], first[3]))
        image_pairs.append(jnp.where(odd, first[3], second[3]))
    row = iota((TILE, LANES), 0)
    sums = jnp.zeros((TILE, LANES), F32)
    for n, value in enumerate((*squares, *source_pairs, *image_pairs)):
        sums = jnp.where(row == n, value, sums)
    scalars = jnp.broadcast_to(jnp.sum(sums, axis=1, keepdims=True), (TILE, LANES))
    v_square = jnp.sum(v_col * v_col, axis=0, keepdims=True)
    source_v = jnp.sum(v_col * b_col, axis=0, keepdims=True)
    for n, value in enumerate((quotient, source_square, source_image, source_v, v_square)):
        scalars = jnp.where(row == 9 + n, value, scalars)
    packed = jnp.zeros((1, LANES), F32)
    for n, column in enumerate((*columns, scalars)):
        size = column.shape[0]
        place = iota((size, LANES), 1) - iota((size, LANES), 0) == n * k_count
        packed = packed + jnp.sum(jnp.where(place, column, 0.0), axis=0, keepdims=True)
    out_ref[...] = jnp.broadcast_to(packed, out_ref.shape)


def finish_kernel(
    count_y,
    gathered_ref,
    b_ref,
    v_ref,
    b_field_ref,
    basis_ref,
    correction_hbm,
    solution_hbm,
    correction_ref,
    solution_ref,
    sems,
):
    k_count = b_ref.shape[0]
    cz = correction_ref.shape[0]
    base = 3 * k_count
    every = gathered_ref[...]
    v_field = expand(basis_ref, v_ref[0:k_count, :])

    def rows(x, amount):
        amount = amount % x.shape[0]
        return jnp.concatenate([x[amount:], x[:amount]], axis=0)

    def column(n):
        return jnp.broadcast_to(every[:, base + n : base + n + 1], every.shape)

    def total(x):
        return jnp.sum(x, axis=0, keepdims=True)

    sums = total(every)
    energy_sum = jnp.broadcast_to(sums[:, base + 10 : base + 11], sums.shape)
    image_sum = jnp.broadcast_to(sums[:, base + 11 : base + 12], sums.shape)
    lane = iota(every.shape, 1)
    vectors = pltpu.roll(every, LANES - k_count, 1) * rows(every, count_y)
    vectors = vectors + pltpu.roll(every, LANES - 2 * k_count, 1) * rows(every, 1)
    v_image_v = jnp.where(lane < k_count, 2.0 * vectors, jnp.where(lane == base + 2, every, 0.0))
    v_image_v = jnp.sum(total(v_image_v), axis=1, keepdims=True)
    quotient = column(9)
    quotient_x = rows(quotient, count_y)
    quotient_y = rows(quotient, 1)
    square_b, b_v, square_v = column(10), column(12), column(13)
    b_image_b, pair_x, pair_y = column(0), 2.0 * column(3), 2.0 * column(4)
    b_image_v = column(1) + rows(column(5), -count_y) + rows(column(6), count_y) + rows(column(7), -1) + rows(column(8), 1)

    step = energy_sum / (image_sum + EPSILON)
    left = 1.0 - step * quotient
    renewed = total(left * (left * square_b - 2.0 * step * b_v) + step * step * square_v)
    ratio = renewed / (energy_sum + EPSILON)
    weight = left + ratio
    weight_x = 1.0 + ratio - step * quotient_x
    weight_y = 1.0 + ratio - step * quotient_y
    curvature = total(weight * (weight * b_image_b + weight_x * pair_x + weight_y * pair_y - 2.0 * step * b_image_v))
    curvature = curvature + step * step * v_image_v
    last_step = renewed / (curvature + EPSILON)

    own_weight = 1.0 + ratio - step * v_ref[k_count : k_count + 1, :]
    b_part = step + last_step * own_weight
    v_part = -last_step * step
    solution = b_part * b_ref[...] + v_part * v_ref[0:k_count, :]
    place = iota(solution.shape, 0) == iota(solution.shape, 1)
    solution_ref[...] = total(jnp.where(place, solution, 0.0))[:, :k_count]
    copies = [pltpu.make_async_copy(solution_ref, solution_hbm, sems.at[cz])]
    copies[0].start()
    for z in range(cz):
        correction_ref[z] = b_part * b_field_ref[z] + v_part * v_field[z]
        copy = pltpu.make_async_copy(correction_ref.at[z], correction_hbm.at[z], sems.at[z])
        copy.start()
        copies.append(copy)
    for copy in copies:
        copy.wait()


def exchange(message, axis, counts, second):
    count_x, count_y = counts
    pairs = []
    for x in range(count_x):
        for y in range(count_y):
            i, count = (x, count_x) if axis == "gx" else (y, count_y)
            j = i ^ 1
            if second:
                j = i - 1 if i % 2 == 0 else i + 1
            if 0 <= j < count:
                partner = (j, y) if axis == "gx" else (x, j)
            else:
                partner = (x, y ^ 1) if axis == "gx" else (x ^ 1, y)
            pairs.append((x * count_y + y, partner[0] * count_y + partner[1]))
    return lax.ppermute(message, ("gx", "gy"), pairs)


def per_device(counts, basis, mobility, accumulation, residual):
    k_count, cz, cy, cx = basis.shape
    devices = counts[0] * counts[1]
    x_message = jax.ShapeDtypeStruct((k_count + TILE, cz * cy), BF16)
    y_message = jax.ShapeDtypeStruct((cz * k_count + round_up(4 * cz, TILE), cx), BF16)
    inputs = [pltpu.with_memory_space_constraint(x, pltpu.HBM) for x in (basis, mobility, accumulation, residual)]
    x1, x2, y1, y2, b, basis, mobility, accumulation = pl.pallas_call(
        functools.partial(edges_kernel, counts),
        out_shape=(
            x_message,
            x_message,
            y_message,
            y_message,
            jax.ShapeDtypeStruct((k_count, LANES), F32),
            jax.ShapeDtypeStruct(basis.shape, BF16),
            jax.ShapeDtypeStruct(mobility.shape, BF16),
            jax.ShapeDtypeStruct(accumulation.shape, F32),
        ),
        in_specs=[HBM] * 4,
        out_specs=(VMEM,) * 8,
        scratch_shapes=[
            pltpu.VMEM(residual.shape, F32),
            pltpu.SemaphoreType.DMA((4,)),
        ],
        compiler_params=PARAMS,
    )(*inputs)
    rx1 = exchange(x1, "gx", counts, False)
    rx2 = exchange(x2, "gx", counts, True)
    ry1 = exchange(y1, "gy", counts, False)
    ry2 = exchange(y2, "gy", counts, True)
    conductance = jax.ShapeDtypeStruct((cz, cy, cx), F32)
    gram, image, b_field = pl.pallas_call(
        gram_kernel,
        out_shape=(
            jax.ShapeDtypeStruct((k_count, k_count * TILE), F32),
            jax.ShapeDtypeStruct((k_count, LANES), F32),
            conductance,
        ),
        in_specs=[VMEM] * 4,
        out_specs=(VMEM,) * 3,
        compiler_params=PARAMS,
        scratch_shapes=[pltpu.VMEM((2 * k_count * TILE, cz * cy // TILE * cx), BF16)],
        cost_estimate=pl.CostEstimate(flops=10**8, bytes_accessed=10**6, transcendentals=0),
    )(basis, mobility, accumulation, b)
    row, v = pl.pallas_call(
        functools.partial(couple_kernel, counts),
        out_shape=(
            jax.ShapeDtypeStruct((devices, LANES), F32),
            jax.ShapeDtypeStruct((k_count + 8, LANES), F32),
        ),
        in_specs=[VMEM] * 11,
        out_specs=(VMEM,) * 2,
        compiler_params=PARAMS,
    )(y2, y1, x2, x1, rx2, ry2, ry1, rx1, b, gram, image)
    gathered = lax.all_to_all(row, ("gx", "gy"), 0, 0, tiled=True)
    correction, solution = pl.pallas_call(
        functools.partial(finish_kernel, counts[1]),
        out_shape=(jax.ShapeDtypeStruct((cz, cy, cx), F32), jax.ShapeDtypeStruct((1, k_count), F32)),
        in_specs=[VMEM] * 5,
        out_specs=(HBM, HBM),
        scratch_shapes=[
            pltpu.VMEM((cz, cy, cx), F32),
            pltpu.VMEM((1, k_count), F32),
            pltpu.SemaphoreType.DMA((cz + 1,)),
        ],
        compiler_params=PARAMS,
    )(gathered, b, v, b_field, basis)
    return correction, solution.reshape(1, 1, k_count)


def solution(mesh):
    counts = (mesh.shape["gx"], mesh.shape["gy"])
    placed = (
        P(None, None, "gy", "gx"),
        P(None, "gy", "gx"),
        P(None, "gy", "gx"),
        P(None, "gy", "gx"),
    )
    return jax.shard_map(
        functools.partial(per_device, counts),
        mesh=mesh,
        in_specs=placed,
        out_specs=(P(None, "gy", "gx"), P("gx", "gy", None)),
        check_vma=False,
    )
```
